32 devices in a mesh: section: 2 (over x), dp: 16 (over z, y, core).
Axes of the slice: x: 2, y: 2, z: 4, core: 2. Of those that a mesh axis runs over, the one named last changes fastest.
Arguments:
- inputs: bfloat16 [2, 16, 512, 768], P(None, 'dp'), may hold values from -6 to 6
- segments: int32 [2, 16, 512], P(None, 'dp'), may hold values from 0 to 15, as said below
- cotangent: bfloat16 [2, 16, 512, 768], P(None, 'dp'), may hold values from -6 to 6
- query_weight: bfloat16 [2, 768, 768], P('section'), may hold values from -0.21875 to 0.21875
- query_bias: bfloat16 [2, 768], P('section'), may hold values from -1.75 to 1.75
- key_weight: bfloat16 [2, 768, 768], P('section'), may hold values from -0.21875 to 0.21875
- value_weight: bfloat16 [2, 768, 768], P('section'), may hold values from -0.21875 to 0.21875
- value_bias: bfloat16 [2, 768], P('section'), may hold values from -1.75 to 1.75
- output_weight: bfloat16 [2, 768, 768], P('section'), may hold values from -0.625 to 0.625
- output_bias: bfloat16 [2, 768], P('section'), may hold values from -1.75 to 1.75
- attention_gain: bfloat16 [2, 768], P('section'), may hold values from 0.5 to 1.5
- attention_shift: bfloat16 [2, 768], P('section'), may hold values from -1.75 to 1.75
- inner_weight: bfloat16 [2, 768, 3072], P('section'), may hold values from -0.21875 to 0.21875
- inner_bias: bfloat16 [2, 3072], P('section'), may hold values from -1.75 to 1.75
- outer_weight: bfloat16 [2, 3072, 768], P('section'), may hold values from -0.109375 to 0.109375
- outer_bias: bfloat16 [2, 768], P('section'), may hold values from -1.75 to 1.75
- feed_gain: bfloat16 [2, 768], P('section'), may hold values from 0.5 to 1.5
- feed_shift: bfloat16 [2, 768], P('section'), may hold values from -1.75 to 1.75
Outputs:
- activations: bfloat16 [2, 2, 16, 512, 768], P('section', None, 'dp')
- input_gradients: bfloat16 [2, 2, 16, 512, 768], P('section', None, 'dp')
- query_weight_gradient: float32 [2, 768, 768], P('section')
- query_bias_gradient: float32 [2, 768], P('section')
- key_weight_gradient: float32 [2, 768, 768], P('section')
- value_weight_gradient: float32 [2, 768, 768], P('section')
- value_bias_gradient: float32 [2, 768], P('section')
- output_weight_gradient: float32 [2, 768, 768], P('section')
- output_bias_gradient: float32 [2, 768], P('section')
- attention_gain_gradient: float32 [2, 768], P('section')
- attention_shift_gradient: float32 [2, 768], P('section')
- inner_weight_gradient: float32 [2, 768, 3072], P('section')
- inner_bias_gradient: float32 [2, 3072], P('section')
- outer_weight_gradient: float32 [2, 3072, 768], P('section')
- outer_bias_gradient: float32 [2, 768], P('section')
- feed_gain_gradient: float32 [2, 768], P('section')
- feed_shift_gradient: float32 [2, 768], P('section')
The draws below stay inside these ranges and needn't reach their ends.
Inputs may be any that keep to these rules, and one draw needn't show every extreme that they name: Along each row the ids never fall; each run of equal ids starts at a multiple of 32 positions and is 1, 4 or 8 times 512 // 16 long; some row holds 16 segments.
All inputs are finite; a program needn't handle non-finite values.
Results may differ from the reference program's by a relative error of at most 0.023.
Values may be sent and summed in bfloat16 or wider, within the bound.
No kernel may reach another device: no remote copies, remote signals or barrier semaphores. Data moves between devices by JAX's collectives and lax.ppermute only.
A program may use at most 320 MiB of HBM per device.

```python
import jax
import jax.numpy as jnp
import numpy as np
from jax import lax

D = 768
HEADS = 12
HEAD = 64
FF = 3072
ROW = 512
MICRO = 2
ROWS = 16


patterns = np.array([[8, 4, 1, 1, 1, 1, 0, 0, 0, 0, 0, 0, 0, 0, 0, 0], [8, 8, 0, 0, 0, 0, 0, 0, 0, 0, 0, 0, 0, 0, 0, 0], [4, 4, 4, 4, 0, 0, 0, 0, 0, 0, 0, 0, 0, 0, 0, 0], [4, 4, 4, 1, 1, 1, 1, 0, 0, 0, 0, 0, 0, 0, 0, 0], [8, 4, 4, 0, 0, 0, 0, 0, 0, 0, 0, 0, 0, 0, 0, 0], [8, 1, 1, 1, 1, 1, 1, 1, 1, 0, 0, 0, 0, 0, 0, 0], [4, 4, 1, 1, 1, 1, 1, 1, 1, 1, 0, 0, 0, 0, 0, 0], [1, 1, 1, 1, 1, 1, 1, 1, 1, 1, 1, 1, 1, 1, 1, 1]], dtype=np.int32)


def draw_segments(key, part):
    key = jax.random.fold_in(key, 7)
    pick_key, order_key, full_key = jax.random.split(key, 3)
    row_count = MICRO * ROWS
    table = jnp.asarray(patterns)
    picked = jax.random.randint(pick_key, (row_count,), 0, 8)
    full_row = jax.random.randint(full_key, (), 0, row_count)
    picked = jnp.where(jnp.arange(row_count, dtype=jnp.int32) == full_row, 7, picked)
    lengths = table[picked]
    ranks = jax.random.randint(order_key, (row_count, 16), 0, 65536) * 16 + jnp.arange(16, dtype=jnp.int32)[None, :]
    order = jnp.argsort(ranks, axis=1)
    lengths = jnp.take_along_axis(lengths, order, axis=1)
    ends = jnp.cumsum(lengths, axis=1) * (ROW // 16)
    position = jnp.arange(ROW, dtype=jnp.int32)
    ident = jnp.sum((ends[:, None, :] <= position[None, :, None]).astype(jnp.int32), axis=2)
    return ident.reshape(MICRO, ROWS, ROW).astype(jnp.int32)


def level_of(own_key, extent, pieces, least, high):
    loudness, own = 1.0, jax.random.fold_in(own_key, 6)
    for axis_at, shards_of in pieces:
        draws = jnp.exp(jax.random.uniform(jax.random.fold_in(own, axis_at), (shards_of,), jnp.float32, least / len(pieces), high / len(pieces)))
        loudness = loudness * jnp.repeat(draws, extent[axis_at] // shards_of).reshape([-1 if axis == axis_at else 1 for axis in range(len(extent))])
    return loudness


def normal_values(key, extent, spread, bound, pieces=(), kind=jnp.bfloat16):
    entries = spread * jax.random.normal(key, extent, jnp.float32)
    if pieces:
        entries = entries * level_of(key, extent, pieces, -0.22, 0.18)
    return jnp.clip(entries, -bound, bound).astype(kind)


def setup_inputs(seed: int = 0) -> dict:
    seeds = jax.random.split(jax.random.key(seed), 19)
    inputs = normal_values(seeds[0], (MICRO, ROWS, ROW, D), 1.0, 6.0, ((1, 16),))
    segments = draw_segments(jax.random.fold_in(seeds[18], 71), 0)
    cotangent = normal_values(seeds[2], (MICRO, ROWS, ROW, D), 1.0, 6.0, ((1, 16),))
    query_weight = normal_values(seeds[3], (2, D, D), D ** -0.5, 0.21875, ((0, 2),))
    query_bias = normal_values(seeds[4], (2, D), 0.3, 1.75, ((0, 2),))
    key_weight = normal_values(seeds[5], (2, D, D), D ** -0.5, 0.21875, ((0, 2),))
    value_weight = normal_values(seeds[6], (2, D, D), D ** -0.5, 0.21875, ((0, 2),))
    value_bias = normal_values(seeds[7], (2, D), 0.3, 1.75, ((0, 2),))
    output_weight = normal_values(seeds[8], (2, D, D), (D // 8) ** -0.5, 0.625, ((0, 2),))
    output_bias = normal_values(seeds[9], (2, D), 0.3, 1.75, ((0, 2),))
    attention_gain = jnp.clip(1.0 + 0.1 * jax.random.normal(seeds[10], (2, D), jnp.float32), 0.5, 1.5).astype(jnp.bfloat16)
    attention_shift = normal_values(seeds[11], (2, D), 0.3, 1.75, ((0, 2),))
    inner_weight = normal_values(seeds[12], (2, D, FF), D ** -0.5, 0.21875, ((0, 2),))
    inner_bias = normal_values(seeds[13], (2, FF), 0.3, 1.75, ((0, 2),))
    outer_weight = normal_values(seeds[14], (2, FF, D), FF ** -0.5, 0.109375, ((0, 2),))
    outer_bias = normal_values(seeds[15], (2, D), 0.3, 1.75, ((0, 2),))
    feed_gain = jnp.clip(1.0 + 0.1 * jax.random.normal(seeds[16], (2, D), jnp.float32), 0.5, 1.5).astype(jnp.bfloat16)
    feed_shift = normal_values(seeds[17], (2, D), 0.3, 1.75, ((0, 2),))
    return {"inputs": inputs, "segments": segments, "cotangent": cotangent, "query_weight": query_weight, "query_bias": query_bias, "key_weight": key_weight, "value_weight": value_weight, "value_bias": value_bias, "output_weight": output_weight, "output_bias": output_bias, "attention_gain": attention_gain, "attention_shift": attention_shift, "inner_weight": inner_weight, "inner_bias": inner_bias, "outer_weight": outer_weight, "outer_bias": outer_bias, "feed_gain": feed_gain, "feed_shift": feed_shift}


@jax.custom_vjp
def low(v):
    return lax.optimization_barrier(v.astype(jnp.bfloat16)).astype(jnp.float32)

@jax.custom_vjp
def low_back(v):
    return v

def low_keep(v):
    return (low(v), None)

def low_pass(kept, grad):
    return (grad,)

def back_keep(v):
    return (v, None)

def back_low(kept, grad):
    return (low(grad),)
low.defvjp(low_keep, low_pass)
low_back.defvjp(back_keep, back_low)

def layer_norm(values_in, norm_gain, norm_shift):
    average = lax.optimization_barrier(jnp.mean(values_in, axis=-1, keepdims=True))
    centered = values_in - average
    variance = lax.optimization_barrier(jnp.mean(centered * centered, axis=-1, keepdims=True))
    return centered * lax.rsqrt(variance + 1e-12) * norm_gain + norm_shift

def matmul(left, right):
    return jnp.dot(left, right, precision=lax.Precision.HIGHEST)

def block_row(params, row_in, segment_row):
    query_weight, query_bias, key_weight, value_weight, value_bias, output_weight, output_bias, attention_gain, attention_shift, inner_weight, inner_bias, outer_weight, outer_bias, feed_gain, feed_shift = params
    length = row_in.shape[0]
    queries = low_back(low(matmul(row_in, query_weight) + query_bias)).reshape(length, HEADS, HEAD)
    keys = low_back(low(matmul(row_in, key_weight))).reshape(length, HEADS, HEAD)
    values_row = low_back(low(matmul(row_in, value_weight) + value_bias)).reshape(length, HEADS, HEAD)
    scores = low_back(jnp.einsum('qhe,khe->hqk', queries, keys, precision=lax.Precision.HIGHEST) * HEAD ** (-0.5))
    same_segment = segment_row[:, None] == segment_row[None, :]
    scores = jnp.where(same_segment[None], scores, -1e+30)
    weights_soft = low(jax.nn.softmax(scores, axis=-1))
    context = jnp.einsum('hqk,khe->qhe', weights_soft, values_row, precision=lax.Precision.HIGHEST)
    context = low_back(low(context.reshape(length, HEADS * HEAD)))
    branch = low_back(matmul(context, output_weight) + output_bias)
    hidden = layer_norm(row_in + branch, attention_gain, attention_shift)
    inner = low_back(matmul(low(hidden), inner_weight) + inner_bias)
    activated = low(jax.nn.gelu(inner, approximate=False))
    outer = low_back(matmul(activated, outer_weight) + outer_bias)
    return layer_norm(hidden + outer, feed_gain, feed_shift)

def run_layer(params, rows_in, segment_rows):

    def one_row(row_pair):
        return block_row(params, row_pair[0], row_pair[1])
    return lax.map(jax.checkpoint(one_row), (rows_in, segment_rows))

def reference(inputs, segments, cotangent, query_weight, query_bias, key_weight, value_weight, value_bias, output_weight, output_bias, attention_gain, attention_shift, inner_weight, inner_bias, outer_weight, outer_bias, feed_gain, feed_shift):
    params = tuple((member.astype(jnp.float32) for member in (query_weight, query_bias, key_weight, value_weight, value_bias, output_weight, output_bias, attention_gain, attention_shift, inner_weight, inner_bias, outer_weight, outer_bias, feed_gain, feed_shift)))
    row_count = MICRO * ROWS
    rows_in = inputs.astype(jnp.float32).reshape(row_count, ROW, D)
    segment_rows = segments.reshape(row_count, ROW)
    probe_zero = jnp.zeros_like(rows_in)

    def forward(layer_params, first_in, probe_value):
        first_out = run_layer(tuple((member[0] for member in layer_params)), first_in, segment_rows)
        middle = low_back(low(first_out) + probe_value)
        last_out = run_layer(tuple((member[1] for member in layer_params)), middle, segment_rows)
        return (last_out, middle)
    last_out, pullback, middle = jax.vjp(forward, params, rows_in, probe_zero, has_aux=True)
    param_grads, input_grad, middle_grad = pullback(cotangent.astype(jnp.float32).reshape(row_count, ROW, D))
    out_shape = (MICRO, ROWS, ROW, D)
    activations = jnp.stack([middle.reshape(out_shape), last_out.reshape(out_shape)]).astype(jnp.bfloat16)
    input_gradients = jnp.stack([input_grad.reshape(out_shape), middle_grad.reshape(out_shape)]).astype(jnp.bfloat16)
    return (activations, input_gradients, param_grads[0], param_grads[1], param_grads[2], param_grads[3], param_grads[4], param_grads[5], param_grads[6], param_grads[7], param_grads[8], param_grads[9], param_grads[10], param_grads[11], param_grads[12], param_grads[13], param_grads[14])
```

```python
from functools import partial

import jax
import jax.numpy as jnp
from jax import lax
from jax.experimental import pallas as pl
from jax.experimental.pallas import tpu as pltpu
from jax.sharding import PartitionSpec as P

HEADS = 12
HEAD = 64
LANES = 128
TILE = 256
VMEM_LIMIT = 60 * 1024 * 1024
BF = jnp.bfloat16
F32 = jnp.float32
ANY = pl.BlockSpec(memory_space=pl.ANY)
SMEM = pl.BlockSpec(memory_space=pltpu.SMEM)
VMEM = pl.BlockSpec(memory_space=pltpu.VMEM)


def dot(left, right):
    return lax.dot_general(left, right, (((1,), (0,)), ((), ())), preferred_element_type=F32)


def dot_nt(left, right):
    return lax.dot_general(left, right, (((1,), (1,)), ((), ())), preferred_element_type=F32)


def dot_tn(left, right):
    return lax.dot_general(left, right, (((0,), (0,)), ((), ())), preferred_element_type=F32)


def gelu_pair(u):
    z = jnp.abs(u) * 0.7071067811865476
    d = 1.0 + 0.3275911 * z
    t = pl.reciprocal(d, approx=True)
    t = t * (2.0 - d * t)
    poly = t * (0.127414796 + t * (-0.142248368 + t * (0.7107068705 + t * (-0.7265760135 + t * 0.5307027145))))
    bell = jnp.exp(-0.5 * u * u)
    tail = poly * bell
    cdf = jnp.where(u >= 0, 1.0 - tail, tail)
    return u * cdf, cdf + u * (bell * 0.3989422804014327)


def ds(index, size):
    return pl.ds(pl.multiple_of(index * size, size), size)


def forward_kernel(go, seg_row, bq, bv, bo, ga, sa, bi, bu, gf, sf,
                   x_h, wq_h, wk_h, wv_h, wo_h, wi_h, wu_h, *rest, n_alias, micro):
    rest = rest[n_alias:]
    outs, scratch = rest[:15], rest[15:]
    (res_h, x_o, q_h, k_h, v_h, e_h, inv_h, ctx_h, na_h, ra_h, hid_h, der_h, act_h, nf_h, rf_h) = outs
    (x, wq, wk, wv, wo, wi, wu, q, k, v, va, e, inv, ctx, na, ra, hid, der, act, nf, rf, res, mask, work, hidden, sin, sout) = scratch
    rows, width = x.shape
    wide = wi.shape[1]

    @pl.when(go[0] == 1)
    def _():
        loads = [(x_h if micro is None else x_h.at[micro], x), (wq_h, wq), (wk_h, wk), (wv_h, wv), (wo_h, wo), (wi_h, wi), (wu_h, wu)]
        loads = [pltpu.make_async_copy(a, b, sin.at[i]) for i, (a, b) in enumerate(loads)]
        for c in loads:
            c.start()
        stores = {}

        def put(i, src, dst):
            c = pltpu.make_async_copy(src, dst, sout.at[i])
            c.start()
            stores[i] = c

        ids = jnp.broadcast_to(seg_row[...].astype(F32), (8, rows))
        mask[...] = jnp.where(jnp.transpose(ids)[:, 0:1] == ids[0:1, :], 0.0, -1e30)
        loads[0].wait()
        put(0, x, x_o)
        loads[1].wait()
        nt = width // TILE
        for j in range(nt):
            cols = slice(j * TILE, (j + 1) * TILE)
            q[:, cols] = ((dot(x[...], wq[:, cols]) + bq[:, cols].astype(F32)).astype(BF) * HEAD ** -0.5).astype(BF)
        put(1, q, q_h)
        loads[2].wait()
        for j in range(nt):
            cols = slice(j * TILE, (j + 1) * TILE)
            k[:, cols] = dot(x[...], wk[:, cols]).astype(BF)
        put(2, k, k_h)
        loads[3].wait()
        for j in range(nt):
            cols = slice(j * TILE, (j + 1) * TILE)
            vv = (dot(x[...], wv[:, cols]) + bv[:, cols].astype(F32)).astype(BF)
            v[:, cols] = vv
            one = jnp.ones((rows, LANES), BF)
            for h in range(TILE // LANES):
                at = (j * (TILE // LANES) + h) * TILE
                va[:, at:at + LANES] = vv[:, h * LANES:(h + 1) * LANES]
                va[:, at + LANES:at + TILE] = one
        put(3, v, v_h)

        low = lax.broadcasted_iota(jnp.int32, (1, LANES), 1) < HEAD
        qb = 128

        def pair(p, _):
            kp = k[:, ds(p, LANES)]
            vp = va[:, ds(p, TILE)]
            kz = [jnp.where(low, kp, jnp.zeros_like(kp)), jnp.where(low, jnp.zeros_like(kp), kp)]
            for b in range(rows // qb):
                rr = slice(b * qb, (b + 1) * qb)
                qp = q[rr, ds(p, LANES)]
                parts = []
                for h in range(2):
                    s = dot_nt(qp, kz[h]) + mask[rr, :]
                    top = jnp.max(s, axis=-1, keepdims=True)
                    ee = jnp.exp(s - top).astype(BF)
                    e[2 * p + h, rr, :] = ee
                    o = dot(ee, vp)
                    r = 1.0 / o[:, LANES:]
                    parts.append((o[:, :LANES] * r, r))
                inv[rr, ds(p, LANES)] = jnp.where(low, parts[0][1], parts[1][1])
                ctx[rr, ds(p, LANES)] = jnp.where(low, parts[0][0], parts[1][0]).astype(BF)
            return 0

        lax.fori_loop(0, width // LANES, pair, 0)
        put(4, e, e_h)
        put(5, inv, inv_h)
        put(6, ctx, ctx_h)
        loads[4].wait()
        for j in range(nt):
            cols = slice(j * TILE, (j + 1) * TILE)
            work[:, cols] = dot(ctx[...], wo[:, cols]) + bo[:, cols].astype(F32) + x[:, cols].astype(F32)

        def norm(b, _):
            rr = ds(b, 64)
            t = work[rr, :]
            t = t - jnp.mean(t, axis=-1, keepdims=True)
            r = lax.rsqrt(jnp.mean(t * t, axis=-1, keepdims=True) + 1e-12)
            n = t * r
            h = n * ga[...].astype(F32) + sa[...].astype(F32)
            na[rr, :] = n.astype(BF)
            ra[rr, :] = jnp.broadcast_to(r, (64, LANES))
            hidden[rr, :] = h
            hid[rr, :] = h.astype(BF)
            return 0

        lax.fori_loop(0, rows // 64, norm, 0, unroll=2)
        put(7, na, na_h)
        put(8, ra, ra_h)
        put(9, hid, hid_h)
        loads[5].wait()

        def feed(j, _):
            cols = ds(j, TILE)
            u = dot(hid[...], wi[:, cols]) + bi[:, cols].astype(F32)
            a, g = gelu_pair(u)
            act[:, cols] = a.astype(BF)
            der[:, cols] = g.astype(BF)
            return 0

        lax.fori_loop(0, wide // TILE, feed, 0, unroll=2)
        put(10, der, der_h)
        put(11, act, act_h)
        loads[6].wait()
        for j in range(nt):
            cols = slice(j * TILE, (j + 1) * TILE)
            work[:, cols] = dot(act[...], wu[:, cols]) + bu[:, cols].astype(F32) + hidden[:, cols]

        def last(b, _):
            rr = ds(b, 64)
            t = work[rr, :]
            t = t - jnp.mean(t, axis=-1, keepdims=True)
            r = lax.rsqrt(jnp.mean(t * t, axis=-1, keepdims=True) + 1e-12)
            n = t * r
            nf[rr, :] = n.astype(BF)
            rf[rr, :] = jnp.broadcast_to(r, (64, LANES))
            res[rr, :] = (n * gf[...].astype(F32) + sf[...].astype(F32)).astype(BF)
            return 0

        lax.fori_loop(0, rows // 64, last, 0, unroll=2)
        put(12, res, res_h)
        put(13, nf, nf_h)
        put(14, rf, rf_h)
        for c in stores.values():
            c.wait()


def run_forward(go, seg, x, w, micro=None, saved=None):
    rows, width = x.shape[-2:]
    wide = w["wi"].shape[1]
    sd = jax.ShapeDtypeStruct
    act = sd((rows, width), BF)
    out_shape = [act] * 5 + [sd((HEADS, rows, rows), BF), sd((rows, width), F32), act, act, sd((rows, LANES), F32), act,
                             sd((rows, wide), BF), sd((rows, wide), BF), act, sd((rows, LANES), F32)]
    vm = pltpu.VMEM
    scratch = [vm((rows, width), BF)] + [vm((width, width), BF)] * 4 + [vm((width, wide), BF), vm((wide, width), BF)]
    scratch += [vm((rows, width), BF)] * 3 + [vm((rows, 2 * width), BF), vm((HEADS, rows, rows), BF), vm((rows, width), F32)]
    scratch += [vm((rows, width), BF)] * 2 + [vm((rows, LANES), F32), vm((rows, width), BF)] + [vm((rows, wide), BF)] * 2
    scratch += [vm((rows, width), BF), vm((rows, LANES), F32), vm((rows, width), BF), vm((rows, rows), F32)]
    scratch += [vm((rows, width), F32)] * 2
    scratch += [pltpu.SemaphoreType.DMA((7,)), pltpu.SemaphoreType.DMA((15,))]
    alias = () if saved is None else tuple(saved)
    args = [go, seg, w["bq"], w["bv"], w["bo"], w["ga"], w["sa"], w["bi"], w["bu"], w["gf"], w["sf"],
            x, w["wq"], w["wk"], w["wv"], w["wo"], w["wi"], w["wu"], *alias]
    outs = pl.pallas_call(
        partial(forward_kernel, n_alias=len(alias), micro=micro),
        out_shape=out_shape,
        in_specs=[SMEM] + [VMEM] * 10 + [ANY] * (7 + len(alias)),
        out_specs=[ANY] * 15,
        scratch_shapes=scratch,
        input_output_aliases={18 + i: 1 + i for i in range(len(alias))},
        compiler_params=pltpu.CompilerParams(vmem_limit_bytes=VMEM_LIMIT),
        cost_estimate=pl.CostEstimate(flops=2 * rows * 10 * width * width, bytes_accessed=40_000_000, transcendentals=0),
        name="forward",
    )(*args)
    return outs[0], outs[1:]


def feed_back_kernel(go, gf, g_h, nf_h, rf_h, der_h, wu_h, wi_h, *rest, n_alias, micro):
    rest = rest[n_alias:]
    og_h, ig_h, hg_h, small_h = rest[:4]
    g, nf, rf, der, wu, wi, og, ig, hg, small, sin, sout = rest[4:]
    rows, width = g.shape
    wide = der.shape[1]

    @pl.when(go[0] == 1)
    def _():
        loads = [(g_h if micro is None else g_h.at[micro], g), (nf_h, nf), (rf_h, rf), (wu_h, wu), (der_h, der), (wi_h, wi)]
        loads = [pltpu.make_async_copy(a, b, sin.at[i]) for i, (a, b) in enumerate(loads)]
        for c in loads:
            c.start()
        for c in loads[:3]:
            c.wait()

        def norm(b, sums):
            rr = ds(b, 64)
            t = g[rr, :].astype(F32)
            n = nf[rr, :].astype(F32)
            s = t * gf[...].astype(F32)
            m1 = jnp.mean(s, axis=-1, keepdims=True)
            m2 = jnp.mean(s * n, axis=-1, keepdims=True)
            f = (s - m1 - n * m2) * rf[rr, 0:1]
            hg[rr, :] = f
            low = f.astype(BF)
            og[rr, :] = low
            parts = (t * n, t, low.astype(F32))
            return tuple(a + jnp.sum(b.reshape(8, 8, width), axis=0) for a, b in zip(sums, parts))

        zero = jnp.zeros((8, width), F32)
        sums = lax.fori_loop(0, rows // 64, norm, (zero, zero, zero), unroll=2)
        small[...] = jnp.zeros_like(small)
        for i in range(3):
            small[i:i + 1, :width] = jnp.sum(sums[i], axis=0, keepdims=True)
        c0 = pltpu.make_async_copy(og, og_h, sout.at[0])
        c0.start()
        loads[3].wait()
        loads[4].wait()

        def inner(j, _):
            cols = ds(j, TILE)
            t = dot_nt(og[...], wu[cols, :]) * der[:, cols].astype(F32)
            low = t.astype(BF)
            ig[:, cols] = low
            small[3:4, cols] = jnp.sum(low.astype(F32), axis=0, keepdims=True)
            return 0

        lax.fori_loop(0, wide // TILE, inner, 0, unroll=2)
        c1 = pltpu.make_async_copy(ig, ig_h, sout.at[1])
        c1.start()
        loads[5].wait()
        for j in range(width // TILE):
            cols = slice(j * TILE, (j + 1) * TILE)
            hg[:, cols] = hg[:, cols] + dot_nt(ig[...], wi[cols, :])
        c2 = pltpu.make_async_copy(hg, hg_h, sout.at[2])
        c2.start()
        c3 = pltpu.make_async_copy(small, small_h, sout.at[3])
        c3.start()
        c0.wait()
        c1.wait()
        c2.wait()
        c3.wait()


def run_feed_back(go, g, saved, w, micro=None, old=None):
    (x, q, k, v, e, inv, ctx, na, ra, hid, der, act, nf, rf) = saved
    rows, width = g.shape[-2:]
    wide = der.shape[1]
    sd, vm = jax.ShapeDtypeStruct, pltpu.VMEM
    alias = () if old is None else tuple(old)
    outs = pl.pallas_call(
        partial(feed_back_kernel, n_alias=len(alias), micro=micro),
        out_shape=[sd((rows, width), BF), sd((rows, wide), BF), sd((rows, width), F32), sd((8, wide), F32)],
        in_specs=[SMEM, VMEM] + [ANY] * (6 + len(alias)),
        out_specs=[ANY] * 4,
        scratch_shapes=[vm((rows, width), BF), vm((rows, width), BF), vm((rows, LANES), F32), vm((rows, wide), BF),
                        vm((wide, width), BF), vm((width, wide), BF), vm((rows, width), BF), vm((rows, wide), BF), vm((rows, width), F32),
                        vm((8, wide), F32), pltpu.SemaphoreType.DMA((6,)), pltpu.SemaphoreType.DMA((4,))],
        input_output_aliases={8 + i: i for i in range(len(alias))},
        compiler_params=pltpu.CompilerParams(vmem_limit_bytes=VMEM_LIMIT),
        cost_estimate=pl.CostEstimate(flops=4 * rows * wide * width, bytes_accessed=20_000_000, transcendentals=0),
        name="feed_back",
    )(go, w["gf"], g, nf, rf, der, w["wu"], w["wi"], *alias)
    return outs


def attention_back_kernel(go, ga, hg_h, na_h, ra_h, wo_h, inv_h, ctx_h, q_h, k_h, v_h, e_h, wq_h, wk_h, wv_h, *rest, n_alias):
    rest = rest[n_alias:]
    lg_h, bg_h, dq_h, dk_h, dv_h, small_h = rest[:6]
    (hg, na, ra, wo, inv, ctx, q, k, v, e, wq, wk, wv, bg, cg, dq, dk, dv, lg, small, sin, sout) = rest[6:]
    rows, width = bg.shape

    @pl.when(go[0] == 1)
    def _():
        loads = [(hg_h, hg), (na_h, na), (ra_h, ra), (wo_h, wo), (inv_h, inv), (ctx_h, ctx), (q_h, q), (k_h, k), (v_h, v),
                 (e_h, e), (wq_h, wq), (wk_h, wk), (wv_h, wv)]
        loads = [pltpu.make_async_copy(a, b, sin.at[i]) for i, (a, b) in enumerate(loads)]
        for c in loads:
            c.start()
        for c in loads[:3]:
            c.wait()

        def norm(b, sums):
            rr = ds(b, 64)
            t = hg[rr, :]
            n = na[rr, :].astype(F32)
            s = t * ga[...].astype(F32)
            m1 = jnp.mean(s, axis=-1, keepdims=True)
            m2 = jnp.mean(s * n, axis=-1, keepdims=True)
            f = (s - m1 - n * m2) * ra[rr, 0:1]
            hg[rr, :] = f
            low = f.astype(BF)
            bg[rr, :] = low
            parts = (t * n, t, low.astype(F32))
            return tuple(a + jnp.sum(b.reshape(8, 8, width), axis=0) for a, b in zip(sums, parts))

        zero = jnp.zeros((8, width), F32)
        sums = lax.fori_loop(0, rows // 64, norm, (zero, zero, zero), unroll=2)
        small[...] = jnp.zeros_like(small)
        for i in range(3):
            small[i:i + 1, :] = jnp.sum(sums[i], axis=0, keepdims=True)
        puts = []

        def put(src, dst):
            c = pltpu.make_async_copy(src, dst, sout.at[len(puts)])
            c.start()
            puts.append(c)

        put(bg, bg_h)
        loads[3].wait()
        for j in range(width // TILE):
            cols = slice(j * TILE, (j + 1) * TILE)
            cg[:, cols] = dot_nt(bg[...], wo[cols, :]).astype(BF)
        for c in loads[4:10]:
            c.wait()

        low = lax.broadcasted_iota(jnp.int32, (1, LANES), 1) < HEAD

        def pair(p, _):
            cols = ds(p, LANES)
            kp = k[:, cols]
            vp = v[:, cols]
            qp = q[:, cols]
            cp = cg[:, cols].astype(F32)
            prod = cp * ctx[:, cols].astype(F32)
            ip = inv[:, cols]
            co = (cp * ip).astype(BF)
            zb = jnp.zeros_like(kp)
            dqs, dks, dvs = [], [], []
            for h in range(2):
                mine = low if h == 0 else jnp.logical_not(low)
                weighted = jnp.sum(jnp.where(mine, prod * ip, 0.0), axis=-1, keepdims=True)
                ch = jnp.where(mine, co, zb)
                ee = e[2 * p + h]
                dp = dot_nt(ch, vp) - weighted
                sg = (ee.astype(F32) * dp).astype(BF)
                dvs.append(dot_tn(ee, ch))
                dqs.append(dot(sg, jnp.where(mine, kp, zb)))
                dks.append(dot_tn(sg, jnp.where(mine, qp, zb)))
            dq[:, cols] = ((dqs[0] + dqs[1]) * HEAD ** -0.5).astype(BF)
            dk[:, cols] = (dks[0] + dks[1]).astype(BF)
            dv[:, cols] = (dvs[0] + dvs[1]).astype(BF)
            return 0

        lax.fori_loop(0, width // LANES, pair, 0)
        put(dq, dq_h)
        put(dk, dk_h)
        put(dv, dv_h)
        for c in loads[10:]:
            c.wait()
        for j in range(width // TILE):
            cols = slice(j * TILE, (j + 1) * TILE)
            t = hg[:, cols] + dot_nt(dq[...], wq[cols, :]) + dot_nt(dk[...], wk[cols, :]) + dot_nt(dv[...], wv[cols, :])
            lg[:, cols] = t.astype(BF)
        put(lg, lg_h)
        small[3:4, :] = jnp.sum(dq[...].astype(F32), axis=0, keepdims=True)
        small[4:5, :] = jnp.sum(dv[...].astype(F32), axis=0, keepdims=True)
        put(small, small_h)
        for c in puts:
            c.wait()


def run_attention_back(go, hg, saved, w, old=None):
    (x, q, k, v, e, inv, ctx, na, ra, hid, der, act, nf, rf) = saved
    rows, width = x.shape
    sd, vm = jax.ShapeDtypeStruct, pltpu.VMEM
    alias = () if old is None else tuple(old)
    row = vm((rows, width), BF)
    sq = vm((width, width), BF)
    outs = pl.pallas_call(
        partial(attention_back_kernel, n_alias=len(alias)),
        out_shape=[sd((rows, width), BF)] * 5 + [sd((8, width), F32)],
        in_specs=[SMEM, VMEM] + [ANY] * (13 + len(alias)),
        out_specs=[ANY] * 6,
        scratch_shapes=[vm((rows, width), F32), row, vm((rows, LANES), F32), sq, vm((rows, width), F32), row, row, row, row,
                        vm((HEADS, rows, rows), BF), sq, sq, sq, row, row, row, row, row, row,
                        vm((8, width), F32), pltpu.SemaphoreType.DMA((13,)), pltpu.SemaphoreType.DMA((6,))],
        input_output_aliases={15 + i: 1 + i for i in range(len(alias))},
        compiler_params=pltpu.CompilerParams(vmem_limit_bytes=VMEM_LIMIT),
        cost_estimate=pl.CostEstimate(flops=16 * rows * width * width, bytes_accessed=30_000_000, transcendentals=0),
        name="attention_back",
    )(go, w["ga"], hg, na, ra, w["wo"], inv, ctx, q, k, v, e, w["wq"], w["wk"], w["wv"], *alias)
    return outs[0], outs[1:]


def wgrad_kernel(half, a0, a1, g0, g1, o):
    o[0] = (dot_tn(a0[...], g0[...]) + dot_tn(a1[...], g1[...])).astype(BF)


def run_wgrad(half, a, g, block, split_left):
    rows, m = a[0].shape
    n = g[0].shape[1]
    if split_left:
        gi, aj, ha, hg, gn = 1, m // 2 // block, m // 2 // block, 0, n
    else:
        gn = m
        gi, aj, ha, hg = n // 2 // gn, m // block, 0, n // 2 // gn
    sa = pl.BlockSpec((rows, block), lambda i, j, h: (0, h[0] * ha + j))
    sg = pl.BlockSpec((rows, gn), lambda i, j, h: (0, h[0] * hg + i))
    return pl.pallas_call(
        wgrad_kernel,
        grid_spec=pltpu.PrefetchScalarGridSpec(
            num_scalar_prefetch=1, grid=(gi, aj), in_specs=[sa, sa, sg, sg],
            out_specs=pl.BlockSpec((1, block, gn), lambda i, j, h: (i * aj + j, 0, 0))),
        out_shape=jax.ShapeDtypeStruct((gi * aj, block, gn), BF),
        compiler_params=pltpu.CompilerParams(vmem_limit_bytes=VMEM_LIMIT),
        cost_estimate=pl.CostEstimate(flops=2 * rows * m * n, bytes_accessed=2 * (2 * rows * (m + n) + m * n), transcendentals=0),
        name="weight_gradient",
    )(half, a[0], a[1], g[0], g[1])


def attention_wgrad_kernel(half, fs0, fs1, as0, as1, *rest):
    ctx, x, bg, dq, dk, dv = [rest[2 * i:2 * i + 2] for i in range(6)]
    o, a_s, g_s, sems = rest[12:]
    width = a_s.shape[-1]
    chunk = o.shape[1] - 16
    sides = (((ctx, bg), (x, dq)), ((x, dk), (x, dv)))
    for side in range(2):
        @pl.when(half[0] == side)
        def _(side=side):
            for s in range(2):
                for m in range(2):
                    pltpu.make_async_copy(sides[side][s][0][m], a_s.at[s, m], sems.at[0, s, m]).start()
                    pltpu.make_async_copy(sides[side][s][1][m], g_s.at[s, m], sems.at[1, s, m]).start()
    o[:, chunk:, :] = jnp.zeros((o.shape[0], 16, width), BF)
    fs = fs0[...] + fs1[...]
    at = as0[...] + as1[...]
    lines = [at[3:4], at[4:5], at[2:3], at[0:1], at[1:2], fs[2:3, :width], fs[0:1, :width], fs[1:2, :width]]
    lines += [fs[3:4, i * width:(i + 1) * width] for i in range(fs.shape[1] // width)]
    lines += [jnp.zeros((16 - len(lines), width), F32)]
    o[0, chunk:, :] = jnp.concatenate(lines, axis=0).astype(BF)
    for s in range(2):
        for m in range(2):
            pltpu.make_async_copy(dv[0], a_s.at[s, m], sems.at[0, s, m]).wait()
            pltpu.make_async_copy(dv[0], g_s.at[s, m], sems.at[1, s, m]).wait()
        per = width // chunk
        for t in range(per):
            cols = slice(t * chunk, (t + 1) * chunk)
            r = dot_tn(a_s[s, 0, :, cols], g_s[s, 0]) + dot_tn(a_s[s, 1, :, cols], g_s[s, 1])
            o[s * per + t, :chunk, :] = r.astype(BF)


def run_attention_wgrad(half, feed_small, att_small, ctx, x, bg, dq, dk, dv):
    rows, width = ctx[0].shape
    chunk = 2 * width // 8
    args = [a for pair in (ctx, x, bg, dq, dk, dv) for a in pair]
    return pl.pallas_call(
        attention_wgrad_kernel,
        out_shape=jax.ShapeDtypeStruct((8, chunk + 16, width), BF),
        in_specs=[SMEM] + [VMEM] * 4 + [ANY] * 12,
        out_specs=VMEM,
        scratch_shapes=[pltpu.VMEM((2, 2, rows, width), BF), pltpu.VMEM((2, 2, rows, width), BF), pltpu.SemaphoreType.DMA((2, 2, 2))],
        compiler_params=pltpu.CompilerParams(vmem_limit_bytes=VMEM_LIMIT),
        cost_estimate=pl.CostEstimate(flops=8 * rows * width * width, bytes_accessed=9_000_000, transcendentals=0),
        name="attention_weight_gradient",
    )(half, *feed_small, *att_small, *args)


def unpack_kernel(place, *rest, kind, extra):
    mine, other = rest[:8], rest[8]
    n_out = {"rows": 1, "columns": 1, "four": 4}[kind]
    outs = rest[9:9 + n_out]
    small = rest[9 + n_out:-4]
    low, high, sin, sout = rest[-4:]
    total, width = low.shape[1:]
    chunk = total - extra
    loads = [pltpu.make_async_copy(mine[u], low.at[u], sin.at[u]) for u in range(8)]
    loads += [pltpu.make_async_copy(other.at[u], low.at[8 + u], sin.at[8 + u]) for u in range(8)]
    for c in loads:
        c.start()
    for u in range(16):
        core = place[0] if u < 8 else 1 - place[0]
        rank = place[1] if u < 8 else 7 - place[1]
        index = core * 8 + lax.rem(rank + 9 - u % 8, 8)
        loads[u].wait()
        high[u] = low[u, :chunk, :].astype(F32)
        if kind == "rows":
            pltpu.make_async_copy(high.at[u], outs[0].at[pl.ds(pl.multiple_of(index * chunk, 8), chunk), :], sout.at[u]).start()
        else:
            per = width // chunk
            block, row = index // per, lax.rem(index, per)
            where = pl.ds(pl.multiple_of(row * chunk, 8), chunk)
            if kind == "columns":
                cols = pl.ds(pl.multiple_of(block * width, width), width)
                pltpu.make_async_copy(high.at[u], outs[0].at[where, cols], sout.at[u]).start()
            else:
                for n in range(4):
                    @pl.when(block == n)
                    def _(n=n, u=u, where=where):
                        pltpu.make_async_copy(high.at[u], outs[n].at[where, :], sout.at[u]).start()
    if extra:
        u = lax.rem(place[1] + 1, 8)
        t = low[u, chunk:, :].astype(F32)
        for i in range(8):
            small[i][...] = t[i:i + 1]
        for i in range(small[8].shape[1] // width):
            small[8][:, i * width:(i + 1) * width] = t[8 + i:9 + i]
    for u in range(16):
        pltpu.make_async_copy(high.at[u], outs[0].at[:chunk, :width], sout.at[u]).wait()


def run_unpack(place, pieces, other, kind, wide=0):
    total, width = pieces[0].shape
    extra = 16 if kind == "four" else 0
    chunk = total - extra
    sd = jax.ShapeDtypeStruct
    if kind == "rows":
        shapes = [sd((16 * chunk, width), F32)]
    elif kind == "columns":
        shapes = [sd((width, 16 * chunk), F32)]
    else:
        shapes = [sd((4 * chunk, width), F32)] * 4
    small = [sd((1, width), F32)] * 8 + [sd((1, wide), F32)] if extra else []
    return pl.pallas_call(
        partial(unpack_kernel, kind=kind, extra=extra),
        out_shape=shapes + small,
        in_specs=[SMEM] + [ANY] * 9,
        out_specs=[ANY] * len(shapes) + [VMEM] * len(small),
        scratch_shapes=[pltpu.VMEM((16, total, width), BF), pltpu.VMEM((16, chunk, width), F32),
                        pltpu.SemaphoreType.DMA((16,)), pltpu.SemaphoreType.DMA((16,))],
        compiler_params=pltpu.CompilerParams(vmem_limit_bytes=VMEM_LIMIT),
        cost_estimate=pl.CostEstimate(flops=0, bytes_accessed=6 * 16 * total * width, transcendentals=0),
        name="unpack",
    )(place, *pieces, other)


def ring_tables():
    chips = [(z, 0) for z in range(4)] + [(z, 1) for z in reversed(range(4))]
    step = []
    for at, (z, y) in enumerate(chips):
        for core in range(2):
            nz, ny = chips[(at + 1) % 8] if core == 0 else chips[at - 1]
            step.append((z * 4 + y * 2 + core, nz * 4 + ny * 2 + core))
    swap = [(d, d ^ 1) for d in range(16)]
    return step, swap


def ring_place():
    d = lax.axis_index("dp")
    z, y, core = d // 4, (d // 2) % 2, d % 2
    at = jnp.where(y == 0, z, 7 - z)
    return core, jnp.where(core == 0, at, 7 - at)


def after(value, *earlier):
    return lax.optimization_barrier((value, *earlier))[0]


def ring_sum(keep, got, rank, step):
    def own(index):
        index = lax.rem(index, 8)
        return lax.dynamic_index_in_dim(keep, index, 0, keepdims=False) + lax.dynamic_index_in_dim(got, index, 0, keepdims=False)

    current = own(rank)
    for s in range(7):
        current = lax.ppermute(current, "dp", step) + own(rank + 7 - s)
    pieces = [current]
    for s in range(7):
        current = lax.ppermute(current, "dp", step)
        pieces.append(current)
    return pieces


def body(inputs, segments, cotangent, query_weight, query_bias, key_weight, value_weight, value_bias, output_weight, output_bias,
         attention_gain, attention_shift, inner_weight, inner_bias, outer_weight, outer_bias, feed_gain, feed_shift):
    micros, local, rows, width = inputs.shape
    wide = inner_weight.shape[2]
    w = dict(wq=query_weight[0], wk=key_weight[0], wv=value_weight[0], wo=output_weight[0], wi=inner_weight[0], wu=outer_weight[0],
             bq=query_bias, bv=value_bias, bo=output_bias, ga=attention_gain, sa=attention_shift, bi=inner_bias, bu=outer_bias,
             gf=feed_gain, sf=feed_shift)
    x_all = inputs.reshape(micros, rows, width)
    g_all = cotangent.reshape(micros, rows, width)
    section = lax.axis_index("section")
    first = section == 0
    on0 = jnp.reshape(1 - section, (1,)).astype(jnp.int32)
    on1 = jnp.reshape(section, (1,)).astype(jnp.int32)
    up = partial(lax.ppermute, axis_name="section", perm=[(0, 1)])
    down = partial(lax.ppermute, axis_name="section", perm=[(1, 0)])

    r00, s0 = run_forward(on0, segments[0], x_all, w, micro=0)
    x10 = up(r00)
    r01, s1 = run_forward(after(on0, r00), segments[1], x_all, w, micro=1)
    x11 = up(r01)
    r10, s0 = run_forward(after(on1, r01), segments[0], x10, w, saved=s0)
    f0 = run_feed_back(on1, g_all, s0, w, micro=0)
    l10, a0 = run_attention_back(on1, f0[2], s0, w)
    g00 = down(l10)
    r11, s1 = run_forward(after(on1, l10), segments[1], x11, w, saved=s1)
    f0 = run_feed_back(after(on0, r11), g00, s0, w, old=f0)
    l00, a0 = run_attention_back(on0, f0[2], s0, w, old=a0)
    f1 = run_feed_back(after(on1, l00), g_all, s1, w, micro=1)
    l11, a1 = run_attention_back(on1, f1[2], s1, w)
    g01 = down(l11)
    f1 = run_feed_back(on0, g01, s1, w, old=f1)
    (x0, q0, k0, v0, e0, inv0, ctx0, na0, ra0, hid0, der0, act0, nf0, rf0) = s0
    (x1, q1, k1, v1, e1, inv1, ctx1, na1, ra1, hid1, der1, act1, nf1, rf1) = s1
    core, rank = ring_place()
    there = jnp.reshape(1 - core, (1,)).astype(jnp.int32)
    here = jnp.reshape(core, (1,)).astype(jnp.int32)
    place = jnp.stack([core, rank]).astype(jnp.int32)
    step, swap = ring_tables()

    def outer(h):
        return run_wgrad(h, (act0, act1), (f0[0], f1[0]), 256, True)

    def inner(h):
        return run_wgrad(h, (hid0, hid1), (f0[1], f1[1]), 256, False)

    def rest(h):
        return run_attention_wgrad(h, (f0[3], f1[3]), (a0[4], a1[4]), (ctx0, ctx1), (x0, x1), (a0[0], a1[0]), (a0[1], a1[1]),
                                   (a0[2], a1[2]), (a0[3], a1[3]))

    def reduced(make):
        sent = make(there)
        got = lax.ppermute(sent, "dp", swap)
        keep = make(after(here, sent))
        shape = (8, -1, width)
        pieces = ring_sum(keep.reshape(shape), got.reshape(shape), rank, step)
        other = lax.ppermute(jnp.stack(pieces), "dp", swap)
        return pieces, other

    ring = lax.axis_size("dp") == 16
    if ring:
        p1, o1 = reduced(outer)
        p2, o2 = reduced(inner)
        l01, a1 = run_attention_back(on0, f1[2], s1, w, old=a1)
        p3, o3 = reduced(rest)
        (outer_g,) = run_unpack(place, p1, o1, "rows")
        (inner_g,) = run_unpack(place, p2, o2, "columns")
        fours = run_unpack(place, p3, o3, "four", wide)
    else:
        zero, one = jnp.zeros((1,), jnp.int32), jnp.ones((1,), jnp.int32)
        l01, a1 = run_attention_back(on0, f1[2], s1, w, old=a1)
        sums = [lax.psum(jnp.stack([make(zero).reshape(8, -1, width), make(one).reshape(8, -1, width)]), "dp").astype(F32)
                for make in (outer, inner, rest)]
        outer_g = sums[0].reshape(wide, width)
        inner_g = sums[1].reshape(wide // width, width, width).transpose(1, 0, 2).reshape(width, wide)
        tail = 2 * width // 8
        lines = sums[2][0, 0, tail:]
        fours = list(sums[2][:, :, :tail].reshape(4, width, width)) + [lines[i:i + 1] for i in range(8)]
        fours.append(lines[8:8 + wide // width].reshape(1, wide))
    (wo_g, wq_g, wk_g, wv_g, bq_g, bv_g, bo_g, ga_g, sa_g, bu_g, gf_g, sf_g, bi_g) = fours
    activations = jnp.where(first, jnp.stack([r00, r01]), jnp.stack([r10, r11]))
    input_gradients = jnp.where(first, jnp.stack([l00, l01]), jnp.stack([l10, l11]))
    shape = (1, micros, local, rows, width)
    return (activations.reshape(shape), input_gradients.reshape(shape), wq_g[None], bq_g, wk_g[None], wv_g[None], bv_g, wo_g[None], bo_g,
            ga_g, sa_g, inner_g[None], bi_g, outer_g[None], bu_g, gf_g, sf_g)


def solution(mesh):
    rows3 = P(None, "dp", None, None)
    matrix, vector = P("section", None, None), P("section", None)
    results = P("section", None, "dp", None, None)
    return jax.shard_map(
        body,
        mesh=mesh,
        in_specs=(rows3, P(None, "dp", None), rows3, matrix, vector, matrix, matrix, vector, matrix, vector, vector, vector,
                  matrix, vector, matrix, vector, vector, vector),
        out_specs=(results, results, matrix, vector, matrix, matrix, vector, matrix, vector, vector, vector, matrix, vector,
                   matrix, vector, vector, vector),
        check_vma=False,
    )
```

```python
from functools import partial

import jax
import jax.numpy as jnp
from jax import lax
from jax.experimental import pallas as pl
from jax.experimental.pallas import tpu as pltpu
from jax.sharding import PartitionSpec as P

HEADS = 12
HEAD = 64
LANES = 128
TILE = 256
VMEM_LIMIT = 60 * 1024 * 1024
MICRO = 2
N_ACT = "act"
N_ACTS = "acts"
N_ACT_T = "act_t"
N_AT = "at"
N_BG = "bg"
N_CF = "cf"
N_CG = "cg"
N_CTX = "ctx"
N_CTX_T = "ctx_t"
N_DER = "der"
N_DK = "dk"
N_DQ = "dq"
N_DV = "dv"
N_E = "e"
N_FS = "fs"
N_G = "g"
N_GA = "ga"
N_GF = "gf"
N_GRADS = "grads"
N_HG = "hg"
N_HID = "hid"
N_HIDDEN = "hidden"
N_HID_T = "hid_t"
N_IG = "ig"
N_INV = "inv"
N_K = "k"
N_KEEP1 = "keep1"
N_KEEP2 = "keep2"
N_KEEP3 = "keep3"
N_LG = "lg"
N_MASK = "mask"
N_NA = "na"
N_NF = "nf"
N_O = "o"
N_OFS = "ofs"
N_OG = "og"
N_PA = "pa"
N_PB = "pb"
N_PB0 = "pb0"
N_PB1 = "pb1"
N_PC = "pc"
N_PS = "ps"
N_Q = "q"
N_RA = "ra"
N_RES = "res"
N_RF = "rf"
N_SENT1 = "sent1"
N_SENT2 = "sent2"
N_SENT3 = "sent3"
N_V = "v"
N_VA = "va"
N_WI = "wi"
N_WK = "wk"
N_WO = "wo"
N_WORK = "work"
N_WQ = "wq"
N_WU = "wu"
N_WV = "wv"
N_X = "x"
N_X_T = "x_t"
N__T = "_t"
BF = jnp.bfloat16
F32 = jnp.float32
ANY = pl.BlockSpec(memory_space=pl.ANY)
SMEM = pl.BlockSpec(memory_space=pltpu.SMEM)
VMEM = pl.BlockSpec(memory_space=pltpu.VMEM)


def dot(left, right):
    return lax.dot_general(left, right, (((1,), (0,)), ((), ())), preferred_element_type=F32)


def dot_nt(left, right):
    return lax.dot_general(left, right, (((1,), (1,)), ((), ())), preferred_element_type=F32)


def dot_tn(left, right):
    return lax.dot_general(left, right, (((0,), (0,)), ((), ())), preferred_element_type=F32)


def gelu_pair(u):
    d = 1.0 + 0.23164188580 * jnp.abs(u)
    t = pl.reciprocal(d, approx=True)
    poly = t * (0.127414796 + t * (-0.142248368 + t * (0.7107068705 + t * (-0.7265760135 + t * 0.5307027145))))
    bell = jnp.exp2(u * u * -0.7213475204444817)
    tail = poly * bell
    cdf = jnp.where(u >= 0, 1.0 - tail, tail)
    return u * cdf, cdf + u * (bell * 0.3989422804014327)


def ds(index, size):
    if isinstance(index, int):
        return slice(index * size, (index + 1) * size)
    return pl.ds(pl.multiple_of(index * size, size), size)


def stage_query(r):
    rows, width = r.x.shape
    for j in range(width // TILE):
        cols = slice(j * TILE, (j + 1) * TILE)
        r.q[:, cols] = ((dot(r.x[...], r.wq[:, cols]) + r.bq[:, cols].astype(F32)).astype(BF) * HEAD ** -0.5).astype(BF)


def stage_key(r):
    for j in range(r.x.shape[1] // TILE):
        cols = slice(j * TILE, (j + 1) * TILE)
        r.k[:, cols] = dot(r.x[...], r.wk[:, cols]).astype(BF)


def stage_value(r):
    rows, width = r.x.shape
    one = jnp.ones((rows, LANES), BF)
    for j in range(width // TILE):
        cols = slice(j * TILE, (j + 1) * TILE)
        vv = (dot(r.x[...], r.wv[:, cols]) + r.bv[:, cols].astype(F32)).astype(BF)
        r.v[:, cols] = vv
        for h in range(TILE // LANES):
            at = (j * (TILE // LANES) + h) * TILE
            r.va[:, at:at + LANES] = vv[:, h * LANES:(h + 1) * LANES]
            r.va[:, at + LANES:at + TILE] = one


def stage_mask(r, seg_row):
    rows = r.x.shape[0]
    ids = jnp.broadcast_to(seg_row[...].astype(F32), (8, rows))
    r.mask[...] = jnp.where(jnp.transpose(ids)[:, 0:1] == ids[0:1, :], 0.0, -1e30)


def stage_attention(r):
    rows, width = r.x.shape
    low = lax.broadcasted_iota(jnp.int32, (1, LANES), 1) < HEAD
    qb = 128

    def pair(p, _):
        kp = r.k[:, ds(p, LANES)]
        vp = r.va[:, ds(p, TILE)]
        kz = [jnp.where(low, kp, jnp.zeros_like(kp)), jnp.where(low, jnp.zeros_like(kp), kp)]
        for b in range(rows // qb):
            rr = slice(b * qb, (b + 1) * qb)
            qp = r.q[rr, ds(p, LANES)]
            parts = []
            for h in range(2):
                s = dot_nt(qp, kz[h]) + r.mask[rr, :]
                top = jnp.max(s, axis=-1, keepdims=True)
                ee = jnp.exp(s - top).astype(BF)
                r.e[2 * p + h, rr, :] = ee
                o = dot(ee, vp)
                inv = 1.0 / o[:, LANES:]
                parts.append((o[:, :LANES] * inv, inv))
            c = jnp.where(low, parts[0][0], parts[1][0])
            r.inv[rr, ds(p, LANES)] = jnp.where(low, parts[0][1], parts[1][1])
            r.cf[rr, ds(p, LANES)] = c
            r.ctx[rr, ds(p, LANES)] = c.astype(BF)
        return 0

    lax.fori_loop(0, width // LANES, pair, 0, unroll=2)


def normal(r, rr, n_ref, s_ref):
    t = r.work[rr, :]
    t = t - jnp.mean(t, axis=-1, keepdims=True)
    scale = lax.rsqrt(jnp.mean(t * t, axis=-1, keepdims=True) + 1e-12)
    n = t * scale
    n_ref[rr, :] = n.astype(BF)
    s_ref[rr, :] = jnp.broadcast_to(scale, (n.shape[0], LANES))
    return n


def stage_branch(r):
    rows, width = r.x.shape
    for j in range(width // TILE):
        cols = slice(j * TILE, (j + 1) * TILE)
        r.work[:, cols] = dot(r.ctx[...], r.wo[:, cols]) + r.bo[:, cols].astype(F32) + r.x[:, cols].astype(F32)

    def norm(b, _):
        rr = ds(b, 64)
        h = normal(r, rr, r.na, r.ra) * r.ga[...].astype(F32) + r.sa[...].astype(F32)
        r.hidden[rr, :] = h
        r.hid[rr, :] = h.astype(BF)
        return 0

    lax.fori_loop(0, rows // 64, norm, 0, unroll=4)


def stage_inner(r):
    wide = r.act.shape[1]

    def feed(j, _):
        cols = ds(j, TILE)
        for b in range(r.hid.shape[0] // LANES):
            rr = slice(b * LANES, (b + 1) * LANES)
            a, g = gelu_pair(dot(r.hid[rr, :], r.wi[:, cols]) + r.bi[:, cols].astype(F32))
            r.act[rr, cols] = a.astype(BF)
            r.der[rr, cols] = g.astype(BF)
        return 0

    lax.fori_loop(0, wide // TILE, feed, 0, unroll=4)


def stage_outer(r):
    rows, width = r.x.shape
    for j in range(width // TILE):
        cols = slice(j * TILE, (j + 1) * TILE)
        r.work[:, cols] = dot(r.act[...], r.wu[:, cols]) + r.bu[:, cols].astype(F32) + r.hidden[:, cols]

    def last(b, _):
        rr = ds(b, 64)
        r.res[rr, :] = (normal(r, rr, r.nf, r.rf) * r.gf[...].astype(F32) + r.sf[...].astype(F32)).astype(BF)
        return 0

    lax.fori_loop(0, rows // 64, last, 0, unroll=4)


def norm_back(grad, n_ref, scale, gain, out, low_out, small):
    rows, width = out.shape

    def norm(b, sums):
        rr = ds(b, 64)
        t = grad[rr, :].astype(F32)
        n = n_ref[rr, :].astype(F32)
        s = t * gain[...].astype(F32)
        m1 = jnp.mean(s, axis=-1, keepdims=True)
        m2 = jnp.mean(s * n, axis=-1, keepdims=True)
        f = (s - m1 - n * m2) * scale[rr, 0:1]
        out[rr, :] = f
        low = f.astype(BF)
        low_out[rr, :] = low
        parts = (t * n, t, low.astype(F32))
        return tuple(a + jnp.sum(b.reshape(8, 8, width), axis=0) for a, b in zip(sums, parts))

    zero = jnp.zeros((8, width), F32)
    sums = lax.fori_loop(0, rows // 64, norm, (zero, zero, zero), unroll=4)
    small[...] = jnp.zeros_like(small)
    for i in range(3):
        small[i:i + 1, :width] = jnp.sum(sums[i], axis=0, keepdims=True)


def stage_inner_back(r):
    wide = r.der.shape[1]

    def inner(j, _):
        cols = ds(j, TILE)
        low = (dot_nt(r.og[...], r.wu[cols, :]) * r.der[:, cols].astype(F32)).astype(BF)
        r.ig[:, cols] = low
        return 0

    lax.fori_loop(0, wide // TILE, inner, 0, unroll=4)


def stage_hidden_back(r):
    for j in range(r.hg.shape[0] // TILE):
        rr = slice(j * TILE, (j + 1) * TILE)
        r.hg[rr, :] = r.hg[rr, :] + dot_nt(r.ig[rr, :], r.wi[...])


def stage_context_back(r):
    for j in range(r.bg.shape[1] // TILE):
        cols = slice(j * TILE, (j + 1) * TILE)
        r.cg[:, cols] = dot_nt(r.bg[...], r.wo[cols, :]).astype(BF)


def attention_back_pair(r, p):
    low = lax.broadcasted_iota(jnp.int32, (1, LANES), 1) < HEAD
    cols = ds(p, LANES)
    kp, vp, qp = r.k[:, cols], r.v[:, cols], r.q[:, cols]
    co = (r.cg[:, cols].astype(F32) * r.inv[:, cols]).astype(BF)
    prod = co.astype(F32) * r.cf[:, cols]
    qt, ct = jnp.transpose(qp), jnp.transpose(co)
    zb = jnp.zeros_like(kp)
    dqs, dks, dvs = [], [], []
    for h in range(2):
        mine = low if h == 0 else jnp.logical_not(low)
        part = slice(h * HEAD, (h + 1) * HEAD)
        weighted = jnp.sum(jnp.where(mine, prod, 0.0), axis=-1, keepdims=True)
        ee = r.e[2 * p + h]
        dp = dot_nt(jnp.where(mine, co, zb), vp) - weighted
        sg = (ee.astype(F32) * dp).astype(BF)
        dvs.append(dot(ct[part], ee))
        dqs.append(dot(sg, jnp.where(mine, kp, zb)))
        dks.append(dot(qt[part], sg))
    r.dq[:, cols] = ((dqs[0] + dqs[1]) * HEAD ** -0.5).astype(BF)
    r.dk[:, cols] = jnp.transpose(jnp.concatenate(dks, axis=0)).astype(BF)
    r.dv[:, cols] = jnp.transpose(jnp.concatenate(dvs, axis=0)).astype(BF)


def stage_attention_back(r):
    def pair(p, _):
        attention_back_pair(r, p)
        return 0

    lax.fori_loop(0, r.cg.shape[1] // LANES, pair, 0, unroll=2)


def stage_layer_grad(r):
    for j in range(r.hg.shape[1] // TILE):
        cols = slice(j * TILE, (j + 1) * TILE)
        t = r.hg[:, cols] + dot_nt(r.dq[...], r.wq[cols, :]) + dot_nt(r.dk[...], r.wk[cols, :]) + dot_nt(r.dv[...], r.wv[cols, :])
        r.lg[:, cols] = t.astype(BF)


class Refs:
    pass


class Moves:
    def __init__(self, sems):
        self.sems, self.open, self.used = sems, {}, 0

    def start(self, *pairs):
        for name, src, dst in pairs:
            self.open[name] = (src, dst, self.used)
            self.used += 1
            self.copy(name).start()

    def copy(self, name):
        src, dst, at = self.open[name]
        return pltpu.make_async_copy(src, dst, self.sems.at[at])

    def wait(self, *names):
        for name in names or list(self.open):
            self.copy(name).wait()
            del self.open[name]


KEPT = (N_X, N_CTX, N_HID, N_ACT)
STATE = (N_Q, N_K, N_V, N_E, N_INV, N_CF, N_NA, N_RA, N_DER, N_NF, N_RF)
FEED = (N_OG, N_IG, N_FS)
ATT = (N_BG, N_DQ, N_DK, N_DV, N_AT)
WEIGHTS = (N_WQ, N_WK, N_WV, N_WO, N_WI, N_WU)
VECTORS = ("bq", "bv", "bo", N_GA, "sa", "bi", "bu", N_GF, "sf")


def shapes_of(rows, width, wide):
    row, row32, broad = ((rows, width), BF), ((rows, width), F32), ((rows, wide), BF)
    square = ((width, width), BF)
    table = {n: row for n in (N_X, N_Q, N_K, N_V, N_CTX, N_NA, N_HID, N_NF, N_RES, N_G, N_OG, N_BG, N_CG, N_DQ, N_DK, N_DV, N_LG)}
    table.update({n: row32 for n in (N_INV, N_CF, N_WORK, N_HIDDEN, N_HG)})
    table.update({n: broad for n in (N_ACT, N_DER, N_IG)})
    table.update({n: square for n in (N_WQ, N_WK, N_WV, N_WO)})
    table.update(wi=((width, wide), BF), wu=((wide, width), BF), e=((HEADS, rows, rows), BF), mask=((rows, rows), F32),
                 va=((rows, 2 * width), BF), ra=((rows, LANES), F32), rf=((rows, LANES), F32), fs=((8, wide), F32), at=((8, width), F32),
                 acts=((MICRO, rows, width), BF), grads=((MICRO, rows, width), BF))
    table.update({n + N__T: (table[n][0][::-1], BF) for n in (N_ACT, N_HID, N_CTX, N_X)})
    part, rest = (8, width // 4, width), (8, width // 4 + 16, width)
    table.update(pa=((2,) + part, BF), pc=((2,) + part, BF), pb=((2,) + rest, BF), sent2=(rest, BF), keep2=(rest, BF))
    table.update({n: (part, BF) for n in (N_SENT1, N_KEEP1, N_SENT3, N_KEEP3)})
    table.update(
                 ps=((8, wide), F32), left=((2, width, rows), BF), right=((4, rows, width), BF))
    return table


def layer_call(kernel, name, sizes, small_in, big_in, outs, alias, buffers, flops, moves=40):
    table = shapes_of(*sizes)
    n_small, n_big = len(small_in), len(big_in)
    names = [n for n in outs if n in alias]

    def run(*refs):
        small, big = refs[:n_small], refs[n_small:n_small + n_big]
        at = n_small + n_big + len(names)
        out = dict(zip(outs, refs[at:at + len(outs)]))
        r = Refs()
        for n, ref in zip(buffers, refs[at + len(outs):-1]):
            setattr(r, n, ref)
        kernel(r, small, big, out, Moves(refs[-1]))

    res = pl.pallas_call(
        run,
        out_shape=[jax.ShapeDtypeStruct(*table[n]) for n in outs],
        in_specs=[SMEM] + [VMEM] * (n_small - 1) + [ANY] * (n_big + len(names)),
        out_specs=[ANY] * len(outs),
        scratch_shapes=[pltpu.VMEM(*table[n]) for n in buffers] + [pltpu.SemaphoreType.DMA((moves,))],
        input_output_aliases={n_small + n_big + i: outs.index(n) for i, n in enumerate(names)},
        compiler_params=pltpu.CompilerParams(vmem_limit_bytes=VMEM_LIMIT),
        cost_estimate=pl.CostEstimate(flops=flops, bytes_accessed=30_000_000, transcendentals=0),
        name=name,
    )(*small_in, *big_in, *[alias[n] for n in names])
    return dict(zip(outs, res))


def run_forward(go, seg, x, micro, w, acts, sizes):
    outs = (N_RES, N_ACTS) + KEPT + STATE

    def kernel(r, small, big, out, mv):
        seg_row = small[1]
        for n, ref in zip(VECTORS, small[2:]):
            setattr(r, n, ref)
        src = dict(zip(WEIGHTS, big[1:]))

        @pl.when(small[0][0] == 1)
        def _():
            forward_stages(r, seg_row, big[0] if micro is None else big[0].at[micro], src, mv,
                           lambda *names: mv.start(*[(N_O + n, getattr(r, n), out[n]) for n in names]))
            mv.start((N_ACTS, r.res, out[N_ACTS].at[micro]))
            mv.wait()

    buffers = KEPT + STATE + WEIGHTS + (N_RES, N_VA, N_MASK, N_WORK, N_HIDDEN)
    rows, width, wide = sizes
    return layer_call(kernel, "forward", sizes, [go, seg] + [w[n] for n in VECTORS], [x] + [w[n] for n in WEIGHTS], outs, {N_ACTS: acts} if micro else {},
                      buffers, 2 * rows * 12 * width * width)


def forward_stages(r, seg_row, x_src, src, mv, put):
    def load(*names):
        mv.start(*[(n, src[n], getattr(r, n)) for n in names])

    mv.start((N_X, x_src, r.x))
    load(N_WQ, N_WK, N_WV)
    stage_mask(r, seg_row)
    mv.wait(N_X, N_WQ)
    stage_query(r)
    mv.wait(N_WK)
    load(N_WO, N_WI)
    stage_key(r)
    mv.wait(N_WV)
    stage_value(r)
    put(N_X, N_Q, N_K, N_V)
    load(N_WU)
    stage_attention(r)
    put(N_E, N_INV, N_CF, N_CTX)
    mv.wait(N_WO)
    stage_branch(r)
    put(N_NA, N_RA, N_HID)
    mv.wait(N_WI)
    stage_inner(r)
    put(N_ACT, N_DER)
    mv.wait(N_WU)
    stage_outer(r)
    put(N_RES, N_NF, N_RF)


def run_layer(go, seg, x, g, micro, w, kept, sizes):
    outs = (N_ACTS, N_LG, N_GRADS) + KEPT + FEED + ATT

    def kernel(r, small, big, out, mv):
        seg_row = small[1]
        for n, ref in zip(VECTORS, small[2:]):
            setattr(r, n, ref)
        src = dict(zip(WEIGHTS, big[2:]))
        r.hg, r.ig = r.work, r.der

        def put(*names):
            mv.start(*[(N_O + n, getattr(r, n), out[n]) for n in names if n in outs])

        @pl.when(small[0][0] == 1)
        def _():
            forward_stages(r, seg_row, big[0], src, mv, put)
            mv.start((N_G, big[1].at[micro], r.g), (N_ACTS, r.res, out[N_ACTS].at[micro]))
            mv.wait(N_G)
            norm_back(r.g, r.nf, r.rf, r.gf, r.hg, r.og, r.fs)
            put(N_OG)
            stage_inner_back(r)
            put(N_IG, N_FS)
            stage_hidden_back(r)
            norm_back(r.hg, r.na, r.ra, r.ga, r.hg, r.bg, r.at)
            put(N_BG)
            stage_context_back(r)
            stage_attention_back(r)
            put(N_DQ, N_DK, N_DV)
            stage_layer_grad(r)
            put(N_LG, N_AT)
            mv.start((N_GRADS, r.lg, out[N_GRADS].at[micro]))
            mv.wait()

    buffers = KEPT + STATE + WEIGHTS + (N_RES, N_VA, N_MASK, N_WORK, N_HIDDEN, N_G, N_OG, N_FS, N_BG, N_CG, N_DQ, N_DK, N_DV,
                                        N_AT, N_LG)
    rows, width, wide = sizes
    return layer_call(kernel, "layer", sizes, [go, seg] + [w[n] for n in VECTORS], [x, g] + [w[n] for n in WEIGHTS], outs, kept,
                      buffers, 2 * rows * 26 * width * width)


def run_feed_back(go, g, state, old, w, sizes):
    outs = FEED + (N_HG,)

    def kernel(r, small, big, out, mv):
        r.gf = small[1]

        def put(*names):
            mv.start(*[(N_O + n, getattr(r, n), out[n]) for n in names])

        @pl.when(small[0][0] == 1)
        def _():
            mv.start(*[(n, src, getattr(r, n)) for n, src in zip((N_G, N_NF, N_RF), big)])
            mv.wait(N_G, N_NF, N_RF)
            mv.start((N_WU, big[3], r.wu), (N_DER, big[4], r.der))
            norm_back(r.g, r.nf, r.rf, r.gf, r.hg, r.og, r.fs)
            put(N_OG)
            mv.wait(N_WU, N_DER)
            mv.start((N_WI, big[5], r.wi))
            stage_inner_back(r)
            put(N_IG, N_FS)
            mv.wait(N_WI)
            stage_hidden_back(r)
            put(N_HG)
            mv.wait()

    rows, width, wide = sizes
    return layer_call(kernel, "feed_back", sizes, [go, w[N_GF]], [g, state[N_NF], state[N_RF], w[N_WU], state[N_DER], w[N_WI]], outs, old,
                      (N_G, N_NF, N_RF, N_WU, N_WI, N_DER, N_IG, N_OG, N_HG, N_FS), 4 * rows * wide * width)


def run_attention_back(go, hg, state, micro, old, w, sizes):
    outs = (N_GRADS,) + ATT

    def kernel(r, small, big, out, mv):
        r.ga = small[1]
        names = (N_HG, N_NA, N_RA, N_WO, N_Q, N_K, N_V, N_INV, N_CF, N_E, N_WQ, N_WK, N_WV)
        src = dict(zip(names, big))

        def load(*names):
            mv.start(*[(n, src[n], getattr(r, n)) for n in names])

        def put(*names):
            mv.start(*[(N_O + n, getattr(r, n), out[n]) for n in names])

        @pl.when(small[0][0] == 1)
        def _():
            load(N_HG, N_NA, N_RA)
            mv.wait(N_HG, N_NA, N_RA)
            load(N_WO, N_Q, N_K, N_V, N_INV, N_CF, N_E)
            norm_back(r.hg, r.na, r.ra, r.ga, r.hg, r.bg, r.at)
            put(N_BG)
            mv.wait(N_WO)
            stage_context_back(r)
            mv.wait(N_Q, N_K, N_V, N_INV, N_CF, N_E)
            load(N_WQ, N_WK, N_WV)
            stage_attention_back(r)
            put(N_DQ, N_DK, N_DV)
            mv.wait(N_WQ, N_WK, N_WV)
            stage_layer_grad(r)
            put(N_AT)
            mv.start((N_GRADS, r.lg, out[N_GRADS].at[micro]))
            mv.wait()

    rows, width, wide = sizes
    big = [hg, state[N_NA], state[N_RA], w[N_WO]] + [state[n] for n in (N_Q, N_K, N_V, N_INV, N_CF, N_E)] + [w[N_WQ], w[N_WK], w[N_WV]]
    return layer_call(kernel, "attention_back", sizes, [go, w[N_GA]], big, outs, old,
                      (N_HG, N_NA, N_RA, N_WO, N_Q, N_K, N_V, N_INV, N_CF, N_E, N_WQ, N_WK, N_WV, N_BG, N_CG, N_DQ, N_DK, N_DV, N_AT, N_LG),
                      16 * rows * width * width)


def run_flip(go, kept, old, sizes):
    outs = (N_ACT_T, N_HID_T, N_CTX_T, N_X_T)
    names = (N_ACT, N_HID, N_CTX, N_X)

    def kernel(r, small, big, out, mv):
        @pl.when(small[0][0] == 1)
        def _():
            mv.start(*[(n, src, getattr(r, n)) for n, src in zip(names, big)])
            for n in reversed(names):
                mv.wait(n)
                src, dst = getattr(r, n), getattr(r, n + N__T)

                def turn(j, _, src=src, dst=dst):
                    dst[ds(j, TILE), :] = jnp.transpose(src[:, ds(j, TILE)])
                    return 0

                lax.fori_loop(0, src.shape[1] // TILE, turn, 0)
                mv.start((n + N__T, dst, out[n + N__T]))
            mv.wait()

    return layer_call(kernel, "transposes", sizes, [go], [kept[n] for n in names], outs, old, names + outs, 4_000_000_000)


def run_partial(go, kept, f, a, sizes):
    outs = (N_PA, N_PC, N_PB, N_PS)
    names = (N_ACT, N_OG, N_HID, N_IG, N_CTX, N_BG, N_X, N_DQ, N_DK, N_DV)
    rows, width, wide = sizes
    chunk = width // 4
    per = width // chunk

    def kernel(r, small, big, out, mv):
        mv.start(*[(n, src, getattr(r, n)) for n, src in zip(names, big)])
        ones = jnp.ones((8, rows), BF)
        mv.wait(N_ACT, N_OG)
        for i in range(2):
            def first(j, _, i=i):
                cols = pl.ds(pl.multiple_of(i * (wide // 2) + 2 * j * chunk, LANES), 2 * chunk)
                t = dot_tn(r.act[:, cols], r.og[...]).astype(BF)
                r.pa[i, 2 * j] = t[:chunk]
                r.pa[i, 2 * j + 1] = t[chunk:]
                return 0

            lax.fori_loop(0, 4, first, 0, unroll=2)
        mv.start((N_PA, r.pa, out[N_PA]))
        mv.wait(N_HID, N_IG)
        r.hid_t[...] = jnp.transpose(r.hid[...])
        for b in range(4):
            g = r.ig[:, b * width:(b + 1) * width]
            t = dot(r.hid_t[...], g).astype(BF)
            for c in range(per):
                r.pc[b // 2, b % 2 * per + c] = t[c * chunk:(c + 1) * chunk]
            r.ps[:, b * width:(b + 1) * width] = dot(ones, g)
        mv.start((N_PC, r.pc, out[N_PC]), (N_PS, r.ps, out[N_PS]))
        mv.wait(N_CTX, N_BG, N_X, N_DQ, N_DK, N_DV)
        r.x_t[...] = jnp.transpose(r.x[...])
        r.ctx_t[...] = jnp.transpose(r.ctx[...])
        r.pb[:, :, chunk:, :] = jnp.zeros((2, 8, 16, width), BF)
        for n, (left, right) in enumerate(((r.ctx_t, r.bg), (r.x_t, r.dq), (r.x_t, r.dk), (r.x_t, r.dv))):
            t = dot(left[...], right[...]).astype(BF)
            for c in range(per):
                r.pb[n // 2, n % 2 * per + c, :chunk, :] = t[c * chunk:(c + 1) * chunk]
        mv.start((N_PB, r.pb, out[N_PB]))
        mv.wait()

    src = dict(kept, **f, **a)
    return layer_call(kernel, "weight_gradient_0", sizes, [go], [src[n] for n in names], outs, {},
                      names + outs + (N_HID_T, N_X_T, N_CTX_T), 2 * rows * 12 * width * width)


def run_feed(go, g, state, t1, t, p, w, sizes):
    outs = (N_FS, N_HG, N_SENT1, N_KEEP1, N_SENT3, N_KEEP3, N_PS)
    rows, width, wide = sizes
    chunk = width // 4
    per = width // chunk
    half = wide // 2

    def kernel(r, small, big, out, mv):
        r.gf = small[1]
        r.ig = r.der
        side = [1 - small[0][1], small[0][1]]
        begin = [pl.multiple_of(n * half, half) for n in side]
        mine, others = small[0][0] == 1, small[0][0] == 0

        @pl.when(mine)
        def _():
            mv.start(*[(n, src, getattr(r, n)) for n, src in zip((N_G, N_NF, N_RF), big)])

        @pl.when(others)
        def _():
            mv.start((N_OG, big[8], r.og), (N_IG, big[9], r.der))

        mv.start(("act0", big[5].at[pl.ds(begin[0], half), :], r.act_t.at[:half, :]), ("pa0", big[10].at[side[0]], r.pa.at[0]))

        @pl.when(mine)
        def _():
            mv.start((N_WU, big[3], r.wu), (N_DER, big[4], r.der))

        mv.start(("act1", big[5].at[pl.ds(begin[1], half), :], r.act_t.at[half:, :]), ("pa1", big[10].at[side[1]], r.pa.at[1]))
        mv.start((N_HID_T, big[6], r.hid_t), ("pc0", big[11].at[side[0]], r.pc.at[0]), ("pc1", big[11].at[side[1]], r.pc.at[1]))

        @pl.when(mine)
        def _():
            mv.start((N_WI, big[7], r.wi))
            mv.wait(N_G, N_NF, N_RF)
            norm_back(r.g, r.nf, r.rf, r.gf, r.hg, r.og, r.fs)
            mv.start((N_OFS, r.fs, out[N_FS]))

        @pl.when(others)
        def _():
            mv.wait(N_OG, N_IG)

        for i, n in enumerate((N_SENT1, N_KEEP1)):
            mv.wait("act%d" % i, "pa%d" % i)

            def outer(j, _, i=i):
                rr = pl.ds(pl.multiple_of(i * half + 2 * j * chunk, 2 * chunk), 2 * chunk)
                t = dot(r.act_t[rr, :], r.og[...])
                r.pa[i, 2 * j] = (r.pa[i, 2 * j].astype(F32) + t[:chunk]).astype(BF)
                r.pa[i, 2 * j + 1] = (r.pa[i, 2 * j + 1].astype(F32) + t[chunk:]).astype(BF)
                return 0

            lax.fori_loop(0, 4, outer, 0, unroll=2)
            mv.start((n, r.pa.at[i], out[n]))

        @pl.when(mine)
        def _():
            mv.wait(N_WU, N_DER)
            stage_inner_back(r)

        mv.wait(N_HID_T)
        ones = jnp.ones((8, rows), BF)
        for i, n in enumerate((N_SENT3, N_KEEP3)):
            mv.wait("pc%d" % i)
            for b in range(2):
                at = pl.multiple_of(begin[i] + b * width, width)
                part = r.der[:, pl.ds(at, width)]
                t = dot(r.hid_t[...], part)
                for c in range(per):
                    r.pc[i, b * per + c] = (r.pc[i, b * per + c].astype(F32) + t[c * chunk:(c + 1) * chunk]).astype(BF)
                r.ps[:, pl.ds(at, width)] = dot(ones, part)
            mv.start((n, r.pc.at[i], out[n]))
        mv.start((N_PS, r.ps, out[N_PS]))

        @pl.when(mine)
        def _():
            mv.wait(N_WI)
            stage_hidden_back(r)
            mv.start((N_HG, r.hg, out[N_HG]))
            mv.wait(N_HG, N_OFS)

        mv.wait(N_SENT1, N_KEEP1, N_SENT3, N_KEEP3, N_PS)

    big = [g, state[N_NF], state[N_RF], w[N_WU], state[N_DER], t[N_ACT_T], t[N_HID_T], w[N_WI], t1[N_OG], t1[N_IG], p[N_PA], p[N_PC]]
    return layer_call(kernel, "feed_gradient", sizes, [go, w[N_GF]], big, outs, {N_FS: t1[N_FS]},
                      (N_G, N_NF, N_RF, N_WU, N_WI, N_DER, N_ACT_T, N_HID_T, N_PA, N_PC, N_HG, N_OG, N_FS, N_PS), 8 * rows * width * wide)


def run_rest(go, hg, state, micro, grads, t1, t, p, sums, w, sizes):
    outs = (N_GRADS, N_SENT2, N_KEEP2)
    rows, width, wide = sizes
    names = (N_HG, N_NA, N_RA, N_WO, N_INV, N_CF, N_Q, N_K, N_V, N_E, N_WQ, N_WK, N_WV)
    right = (N_BG, N_DQ, N_DK, N_DV)

    def kernel(r, small, big, out, mv):
        r.ga, fs0, fs1, at0, at1, ps0, ps1, dq0, dv0 = small[1:]
        for i, n in enumerate(right):
            setattr(r, n, r.right.at[i])
        side = [1 - small[0][1], small[0][1]]
        mine, others = small[0][0] == 1, small[0][0] == 0
        src = dict(zip(names, big))
        pairs = width // LANES

        def load(*names):
            mv.start(*[(n, src[n], getattr(r, n)) for n in names])

        @pl.when(mine)
        def _():
            load(N_HG, N_NA, N_RA)
            load(N_WO, N_INV, N_CF, N_Q, N_K, N_V)
            for p in range(0, pairs, 2):
                mv.start(("e%d" % p, big[9].at[2 * p:2 * p + 4], r.e.at[2 * p:2 * p + 4]))
            load(N_WQ, N_WK, N_WV)

        @pl.when(others)
        def _():
            mv.start(*[(n, ref, getattr(r, n)) for n, ref in zip(right, big[15:])])

        mv.start((N_CTX_T, big[13], r.left.at[0]), (N_X_T, big[14], r.left.at[1]))
        mv.start((N_PB0, big[19].at[side[0]], r.pb.at[0]), (N_PB1, big[19].at[side[1]], r.pb.at[1]))
        chunk = r.pb.shape[2] - 16
        per = width // chunk

        @pl.when(mine)
        def _():
            mv.wait(N_HG, N_NA, N_RA)
            norm_back(r.hg, r.na, r.ra, r.ga, r.hg, r.bg, r.at)
            mv.wait(N_WO)
            stage_context_back(r)
            mv.wait(N_INV, N_CF, N_Q, N_K, N_V)
            for p in range(pairs):
                if p % 2 == 0:
                    mv.copy("e%d" % p).wait()
                    del mv.open["e%d" % p]
                attention_back_pair(r, p)

        @pl.when(others)
        def _():
            mv.wait(*right)
            r.at[...] = at1[...]

        mv.wait(N_CTX_T, N_X_T, N_PB0, N_PB1)
        ones = jnp.ones((8, rows), BF)
        fs = fs0[...] + fs1[...]
        at = at0[...] + r.at[...]
        ps = ps0[...] + ps1[...]
        dqs = dot(ones, dq0[...]) + dot(ones, r.right[1])
        dvs = dot(ones, dv0[...]) + dot(ones, r.right[3])
        lines = [dqs[0:1], dvs[0:1], at[2:3], at[0:1], at[1:2], fs[2:3, :width], fs[0:1, :width], fs[1:2, :width]]
        lines += [ps[0:1, i * width:(i + 1) * width] for i in range(wide // width)]
        lines += [jnp.zeros((16 - len(lines), width), F32)]
        lines = jnp.concatenate(lines, axis=0).astype(BF)
        r.pb[0, 0, chunk:, :] = lines
        r.pb[1, 0, chunk:, :] = lines
        for n in range(4):
            which = side[n // 2] * 2 + n % 2
            lhs = jnp.minimum(which, 1)
            v = dot(r.left[lhs], r.right[which])
            for c in range(per):
                at = n % 2 * per + c
                r.pb[n // 2, at, :chunk, :] = (r.pb[n // 2, at, :chunk, :].astype(F32) + v[c * chunk:(c + 1) * chunk]).astype(BF)
            if n % 2:
                mv.start((outs[1 + n // 2], r.pb.at[n // 2], out[outs[1 + n // 2]]))

        @pl.when(mine)
        def _():
            mv.wait(N_WQ, N_WK, N_WV)
            stage_layer_grad(r)
            mv.start((N_GRADS, r.lg, out[N_GRADS].at[micro]))
            mv.wait(N_GRADS)

        mv.wait(N_SENT2, N_KEEP2)

    big = [hg] + [state[N_NA], state[N_RA], w[N_WO]] + [state[n] for n in (N_INV, N_CF, N_Q, N_K, N_V, N_E)] + [w[N_WQ], w[N_WK], w[N_WV]]
    big += [t[N_CTX_T], t[N_X_T]] + [t1[n] for n in right] + [p[N_PB]]
    return layer_call(kernel, "attention_gradient", sizes, [go, w[N_GA]] + sums, big, outs, {N_GRADS: grads},
                      names + (N_CG, "right", "left", N_PB, N_AT, N_LG), 24 * rows * width * width)


def unpack_kernel(place, *rest, kinds, pieces, n_alias, n_lines):
    count = len(pieces)
    n_take = 2 * count * len(kinds)
    take, rest = rest[:n_take], rest[n_take:]
    lines, rest = rest[:n_lines], rest[n_lines + n_alias:]
    outs, small = rest[:n_alias], rest[n_alias:-5]
    low, high, tiny, sin, sout = rest[-5:]
    chunk, width = high.shape[1:]
    per = width // chunk
    loads = [pltpu.make_async_copy(src.at[:chunk, :], low.at[u], sin.at[u]) for u, src in enumerate(take)]
    loads += [pltpu.make_async_copy(src.at[chunk:, :], tiny.at[u], sin.at[n_take + u]) for u, src in enumerate(lines)]
    for c in loads:
        c.start()
    for u in range(n_take):
        kind, at = kinds[u // (2 * count)], u % (2 * count)
        first = sum((1, 1, 4)[k] for k in kinds[:u // (2 * count)])
        core = place[0] if at < count else 1 - place[0]
        rank = place[1] if at < count else 7 - place[1]
        index = core * 8 + lax.rem(rank + 9 - pieces[at % count], 8)
        loads[u].wait()
        high[u] = low[u].astype(F32)
        row = pl.ds(pl.multiple_of(lax.rem(index, per) * chunk, 8), chunk)
        if kind == 0:
            pltpu.make_async_copy(high.at[u], outs[first].at[pl.ds(pl.multiple_of(index * chunk, 8), chunk), :], sout.at[u]).start()
        elif kind == 1:
            col = pl.ds(pl.multiple_of(index // per * width, width), width)
            pltpu.make_async_copy(high.at[u], outs[first].at[row, col], sout.at[u]).start()
        else:
            for n in range(4):
                @pl.when(index // per == n)
                def _(n=n, u=u, row=row, first=first):
                    pltpu.make_async_copy(high.at[u], outs[first + n].at[row, :], sout.at[u]).start()
    if n_lines:
        for c in loads[n_take:]:
            c.wait()
        t = tiny[lax.rem(place[1] + 1, 8)].astype(F32)
        for i in range(8):
            small[i][...] = t[i:i + 1]
        for i in range(small[8].shape[1] // width):
            small[8][:, i * width:(i + 1) * width] = t[8 + i:9 + i]
    for u in range(n_take):
        pltpu.make_async_copy(high.at[u], outs[0].at[:chunk, :width], sout.at[u]).wait()


def run_unpack(place, rings, kinds, pieces, old, final):
    width = rings[0].pieces[0].shape[1]
    chunk = width // 4
    count, wide = len(pieces), 4 * width
    sd = jax.ShapeDtypeStruct
    shapes = [s for k in kinds for s in ([sd((wide, width), F32)], [sd((width, wide), F32)], [sd((width, width), F32)] * 4)[k]]
    lines = rings[-1].pieces if final else []
    small = [sd((1, width), F32)] * 8 + [sd((1, wide), F32)] if lines else []
    take = [side[u] for ring in rings for side in (ring.pieces, ring.others) for u in pieces]
    n_in = 1 + len(take) + len(lines)
    old = list(old or [])

    def kernel(*refs):
        inputs, rest = refs[:n_in], refs[n_in + len(old):]
        unpack_kernel(*inputs, *[None] * len(shapes), *rest, kinds=kinds, pieces=pieces, n_alias=len(shapes), n_lines=len(lines))

    n = len(take)
    return pl.pallas_call(
        kernel,
        out_shape=shapes + small,
        in_specs=[SMEM] + [ANY] * (n_in - 1 + len(old)),
        out_specs=[ANY] * len(shapes) + [VMEM] * len(small),
        scratch_shapes=[pltpu.VMEM((n, chunk, width), BF), pltpu.VMEM((n, chunk, width), F32), pltpu.VMEM((8, 16, width), BF),
                        pltpu.SemaphoreType.DMA((n + 8,)), pltpu.SemaphoreType.DMA((n,))],
        input_output_aliases={n_in + i: i for i in range(len(old))},
        compiler_params=pltpu.CompilerParams(vmem_limit_bytes=VMEM_LIMIT),
        cost_estimate=pl.CostEstimate(flops=0, bytes_accessed=6 * n * chunk * width, transcendentals=0),
        name="unpack",
    )(place, *take, *lines, *old)


def ring_tables():
    chips = [(z, 0) for z in range(4)] + [(z, 1) for z in reversed(range(4))]
    step = []
    for at, (z, y) in enumerate(chips):
        for core in range(2):
            nz, ny = chips[(at + 1) % 8] if core == 0 else chips[at - 1]
            step.append((z * 4 + y * 2 + core, nz * 4 + ny * 2 + core))
    swap = [(d, d ^ 1) for d in range(16)]
    return step, swap


def ring_place():
    d = lax.axis_index("dp")
    z, y, core = d // 4, (d // 2) % 2, d % 2
    at = jnp.where(y == 0, z, 7 - z)
    return core, jnp.where(core == 0, at, 7 - at)


def after(value, *earlier):
    return lax.optimization_barrier((value, *earlier))[0]


class Ring:
    def __init__(self, parts, rank, step, swap):
        self.parts, self.rank, self.step, self.swap = parts, rank, step, swap
        self.count, self.pieces, self.others = 0, [], []
        self.current = self.own(rank)

    def own(self, index):
        index = lax.rem(index, 8)
        return sum(lax.dynamic_index_in_dim(part, index, 0, keepdims=False) for part in self.parts)

    def advance(self):
        got = lax.ppermute(self.current, "dp", self.step)
        if self.count < 7:
            got = got + self.own(self.rank + 7 - self.count)
        self.current = got
        self.count += 1
        if self.count >= 7:
            self.pieces.append(self.current)
            self.others.append(lax.ppermute(self.current, "dp", self.swap))

    def hold(self, *earlier):
        self.current = after(self.current, *earlier)


def body(inputs, segments, cotangent, query_weight, query_bias, key_weight, value_weight, value_bias, output_weight, output_bias,
         attention_gain, attention_shift, inner_weight, inner_bias, outer_weight, outer_bias, feed_gain, feed_shift):
    micros, local, rows, width = inputs.shape
    wide = inner_weight.shape[2]
    sizes = (rows, width, wide)
    w = dict(wq=query_weight[0], wk=key_weight[0], wv=value_weight[0], wo=output_weight[0], wi=inner_weight[0], wu=outer_weight[0],
             bq=query_bias, bv=value_bias, bo=output_bias, ga=attention_gain, sa=attention_shift, bi=inner_bias, bu=outer_bias,
             gf=feed_gain, sf=feed_shift)
    x_all = inputs.reshape(micros, rows, width)
    g_all = cotangent.reshape(micros, rows, width)
    section = lax.axis_index("section")
    core, rank = ring_place()
    on0 = jnp.stack([1 - section, core]).astype(jnp.int32)
    on1 = jnp.stack([section, core]).astype(jnp.int32)
    place = jnp.stack([core, rank]).astype(jnp.int32)
    up = partial(lax.ppermute, axis_name="section", perm=[(0, 1)])
    down = partial(lax.ppermute, axis_name="section", perm=[(1, 0)])

    def some(source, names):
        return {n: source[n] for n in names}

    s0 = run_forward(on0, segments[0], x_all, 0, w, None, sizes)
    x10 = up(s0[N_RES])
    s1 = run_forward(on0, segments[1], x_all, 1, w, s0[N_ACTS], sizes)
    x11 = up(s1[N_RES])
    t0 = run_layer(after(on1, s1[N_RES]), segments[0], x10, g_all, 0, w, dict(some(s0, KEPT), acts=s1[N_ACTS]), sizes)
    g00 = down(t0[N_LG])
    flip = run_flip(after(on0, t0[N_LG]), s1, {}, sizes)
    t1 = run_layer(after(on1, flip[N_ACT_T]), segments[1], x11, g_all, 1, w, dict(some(s1, KEPT), acts=t0[N_ACTS], grads=t0[N_GRADS]), sizes)
    g01 = down(t1[N_LG])
    f0 = run_feed_back(after(on0, t1[N_LG]), g00, s0, some(t0, FEED), w, sizes)
    a0 = run_attention_back(on0, f0[N_HG], s0, 0, dict(some(t0, ATT), grads=t1[N_GRADS]), w, sizes)
    flip = run_flip(after(on1, a0[N_GRADS]), t1, flip, sizes)
    part = run_partial(on0, t0, some(f0, FEED), some(a0, ATT), sizes)
    step, swap = ring_tables()
    ring = lax.axis_size("dp") == 16
    f1 = run_feed(after(on0, part[N_PB]), g01, s1, t1, flip, part, w, sizes)
    sums = [f0[N_FS], f1[N_FS], a0[N_AT], t1[N_AT], part[N_PS], f1[N_PS], a0[N_DQ], a0[N_DV]]
    r1 = run_rest(on0, f1[N_HG], s1, 1, a0[N_GRADS], t1, flip, part, sums, w, sizes)
    if ring:
        pairs = [(f1[N_SENT1], f1[N_KEEP1]), (f1[N_SENT3], f1[N_KEEP3]), (r1[N_SENT2], r1[N_KEEP2])]
        rings = [Ring((keep, lax.ppermute(sent, "dp", swap)), rank, step, swap) for sent, keep in pairs]
        for count in range(1, 15):
            for each in rings:
                each.advance()
            now = [each.current for each in rings]
            if count == 11:
                weights = run_unpack(after(place, *now), rings, (0, 1, 2), range(4), None, False)
            if count == 12:
                for each in rings:
                    each.hold(weights[0])
            if count == 13:
                weights = run_unpack(after(place, *now), rings, (0, 1, 2), range(4, 6), weights, False)
        unpacked = run_unpack(place, rings, (0, 1, 2), range(6, 8), weights, True)
        outer_g, inner_g, fours = unpacked[0], unpacked[1], unpacked[2:]
    else:
        total = []
        for sent, keep in ((f1[N_SENT1], f1[N_KEEP1]), (f1[N_SENT3], f1[N_KEEP3]), (r1[N_SENT2], r1[N_KEEP2])):
            whole = jnp.where(core == 0, jnp.stack([keep, sent]), jnp.stack([sent, keep]))
            total.append(lax.psum(whole, "dp").astype(F32))
        tail = width // 4
        outer_g = total[0].reshape(wide, width)
        inner_g = total[1].reshape(wide // width, width, width).transpose(1, 0, 2).reshape(width, wide)
        lines = total[2][0, 0, tail:]
        fours = list(total[2][:, :, :tail].reshape(4, width, width)) + [lines[i:i + 1] for i in range(8)]
        fours.append(lines[8:8 + wide // width].reshape(1, wide))
    (wo_g, wq_g, wk_g, wv_g, bq_g, bv_g, bo_g, ga_g, sa_g, bu_g, gf_g, sf_g, bi_g) = fours
    shape = (1, micros, local, rows, width)
    return (t1[N_ACTS].reshape(shape), r1[N_GRADS].reshape(shape), wq_g[None], bq_g, wk_g[None], wv_g[None], bv_g, wo_g[None], bo_g,
            ga_g, sa_g, inner_g[None], bi_g, outer_g[None], bu_g, gf_g, sf_g)


def solution(mesh):
    rows3 = P(None, "dp", None, None)
    matrix, vector = P("section", None, None), P("section", None)
    results = P("section", None, "dp", None, None)
    return jax.shard_map(
        body,
        mesh=mesh,
        in_specs=(rows3, P(None, "dp", None), rows3, matrix, vector, matrix, matrix, vector, matrix, vector, vector, vector,
                  matrix, vector, matrix, vector, vector, vector),
        out_specs=(results, results, matrix, vector, matrix, matrix, vector, matrix, vector, vector, vector, matrix, vector,
                   matrix, vector, vector, vector),
        check_vma=False,
    )
```

```python
from functools import partial

import jax
import jax.numpy as jnp
from jax import lax
from jax.experimental import pallas as pl
from jax.experimental.pallas import tpu as pltpu
from jax.sharding import PartitionSpec as P

HEADS = 12
HEAD = 64
LANES = 128
TILE = 256
VMEM_LIMIT = 127 * 512 * 1024
MICRO = 2
N_ACT = "act"
N_ACTS = "acts"
N_ACT_T = "act_t"
N_AT = "at"
N_BG = "bg"
N_CF = "cf"
N_CG = "cg"
N_CTX = "ctx"
N_CTX_T = "ctx_t"
N_DER = "der"
N_DK = "dk"
N_DQ = "dq"
N_DV = "dv"
N_E = "e"
N_FS = "fs"
N_G = "g"
N_GA = "ga"
N_GF = "gf"
N_GRADS = "grads"
N_HG = "hg"
N_HID = "hid"
N_HIDDEN = "hidden"
N_HID_T = "hid_t"
N_IG = "ig"
N_INV = "inv"
N_K = "k"
N_KEEP1 = "keep1"
N_KEEP2 = "keep2"
N_KEEP3 = "keep3"
N_LG = "lg"
N_MASK = "mask"
N_NA = "na"
N_NF = "nf"
N_O = "o"
N_OFS = "ofs"
N_OG = "og"
N_PA = "pa"
N_PB = "pb"
N_PB0 = "pb0"
N_PB1 = "pb1"
N_PC = "pc"
N_PS = "ps"
N_Q = "q"
N_RA = "ra"
N_RES = "res"
N_RF = "rf"
N_SENT1 = "sent1"
N_SENT2 = "sent2"
N_SENT3 = "sent3"
N_V = "v"
N_VA = "va"
N_WI = "wi"
N_WK = "wk"
N_WO = "wo"
N_WORK = "work"
N_WQ = "wq"
N_WU = "wu"
N_WV = "wv"
N_X = "x"
N_X_T = "x_t"
N__T = "_t"
BF = jnp.bfloat16
F32 = jnp.float32
ANY = pl.BlockSpec(memory_space=pl.ANY)
SMEM = pl.BlockSpec(memory_space=pltpu.SMEM)
VMEM = pl.BlockSpec(memory_space=pltpu.VMEM)


def dot(left, right):
    return lax.dot_general(left, right, (((1,), (0,)), ((), ())), preferred_element_type=F32)


def dot_nt(left, right):
    return lax.dot_general(left, right, (((1,), (1,)), ((), ())), preferred_element_type=F32)


def dot_tn(left, right):
    return lax.dot_general(left, right, (((0,), (0,)), ((), ())), preferred_element_type=F32)


def gelu_pair(u):
    d = 1.0 + 0.23164188580 * jnp.abs(u)
    t = pl.reciprocal(d, approx=True)
    poly = t * (0.127414796 + t * (-0.142248368 + t * (0.7107068705 + t * (-0.7265760135 + t * 0.5307027145))))
    bell = jnp.exp2(u * u * -0.7213475204444817)
    tail = poly * bell
    cdf = jnp.where(u >= 0, 1.0 - tail, tail)
    return u * cdf, cdf + u * (bell * 0.3989422804014327)


def ds(index, size):
    if isinstance(index, int):
        return slice(index * size, (index + 1) * size)
    return pl.ds(pl.multiple_of(index * size, size), size)


def stage_query(r):
    rows, width = r.x.shape
    for j in range(width // TILE):
        cols = slice(j * TILE, (j + 1) * TILE)
        r.q[:, cols] = ((dot(r.x[...], r.wq[:, cols]) + r.bq[:, cols].astype(F32)).astype(BF) * HEAD ** -0.5).astype(BF)


def stage_key(r):
    for j in range(r.x.shape[1] // TILE):
        cols = slice(j * TILE, (j + 1) * TILE)
        r.k[:, cols] = dot(r.x[...], r.wk[:, cols]).astype(BF)


def stage_value(r):
    rows, width = r.x.shape
    one = jnp.ones((rows, LANES), BF)
    for j in range(width // TILE):
        cols = slice(j * TILE, (j + 1) * TILE)
        vv = (dot(r.x[...], r.wv[:, cols]) + r.bv[:, cols].astype(F32)).astype(BF)
        r.v[:, cols] = vv
        for h in range(TILE // LANES):
            at = (j * (TILE // LANES) + h) * TILE
            r.va[:, at:at + LANES] = vv[:, h * LANES:(h + 1) * LANES]
            r.va[:, at + LANES:at + TILE] = one


def stage_mask(r, seg_row):
    rows = r.x.shape[0]
    ids = jnp.broadcast_to(seg_row.astype(F32), (8, rows))
    r.mask[...] = jnp.where(jnp.transpose(ids)[:, 0:1] == ids[0:1, :], 0.0, -1e30)


def stage_attention(r):
    rows, width = r.x.shape
    low = lax.broadcasted_iota(jnp.int32, (1, LANES), 1) < HEAD
    qb = 128

    def pair(p, _):
        kp = r.k[:, ds(p, LANES)]
        vp = r.va[:, ds(p, TILE)]
        kz = [jnp.where(low, kp, jnp.zeros_like(kp)), jnp.where(low, jnp.zeros_like(kp), kp)]
        for b in range(rows // qb):
            rr = slice(b * qb, (b + 1) * qb)
            qp = r.q[rr, ds(p, LANES)]
            parts = []
            for h in range(2):
                s = dot_nt(qp, kz[h]) + r.mask[rr, :]
                top = jnp.max(s, axis=-1, keepdims=True)
                ee = jnp.exp(s - top).astype(BF)
                r.e[2 * p + h, rr, :] = ee
                o = dot(ee, vp)
                inv = 1.0 / o[:, LANES:]
                parts.append((o[:, :LANES] * inv, inv))
            c = jnp.where(low, parts[0][0], parts[1][0])
            r.inv[rr, ds(p, LANES)] = jnp.where(low, parts[0][1], parts[1][1])
            r.cf[rr, ds(p, LANES)] = c
            r.ctx[rr, ds(p, LANES)] = c.astype(BF)
        return 0

    lax.fori_loop(0, width // LANES, pair, 0, unroll=2)


def normal(r, rr, n_ref, s_ref):
    t = r.work[rr, :]
    t = t - jnp.mean(t, axis=-1, keepdims=True)
    scale = lax.rsqrt(jnp.mean(t * t, axis=-1, keepdims=True) + 1e-12)
    n = t * scale
    n_ref[rr, :] = n.astype(BF)
    s_ref[rr, :] = jnp.broadcast_to(scale, (n.shape[0], LANES))
    return n


def stage_branch(r):
    rows, width = r.x.shape
    for j in range(width // TILE):
        cols = slice(j * TILE, (j + 1) * TILE)
        r.work[:, cols] = dot(r.ctx[...], r.wo[:, cols]) + r.bo[:, cols].astype(F32) + r.x[:, cols].astype(F32)

    def norm(b, _):
        rr = ds(b, 64)
        h = normal(r, rr, r.na, r.ra) * r.ga[...].astype(F32) + r.sa[...].astype(F32)
        r.hidden[rr, :] = h
        r.hid[rr, :] = h.astype(BF)
        return 0

    lax.fori_loop(0, rows // 64, norm, 0, unroll=4)


def stage_inner(r):
    wide = r.act.shape[1]

    def feed(j, _):
        cols = ds(j, TILE)
        for b in range(r.hid.shape[0] // LANES):
            rr = slice(b * LANES, (b + 1) * LANES)
            a, g = gelu_pair(dot(r.hid[rr, :], r.wi[:, cols]) + r.bi[:, cols].astype(F32))
            r.act[rr, cols] = a.astype(BF)
            r.der[rr, cols] = g.astype(BF)
        return 0

    lax.fori_loop(0, wide // TILE, feed, 0, unroll=4)


def stage_outer(r):
    rows, width = r.x.shape
    for j in range(width // TILE):
        cols = slice(j * TILE, (j + 1) * TILE)
        r.work[:, cols] = dot(r.act[...], r.wu[:, cols]) + r.bu[:, cols].astype(F32) + r.hidden[:, cols]

    def last(b, _):
        rr = ds(b, 64)
        r.res[rr, :] = (normal(r, rr, r.nf, r.rf) * r.gf[...].astype(F32) + r.sf[...].astype(F32)).astype(BF)
        return 0

    lax.fori_loop(0, rows // 64, last, 0, unroll=4)


def norm_back(grad, n_ref, scale, gain, out, low_out, small):
    rows, width = out.shape

    def norm(b, sums):
        rr = ds(b, 64)
        t = grad[rr, :].astype(F32)
        n = n_ref[rr, :].astype(F32)
        s = t * gain[...].astype(F32)
        m1 = jnp.mean(s, axis=-1, keepdims=True)
        m2 = jnp.mean(s * n, axis=-1, keepdims=True)
        f = (s - m1 - n * m2) * scale[rr, 0:1]
        out[rr, :] = f
        low = f.astype(BF)
        low_out[rr, :] = low
        parts = (t * n, t, low.astype(F32))
        return tuple(a + jnp.sum(b.reshape(8, 8, width), axis=0) for a, b in zip(sums, parts))

    zero = jnp.zeros((8, width), F32)
    sums = lax.fori_loop(0, rows // 64, norm, (zero, zero, zero), unroll=8)
    small[...] = jnp.zeros_like(small)
    for i in range(3):
        small[i:i + 1, :width] = jnp.sum(sums[i], axis=0, keepdims=True)


def stage_inner_back(r):
    wide = r.der.shape[1]

    def inner(j, _):
        cols = ds(j, TILE)
        low = (dot_nt(r.og[...], r.wu[cols, :]) * r.der[:, cols].astype(F32)).astype(BF)
        r.ig[:, cols] = low
        return 0

    lax.fori_loop(0, wide // TILE, inner, 0, unroll=4)


def stage_hidden_back(r):
    for j in range(r.hg.shape[0] // TILE):
        rr = slice(j * TILE, (j + 1) * TILE)
        r.hg[rr, :] = r.hg[rr, :] + dot_nt(r.ig[rr, :], r.wi[...])


def stage_context_back(r):
    for j in range(r.bg.shape[1] // TILE):
        cols = slice(j * TILE, (j + 1) * TILE)
        r.cg[:, cols] = dot_nt(r.bg[...], r.wo[cols, :]).astype(BF)


def attention_back_pair(r, p):
    low = lax.broadcasted_iota(jnp.int32, (1, LANES), 1) < HEAD
    cols = ds(p, LANES)
    kp, vp, qp = r.k[:, cols], r.v[:, cols], r.q[:, cols]
    co = (r.cg[:, cols].astype(F32) * r.inv[:, cols]).astype(BF)
    prod = co.astype(F32) * r.cf[:, cols]
    qt, ct = jnp.transpose(qp), jnp.transpose(co)
    zb = jnp.zeros_like(kp)
    dqs, dks, dvs = [], [], []
    for h in range(2):
        mine = low if h == 0 else jnp.logical_not(low)
        part = slice(h * HEAD, (h + 1) * HEAD)
        weighted = jnp.sum(jnp.where(mine, prod, 0.0), axis=-1, keepdims=True)
        ee = r.e[2 * p + h]
        dp = dot_nt(jnp.where(mine, co, zb), vp) - weighted
        sg = (ee.astype(F32) * dp).astype(BF)
        dvs.append(dot(ct[part], ee))
        dqs.append(dot(sg, jnp.where(mine, kp, zb)))
        dks.append(dot(qt[part], sg))
    r.dq[:, cols] = ((dqs[0] + dqs[1]) * HEAD ** -0.5).astype(BF)
    r.dk[:, cols] = jnp.transpose(jnp.concatenate(dks, axis=0)).astype(BF)
    r.dv[:, cols] = jnp.transpose(jnp.concatenate(dvs, axis=0)).astype(BF)


def stage_attention_back(r):
    def pair(p, _):
        attention_back_pair(r, p)
        return 0

    lax.fori_loop(0, r.cg.shape[1] // LANES, pair, 0, unroll=2)


def stage_layer_grad(r):
    for j in range(r.hg.shape[1] // TILE):
        cols = slice(j * TILE, (j + 1) * TILE)
        t = r.hg[:, cols] + dot_nt(r.dq[...], r.wq[cols, :]) + dot_nt(r.dk[...], r.wk[cols, :]) + dot_nt(r.dv[...], r.wv[cols, :])
        r.lg[:, cols] = t.astype(BF)


class Refs:
    pass


class Moves:
    def __init__(self, sems):
        self.sems, self.open, self.used = sems, {}, 0

    def start(self, *pairs):
        for name, src, dst in pairs:
            self.open[name] = (src, dst, self.used)
            self.used += 1
            self.copy(name).start()

    def copy(self, name):
        src, dst, at = self.open[name]
        return pltpu.make_async_copy(src, dst, self.sems.at[at])

    def wait(self, *names):
        for name in names or list(self.open):
            self.copy(name).wait()
            del self.open[name]


KEPT = (N_X, N_CTX, N_HID, N_ACT)
STATE = (N_Q, N_K, N_V, N_E, N_INV, N_CF, N_NA, N_RA, N_DER, N_NF, N_RF)
FEED = (N_OG, N_IG, N_FS)
ATT = (N_BG, N_DQ, N_DK, N_DV, N_AT)
WEIGHTS = (N_WQ, N_WK, N_WV, N_WO, N_WI, N_WU)
VECTORS = ("bq", "bv", "bo", N_GA, "sa", "bi", "bu", N_GF, "sf")


def shapes_of(rows, width, wide):
    row, row32, broad = ((rows, width), BF), ((rows, width), F32), ((rows, wide), BF)
    square = ((width, width), BF)
    table = {n: row for n in (N_X, N_Q, N_K, N_V, N_CTX, N_NA, N_HID, N_NF, N_RES, N_G, N_OG, N_BG, N_CG, N_DQ, N_DK, N_DV, N_LG)}
    table.update({n: row32 for n in (N_INV, N_CF, N_WORK, N_HIDDEN, N_HG)})
    table.update({n: broad for n in (N_ACT, N_DER, N_IG)})
    table.update({n: square for n in (N_WQ, N_WK, N_WV, N_WO)})
    table.update(wi=((width, wide), BF), wu=((wide, width), BF), e=((HEADS, rows, rows), BF), mask=((rows, rows), F32),
                 va=((rows, 2 * width), BF), ra=((rows, LANES), F32), rf=((rows, LANES), F32), fs=((8, wide), F32), at=((8, width), F32),
                 acts=((MICRO, rows, width), BF), grads=((MICRO, rows, width), BF))
    table.update({n + N__T: (table[n][0][::-1], BF) for n in (N_ACT, N_HID, N_CTX, N_X)})
    part, rest = (8, width // 4, width), (8, width // 4 + 16, width)
    table.update(pa=((2,) + part, BF), pc=((2,) + part, BF), pb=((2,) + rest, BF), sent2=(rest, BF), keep2=(rest, BF))
    table.update({n: (part, BF) for n in (N_SENT1, N_KEEP1, N_SENT3, N_KEEP3)})
    table.update(
                 ps=((8, wide), F32), left=((2, width, rows), BF), right=((4, rows, width), BF))
    return table


def layer_call(kernel, name, sizes, small_in, big_in, outs, alias, buffers, flops, moves=40):
    table = shapes_of(*sizes)
    n_small, n_big = len(small_in), len(big_in)
    names = [n for n in outs if n in alias]

    def run(*refs):
        small, big = refs[:n_small], refs[n_small:n_small + n_big]
        at = n_small + n_big + len(names)
        out = dict(zip(outs, refs[at:at + len(outs)]))
        r = Refs()
        for n, ref in zip(buffers, refs[at + len(outs):-1]):
            setattr(r, n, ref)
        kernel(r, small, big, out, Moves(refs[-1]))

    res = pl.pallas_call(
        run,
        out_shape=[jax.ShapeDtypeStruct(*table[n]) for n in outs],
        in_specs=[SMEM] + [VMEM] * (n_small - 1) + [ANY] * (n_big + len(names)),
        out_specs=[ANY] * len(outs),
        scratch_shapes=[pltpu.VMEM(*table[n]) for n in buffers] + [pltpu.SemaphoreType.DMA((moves,))],
        input_output_aliases={n_small + n_big + i: outs.index(n) for i, n in enumerate(names)},
        compiler_params=pltpu.CompilerParams(vmem_limit_bytes=VMEM_LIMIT),
        cost_estimate=pl.CostEstimate(flops=flops, bytes_accessed=30_000_000, transcendentals=0),
        name=name,
    )(*small_in, *big_in, *[alias[n] for n in names])
    return dict(zip(outs, res))


def run_forward(go, seg, x, micro, w, acts, sizes):
    outs = (N_RES, N_ACTS) + KEPT + STATE

    def kernel(r, small, big, out, mv):
        seg_row = small[1]
        for n, ref in zip(VECTORS, small[2:]):
            setattr(r, n, ref)
        src = dict(zip(WEIGHTS, big[1:]))

        @pl.when(small[0][0] == 1)
        def _():
            forward_stages(r, seg_row[micro], big[0].at[micro], src, mv,
                           lambda *names: mv.start(*[(N_O + n, getattr(r, n), out[n]) for n in names]))
            mv.start((N_ACTS, r.res, out[N_ACTS].at[micro]))
            mv.wait()

    buffers = KEPT + STATE + WEIGHTS + (N_RES, N_VA, N_MASK, N_WORK, N_HIDDEN)
    rows, width, wide = sizes
    return layer_call(kernel, "forward", sizes, [go, seg] + [w[n] for n in VECTORS], [x] + [w[n] for n in WEIGHTS], outs, {N_ACTS: acts} if micro else {},
                      buffers, 2 * rows * 12 * width * width)


def forward_stages(r, seg_row, x_src, src, mv, put):
    def load(*names):
        mv.start(*[(n, src[n], getattr(r, n)) for n in names])

    mv.start((N_X, x_src, r.x))
    load(N_WQ, N_WK, N_WV)
    stage_mask(r, seg_row)
    mv.wait(N_X, N_WQ)
    stage_query(r)
    mv.wait(N_WK)
    load(N_WO, N_WI)
    stage_key(r)
    mv.wait(N_WV)
    stage_value(r)
    put(N_X, N_Q, N_K, N_V)
    load(N_WU)
    stage_attention(r)
    put(N_E, N_INV, N_CF, N_CTX)
    mv.wait(N_WO)
    stage_branch(r)
    put(N_NA, N_RA, N_HID)
    mv.wait(N_WI)
    stage_inner(r)
    put(N_ACT, N_DER)
    mv.wait(N_WU)
    stage_outer(r)
    put(N_RES, N_NF, N_RF)


def run_layer(go, seg, x, g, micro, w, kept, sizes):
    outs = (N_ACTS, N_LG, N_GRADS) + KEPT + FEED + ATT

    def kernel(r, small, big, out, mv):
        seg_row = small[1]
        for n, ref in zip(VECTORS, small[2:]):
            setattr(r, n, ref)
        src = dict(zip(WEIGHTS, big[2:]))
        r.hg, r.ig = r.work, r.der

        def put(*names):
            mv.start(*[(N_O + n, getattr(r, n), out[n]) for n in names if n in outs])

        @pl.when(small[0][0] == 1)
        def _():
            forward_stages(r, seg_row[micro], big[0], src, mv, put)
            mv.start((N_G, big[1].at[micro], r.g), (N_ACTS, r.res, out[N_ACTS].at[micro]))
            mv.wait(N_G)
            norm_back(r.g, r.nf, r.rf, r.gf, r.hg, r.og, r.fs)
            put(N_OG)
            stage_inner_back(r)
            put(N_IG, N_FS)
            stage_hidden_back(r)
            norm_back(r.hg, r.na, r.ra, r.ga, r.hg, r.bg, r.at)
            put(N_BG)
            stage_context_back(r)
            stage_attention_back(r)
            put(N_DQ, N_DK, N_DV)
            stage_layer_grad(r)
            put(N_LG, N_AT)
            mv.start((N_GRADS, r.lg, out[N_GRADS].at[micro]))
            mv.wait()

    buffers = KEPT + STATE + WEIGHTS + (N_RES, N_VA, N_MASK, N_WORK, N_HIDDEN, N_G, N_OG, N_FS, N_BG, N_CG, N_DQ, N_DK, N_DV,
                                        N_AT, N_LG)
    rows, width, wide = sizes
    return layer_call(kernel, "layer", sizes, [go, seg] + [w[n] for n in VECTORS], [x, g] + [w[n] for n in WEIGHTS], outs, kept,
                      buffers, 2 * rows * 26 * width * width)


def run_back(go, g, state, micro, old, w, sizes):
    outs = (N_GRADS,) + FEED + ATT
    names = (N_G, N_NF, N_RF, N_WU, N_DER, N_WI, N_NA, N_RA, N_WO, N_Q, N_K, N_V, N_INV, N_CF, N_E, N_WQ, N_WK, N_WV)

    def kernel(r, small, big, out, mv):
        r.gf, r.ga = small[1:3]
        r.ig = r.der
        src = dict(zip(names, big))

        def load(*names):
            mv.start(*[(n, src[n], getattr(r, n)) for n in names])

        def put(*names):
            mv.start(*[(N_O + n, getattr(r, n), out[n]) for n in names])

        @pl.when(small[0][0] == 1)
        def _():
            load(N_G, N_NF, N_RF)
            load(N_WU, N_DER)
            mv.wait(N_G, N_NF, N_RF)
            norm_back(r.g, r.nf, r.rf, r.gf, r.hg, r.og, r.fs)
            put(N_OG)
            mv.wait(N_WU, N_DER)
            load(N_WI, N_NA, N_RA, N_WO)
            stage_inner_back(r)
            put(N_IG, N_FS)
            mv.wait(N_WI)
            load(N_Q, N_K, N_V, N_INV, N_CF, N_E)
            stage_hidden_back(r)
            mv.wait(N_NA, N_RA, N_WO)
            norm_back(r.hg, r.na, r.ra, r.ga, r.hg, r.bg, r.at)
            put(N_BG, N_AT)
            load(N_WQ, N_WK, N_WV)
            stage_context_back(r)
            mv.wait(N_Q, N_K, N_V, N_INV, N_CF, N_E)
            stage_attention_back(r)
            put(N_DQ, N_DK, N_DV)
            mv.wait(N_WQ, N_WK, N_WV)
            stage_layer_grad(r)
            mv.start((N_GRADS, r.lg, out[N_GRADS].at[micro]))
            mv.wait()

    rows, width, wide = sizes
    big = [g, state[N_NF], state[N_RF], w[N_WU], state[N_DER], w[N_WI], state[N_NA], state[N_RA], w[N_WO]]
    big += [state[n] for n in (N_Q, N_K, N_V, N_INV, N_CF, N_E)] + [w[N_WQ], w[N_WK], w[N_WV]]
    return layer_call(kernel, "backward", sizes, [go, w[N_GF], w[N_GA]], big, outs, old,
                      names + (N_OG, N_HG, N_FS, N_BG, N_CG, N_DQ, N_DK, N_DV, N_AT, N_LG), 2 * rows * 14 * width * width)


def run_flip(go, kept, old, sizes):
    outs = (N_ACT_T, N_HID_T, N_CTX_T, N_X_T)
    names = (N_ACT, N_HID, N_CTX, N_X)

    def kernel(r, small, big, out, mv):
        @pl.when(small[0][0] == 1)
        def _():
            mv.start(*[(n, src, getattr(r, n)) for n, src in zip(names, big)])
            for n in reversed(names):
                mv.wait(n)
                src, dst = getattr(r, n), getattr(r, n + N__T)

                def turn(j, _, src=src, dst=dst):
                    dst[ds(j, TILE), :] = jnp.transpose(src[:, ds(j, TILE)])
                    return 0

                lax.fori_loop(0, src.shape[1] // TILE, turn, 0)
                mv.start((n + N__T, dst, out[n + N__T]))
            mv.wait()

    return layer_call(kernel, "transposes", sizes, [go], [kept[n] for n in names], outs, old, names + outs, 4_000_000_000)


def run_partial(go, kept, a, kept1, flip, sizes):
    turned = (N_ACT_T, N_HID_T, N_CTX_T, N_X_T)
    outs = (N_PA, N_PC, N_PB, N_PS) + turned
    names = (N_ACT, N_OG, N_HID, N_IG, N_CTX, N_BG, N_X, N_DQ, N_DK, N_DV)
    rows, width, wide = sizes
    chunk = width // 4
    per = width // chunk

    def kernel(r, small, big, out, mv):
        mv.start(*[(n, src, getattr(r, n)) for n, src in zip(names, big)])
        ones = jnp.ones((8, rows), BF)
        mv.wait(N_ACT, N_OG)
        for i in range(2):
            def first(j, _, i=i):
                cols = pl.ds(pl.multiple_of(i * (wide // 2) + 2 * j * chunk, LANES), 2 * chunk)
                t = dot_tn(r.act[:, cols], r.og[...]).astype(BF)
                r.pa[i, 2 * j] = t[:chunk]
                r.pa[i, 2 * j + 1] = t[chunk:]
                return 0

            lax.fori_loop(0, 4, first, 0, unroll=2)
        mv.start((N_PA, r.pa, out[N_PA]))
        mv.wait(N_HID, N_IG)
        r.hid_t[...] = jnp.transpose(r.hid[...])
        for b in range(4):
            g = r.ig[:, b * width:(b + 1) * width]
            t = dot(r.hid_t[...], g).astype(BF)
            for c in range(per):
                r.pc[b // 2, b % 2 * per + c] = t[c * chunk:(c + 1) * chunk]
            r.ps[:, b * width:(b + 1) * width] = dot(ones, g)
        mv.start((N_PC, r.pc, out[N_PC]), (N_PS, r.ps, out[N_PS]))
        mv.wait(N_CTX, N_BG, N_X, N_DQ, N_DK, N_DV)
        r.x_t[...] = jnp.transpose(r.x[...])
        r.ctx_t[...] = jnp.transpose(r.ctx[...])
        r.pb[:, :, chunk:, :] = jnp.zeros((2, 8, 16, width), BF)
        for n, (left, right) in enumerate(((r.ctx_t, r.bg), (r.x_t, r.dq), (r.x_t, r.dk), (r.x_t, r.dv))):
            t = dot(left[...], right[...]).astype(BF)
            for c in range(per):
                r.pb[n // 2, n % 2 * per + c, :chunk, :] = t[c * chunk:(c + 1) * chunk]
        mv.start((N_PB, r.pb, out[N_PB]))

        @pl.when(small[0][0] == 0)
        def _():
            for i, n in enumerate((N_ACT, N_HID, N_CTX, N_X)):
                mv.start((n, big[10 + i], getattr(r, n)))
            for i, n in enumerate((N_ACT, N_HID, N_CTX, N_X)):
                mv.wait(n)
                src, dst = getattr(r, n), getattr(r, turned[i])

                def turn(j, _, src=src, dst=dst):
                    dst[ds(j, TILE), :] = jnp.transpose(src[:, ds(j, TILE)])
                    return 0

                lax.fori_loop(0, src.shape[1] // TILE, turn, 0)
                mv.start((turned[i], dst, out[turned[i]]))
            mv.wait(*turned)

        mv.wait(N_PA, N_PC, N_PB, N_PS)

    src = dict(kept, **a)
    big = [src[n] for n in names] + [kept1[n] for n in (N_ACT, N_HID, N_CTX, N_X)]
    res = layer_call(kernel, "weight_gradient_0", sizes, [go], big, outs, flip, names + outs, 2 * rows * 12 * width * width)
    return res, res


def run_feed(go, g, state, t1, t, p, w, sizes):
    outs = (N_FS, N_HG, N_SENT1, N_KEEP1, N_SENT3, N_KEEP3, N_PS)
    rows, width, wide = sizes
    chunk = width // 4
    per = width // chunk
    half = wide // 2

    def kernel(r, small, big, out, mv):
        r.gf = small[1]
        r.ig = r.der
        side = [1 - small[0][1], small[0][1]]
        begin = [pl.multiple_of(n * half, half) for n in side]
        mine, others = small[0][0] == 1, small[0][0] == 0

        @pl.when(mine)
        def _():
            mv.start(*[(n, src, getattr(r, n)) for n, src in zip((N_G, N_NF, N_RF), big)])

        @pl.when(others)
        def _():
            mv.start((N_OG, big[8], r.og), (N_IG, big[9], r.der))

        mv.start(("act0", big[5].at[pl.ds(begin[0], half), :], r.act_t.at[:half, :]), ("pa0", big[10].at[side[0]], r.pa.at[0]))

        @pl.when(mine)
        def _():
            mv.start((N_WU, big[3], r.wu), (N_DER, big[4], r.der))

        mv.start(("act1", big[5].at[pl.ds(begin[1], half), :], r.act_t.at[half:, :]), ("pa1", big[10].at[side[1]], r.pa.at[1]))
        mv.start((N_HID_T, big[6], r.hid_t), ("pc0", big[11].at[side[0]], r.pc.at[0]), ("pc1", big[11].at[side[1]], r.pc.at[1]))

        @pl.when(mine)
        def _():
            mv.start((N_WI, big[7], r.wi))
            mv.wait(N_G, N_NF, N_RF)
            norm_back(r.g, r.nf, r.rf, r.gf, r.hg, r.og, r.fs)
            mv.start((N_OFS, r.fs, out[N_FS]))

        @pl.when(others)
        def _():
            mv.wait(N_OG, N_IG)

        for i, n in enumerate((N_SENT1, N_KEEP1)):
            mv.wait("act%d" % i, "pa%d" % i)

            def outer(j, _, i=i):
                rr = pl.ds(pl.multiple_of(i * half + 2 * j * chunk, 2 * chunk), 2 * chunk)
                t = dot(r.act_t[rr, :], r.og[...])
                r.pa[i, 2 * j] = (r.pa[i, 2 * j].astype(F32) + t[:chunk]).astype(BF)
                r.pa[i, 2 * j + 1] = (r.pa[i, 2 * j + 1].astype(F32) + t[chunk:]).astype(BF)
                return 0

            lax.fori_loop(0, 4, outer, 0, unroll=2)
            mv.start((n, r.pa.at[i], out[n]))

        @pl.when(mine)
        def _():
            mv.wait(N_WU, N_DER)
            stage_inner_back(r)

        mv.wait(N_HID_T)
        ones = jnp.ones((8, rows), BF)
        for i, n in enumerate((N_SENT3, N_KEEP3)):
            mv.wait("pc%d" % i)
            for b in range(2):
                at = pl.multiple_of(begin[i] + b * width, width)
                part = r.der[:, pl.ds(at, width)]
                t = dot(r.hid_t[...], part)
                for c in range(per):
                    r.pc[i, b * per + c] = (r.pc[i, b * per + c].astype(F32) + t[c * chunk:(c + 1) * chunk]).astype(BF)
                r.ps[:, pl.ds(at, width)] = dot(ones, part)
            mv.start((n, r.pc.at[i], out[n]))
        mv.start((N_PS, r.ps, out[N_PS]))

        @pl.when(mine)
        def _():
            mv.wait(N_WI)
            stage_hidden_back(r)
            mv.start((N_HG, r.hg, out[N_HG]))
            mv.wait(N_HG, N_OFS)

        mv.wait(N_SENT1, N_KEEP1, N_SENT3, N_KEEP3, N_PS)

    big = [g, state[N_NF], state[N_RF], w[N_WU], state[N_DER], t[N_ACT_T], t[N_HID_T], w[N_WI], t1[N_OG], t1[N_IG], p[N_PA], p[N_PC]]
    return layer_call(kernel, "feed_gradient", sizes, [go, w[N_GF]], big, outs, {N_FS: t1[N_FS]},
                      (N_G, N_NF, N_RF, N_WU, N_WI, N_DER, N_ACT_T, N_HID_T, N_PA, N_PC, N_HG, N_OG, N_FS, N_PS), 8 * rows * width * wide)


def run_rest(go, hg, state, micro, grads, t1, t, p, sums, w, sizes):
    outs = (N_GRADS, N_SENT2, N_KEEP2)
    rows, width, wide = sizes
    names = (N_HG, N_NA, N_RA, N_WO, N_INV, N_CF, N_Q, N_K, N_V, N_E, N_WQ, N_WK, N_WV)
    right = (N_BG, N_DQ, N_DK, N_DV)

    def kernel(r, small, big, out, mv):
        r.ga, fs0, fs1, at0, at1, ps0, ps1, dq0, dv0 = small[1:]
        for i, n in enumerate(right):
            setattr(r, n, r.right.at[i])
        side = [1 - small[0][1], small[0][1]]
        mine, others = small[0][0] == 1, small[0][0] == 0
        src = dict(zip(names, big))
        pairs = width // LANES

        def load(*names):
            mv.start(*[(n, src[n], getattr(r, n)) for n in names])

        @pl.when(mine)
        def _():
            load(N_HG, N_NA, N_RA)
            load(N_WO, N_INV, N_CF, N_Q, N_K, N_V)
            for p in range(0, pairs, 2):
                mv.start(("e%d" % p, big[9].at[2 * p:2 * p + 4], r.e.at[2 * p:2 * p + 4]))
            load(N_WQ, N_WK, N_WV)

        @pl.when(others)
        def _():
            mv.start(*[(n, ref, getattr(r, n)) for n, ref in zip(right, big[15:])])

        mv.start((N_CTX_T, big[13], r.left.at[0]), (N_X_T, big[14], r.left.at[1]))
        mv.start((N_PB0, big[19].at[side[0]], r.pb.at[0]), (N_PB1, big[19].at[side[1]], r.pb.at[1]))
        chunk = r.pb.shape[2] - 16
        per = width // chunk

        @pl.when(mine)
        def _():
            mv.wait(N_HG, N_NA, N_RA)
            norm_back(r.hg, r.na, r.ra, r.ga, r.hg, r.bg, r.at)
            mv.wait(N_WO)
            stage_context_back(r)
            mv.wait(N_INV, N_CF, N_Q, N_K, N_V)
            for p in range(pairs):
                if p % 2 == 0:
                    mv.copy("e%d" % p).wait()
                    del mv.open["e%d" % p]
                attention_back_pair(r, p)

        @pl.when(others)
        def _():
            mv.wait(*right)
            r.at[...] = at1[...]

        mv.wait(N_CTX_T, N_X_T, N_PB0, N_PB1)
        ones = jnp.ones((8, rows), BF)
        fs = fs0[...] + fs1[...]
        at = at0[...] + r.at[...]
        ps = ps0[...] + ps1[...]
        dqs = dot(ones, dq0[...]) + dot(ones, r.right[1])
        dvs = dot(ones, dv0[...]) + dot(ones, r.right[3])
        lines = [dqs[0:1], dvs[0:1], at[2:3], at[0:1], at[1:2], fs[2:3, :width], fs[0:1, :width], fs[1:2, :width]]
        lines += [ps[0:1, i * width:(i + 1) * width] for i in range(wide // width)]
        lines += [jnp.zeros((16 - len(lines), width), F32)]
        lines = jnp.concatenate(lines, axis=0).astype(BF)
        r.pb[0, 0, chunk:, :] = lines
        r.pb[1, 0, chunk:, :] = lines
        for n in range(4):
            which = side[n // 2] * 2 + n % 2
            lhs = jnp.minimum(which, 1)
            v = dot(r.left[lhs], r.right[which])
            for c in range(per):
                at = n % 2 * per + c
                r.pb[n // 2, at, :chunk, :] = (r.pb[n // 2, at, :chunk, :].astype(F32) + v[c * chunk:(c + 1) * chunk]).astype(BF)
            if n % 2:
                mv.start((outs[1 + n // 2], r.pb.at[n // 2], out[outs[1 + n // 2]]))

        @pl.when(mine)
        def _():
            mv.wait(N_WQ, N_WK, N_WV)
            stage_layer_grad(r)
            mv.start((N_GRADS, r.lg, out[N_GRADS].at[micro]))
            mv.wait(N_GRADS)

        mv.wait(N_SENT2, N_KEEP2)

    big = [hg] + [state[N_NA], state[N_RA], w[N_WO]] + [state[n] for n in (N_INV, N_CF, N_Q, N_K, N_V, N_E)] + [w[N_WQ], w[N_WK], w[N_WV]]
    big += [t[N_CTX_T], t[N_X_T]] + [t1[n] for n in right] + [p[N_PB]]
    return layer_call(kernel, "attention_gradient", sizes, [go, w[N_GA]] + sums, big, outs, {N_GRADS: grads},
                      names + (N_CG, "right", "left", N_PB, N_AT, N_LG), 24 * rows * width * width)


def unpack_kernel(place, *rest, kinds, pieces, n_alias, n_lines):
    count = len(pieces)
    n_take = 2 * count * len(kinds)
    take, rest = rest[:n_take], rest[n_take:]
    lines, rest = rest[:n_lines], rest[n_lines + n_alias:]
    outs, small = rest[:n_alias], rest[n_alias:-5]
    low, high, tiny, sin, sout = rest[-5:]
    chunk, width = high.shape[1:]
    per = width // chunk
    loads = [pltpu.make_async_copy(src.at[:chunk, :], low.at[u], sin.at[u]) for u, src in enumerate(take)]
    loads += [pltpu.make_async_copy(src.at[chunk:, :], tiny.at[u], sin.at[n_take + u]) for u, src in enumerate(lines)]
    for c in loads:
        c.start()
    for u in range(n_take):
        kind, at = kinds[u // (2 * count)], u % (2 * count)
        first = sum((1, 1, 4)[k] for k in kinds[:u // (2 * count)])
        core = place[0] if at < count else 1 - place[0]
        rank = place[1] if at < count else 7 - place[1]
        index = core * 8 + lax.rem(rank + 9 - pieces[at % count], 8)
        loads[u].wait()
        high[u] = low[u].astype(F32)
        row = pl.ds(pl.multiple_of(lax.rem(index, per) * chunk, 8), chunk)
        if kind == 0:
            pltpu.make_async_copy(high.at[u], outs[first].at[pl.ds(pl.multiple_of(index * chunk, 8), chunk), :], sout.at[u]).start()
        elif kind == 1:
            col = pl.ds(pl.multiple_of(index // per * width, width), width)
            pltpu.make_async_copy(high.at[u], outs[first].at[row, col], sout.at[u]).start()
        else:
            for n in range(4):
                @pl.when(index // per == n)
                def _(n=n, u=u, row=row, first=first):
                    pltpu.make_async_copy(high.at[u], outs[first + n].at[row, :], sout.at[u]).start()
    if n_lines:
        for c in loads[n_take:]:
            c.wait()
        t = tiny[lax.rem(place[1] + 1, 8)].astype(F32)
        for i in range(8):
            small[i][...] = t[i:i + 1]
        for i in range(small[8].shape[1] // width):
            small[8][:, i * width:(i + 1) * width] = t[8 + i:9 + i]
    for u in range(n_take):
        pltpu.make_async_copy(high.at[u], outs[0].at[:chunk, :width], sout.at[u]).wait()


def run_unpack(place, rings, kinds, pieces, old, final):
    width = rings[0].pieces[0].shape[1]
    chunk = width // 4
    count, wide = len(pieces), 4 * width
    sd = jax.ShapeDtypeStruct
    shapes = [s for k in kinds for s in ([sd((wide, width), F32)], [sd((width, wide), F32)], [sd((width, width), F32)] * 4)[k]]
    lines = rings[-1].pieces if final else []
    small = [sd((1, width), F32)] * 8 + [sd((1, wide), F32)] if lines else []
    take = [side[u] for ring in rings for side in (ring.pieces, ring.others) for u in pieces]
    n_in = 1 + len(take) + len(lines)
    old = list(old or [])

    def kernel(*refs):
        inputs, rest = refs[:n_in], refs[n_in + len(old):]
        unpack_kernel(*inputs, *[None] * len(shapes), *rest, kinds=kinds, pieces=pieces, n_alias=len(shapes), n_lines=len(lines))

    n = len(take)
    return pl.pallas_call(
        kernel,
        out_shape=shapes + small,
        in_specs=[SMEM] + [ANY] * (n_in - 1 + len(old)),
        out_specs=[ANY] * len(shapes) + [VMEM] * len(small),
        scratch_shapes=[pltpu.VMEM((n, chunk, width), BF), pltpu.VMEM((n, chunk, width), F32), pltpu.VMEM((8, 16, width), BF),
                        pltpu.SemaphoreType.DMA((n + 8,)), pltpu.SemaphoreType.DMA((n,))],
        input_output_aliases={n_in + i: i for i in range(len(old))},
        compiler_params=pltpu.CompilerParams(vmem_limit_bytes=VMEM_LIMIT),
        cost_estimate=pl.CostEstimate(flops=0, bytes_accessed=6 * n * chunk * width, transcendentals=0),
        name="unpack",
    )(place, *take, *lines, *old)


def ring_tables():
    chips = [(z, 0) for z in range(4)] + [(z, 1) for z in reversed(range(4))]
    step = []
    for at, (z, y) in enumerate(chips):
        for core in range(2):
            nz, ny = chips[(at + 1) % 8] if core == 0 else chips[at - 1]
            step.append((z * 4 + y * 2 + core, nz * 4 + ny * 2 + core))
    swap = [(d, d ^ 1) for d in range(16)]
    return step, swap


def ring_place():
    d = lax.axis_index("dp")
    z, y, core = d // 4, (d // 2) % 2, d % 2
    at = jnp.where(y == 0, z, 7 - z)
    return core, jnp.where(core == 0, at, 7 - at)


def after(value, *earlier):
    return lax.optimization_barrier((value, *earlier))[0]


class Ring:
    def __init__(self, parts, rank, step, swap):
        self.parts, self.rank, self.step, self.swap = parts, rank, step, swap
        self.count, self.pieces, self.others = 0, [], []
        self.current = self.own(rank)

    def own(self, index):
        index = lax.rem(index, 8)
        return sum(lax.dynamic_index_in_dim(part, index, 0, keepdims=False) for part in self.parts)

    def advance(self):
        got = lax.ppermute(self.current, "dp", self.step)
        if self.count < 7:
            got = got + self.own(self.rank + 7 - self.count)
        self.current = got
        self.count += 1
        if self.count >= 7:
            self.pieces.append(self.current)
            self.others.append(lax.ppermute(self.current, "dp", self.swap))

    def hold(self, *earlier):
        self.current = after(self.current, *earlier)


def body(inputs, segments, cotangent, query_weight, query_bias, key_weight, value_weight, value_bias, output_weight, output_bias,
         attention_gain, attention_shift, inner_weight, inner_bias, outer_weight, outer_bias, feed_gain, feed_shift):
    micros, local, rows, width = inputs.shape
    wide = inner_weight.shape[2]
    sizes = (rows, width, wide)
    w = dict(wq=query_weight[0], wk=key_weight[0], wv=value_weight[0], wo=output_weight[0], wi=inner_weight[0], wu=outer_weight[0],
             bq=query_bias, bv=value_bias, bo=output_bias, ga=attention_gain, sa=attention_shift, bi=inner_bias, bu=outer_bias,
             gf=feed_gain, sf=feed_shift)
    x_all = inputs.reshape(micros, rows, width)
    g_all = cotangent.reshape(micros, rows, width)
    section = lax.axis_index("section")
    core, rank = ring_place()
    on0 = jnp.stack([1 - section, core]).astype(jnp.int32)
    on1 = jnp.stack([section, core]).astype(jnp.int32)
    place = jnp.stack([core, rank]).astype(jnp.int32)
    up = partial(lax.ppermute, axis_name="section", perm=[(0, 1)])
    down = partial(lax.ppermute, axis_name="section", perm=[(1, 0)])

    def some(source, names):
        return {n: source[n] for n in names}

    s0 = run_forward(on0, segments, x_all, 0, w, None, sizes)
    x10 = up(s0[N_RES])
    s1 = run_forward(on0, segments, x_all, 1, w, s0[N_ACTS], sizes)
    x11 = up(s1[N_RES])
    flip = run_flip(after(on0, s1[N_RES]), s1, {}, sizes)
    t0 = run_layer(after(on1, flip[N_ACT_T]), segments, x10, g_all, 0, w, dict(some(s0, KEPT), acts=s1[N_ACTS]), sizes)
    g00 = down(t0[N_LG])
    t1 = run_layer(after(on1, t0[N_LG]), segments, x11, g_all, 1, w, dict(some(s1, KEPT), acts=t0[N_ACTS], grads=t0[N_GRADS]), sizes)
    g01 = down(t1[N_LG])
    a0 = run_back(after(on0, t1[N_LG]), g00, s0, 0, dict(some(t0, FEED + ATT), grads=t1[N_GRADS]), w, sizes)
    part, flip = run_partial(after(on0, a0[N_GRADS]), t0, a0, t1, flip, sizes)
    step, swap = ring_tables()
    ring = lax.axis_size("dp") == 16
    f1 = run_feed(after(on0, part[N_PB]), g01, s1, t1, flip, part, w, sizes)
    sums = [a0[N_FS], f1[N_FS], a0[N_AT], t1[N_AT], part[N_PS], f1[N_PS], a0[N_DQ], a0[N_DV]]
    r1 = run_rest(on0, f1[N_HG], s1, 1, a0[N_GRADS], t1, flip, part, sums, w, sizes)
    if ring:
        pairs = [(f1[N_SENT1], f1[N_KEEP1]), (f1[N_SENT3], f1[N_KEEP3]), (r1[N_SENT2], r1[N_KEEP2])]
        rings = []
        for sent, keep in pairs:
            first = after(rank, *[each.current for each in rings])
            rings.append(Ring((keep, lax.ppermute(sent, "dp", swap)), first, step, swap))
        for count in range(1, 15):
            for each in rings:
                each.advance()
            if count == 11:
                weights = run_unpack(after(place, *[each.current for each in rings]), rings, (0, 1, 2), range(4), None, False)
            if count == 12:
                for each in rings:
                    each.hold(weights[0])
        unpacked = run_unpack(place, rings, (0, 1, 2), range(4, 8), weights, True)
        outer_g, inner_g, fours = unpacked[0], unpacked[1], unpacked[2:]
    else:
        total = []
        for sent, keep in ((f1[N_SENT1], f1[N_KEEP1]), (f1[N_SENT3], f1[N_KEEP3]), (r1[N_SENT2], r1[N_KEEP2])):
            whole = jnp.where(core == 0, jnp.stack([keep, sent]), jnp.stack([sent, keep]))
            total.append(lax.psum(whole, "dp").astype(F32))
        tail = width // 4
        outer_g = total[0].reshape(wide, width)
        inner_g = total[1].reshape(wide // width, width, width).transpose(1, 0, 2).reshape(width, wide)
        lines = total[2][0, 0, tail:]
        fours = list(total[2][:, :, :tail].reshape(4, width, width)) + [lines[i:i + 1] for i in range(8)]
        fours.append(lines[8:8 + wide // width].reshape(1, wide))
    (wo_g, wq_g, wk_g, wv_g, bq_g, bv_g, bo_g, ga_g, sa_g, bu_g, gf_g, sf_g, bi_g) = fours
    shape = (1, micros, local, rows, width)
    return (t1[N_ACTS].reshape(shape), r1[N_GRADS].reshape(shape), wq_g[None], bq_g, wk_g[None], wv_g[None], bv_g, wo_g[None], bo_g,
            ga_g, sa_g, inner_g[None], bi_g, outer_g[None], bu_g, gf_g, sf_g)


def solution(mesh):
    rows3 = P(None, "dp", None, None)
    matrix, vector = P("section", None, None), P("section", None)
    results = P("section", None, "dp", None, None)
    return jax.shard_map(
        body,
        mesh=mesh,
        in_specs=(rows3, P(None, "dp", None), rows3, matrix, vector, matrix, matrix, vector, matrix, vector, vector, vector,
                  matrix, vector, matrix, vector, vector, vector),
        out_specs=(results, results, matrix, vector, matrix, matrix, vector, matrix, vector, vector, vector, matrix, vector,
                   matrix, vector, vector, vector),
        check_vma=False,
    )
```

```python
from functools import partial

import jax
import jax.numpy as jnp
from jax import lax
from jax.experimental import pallas as pl
from jax.experimental.pallas import tpu as pltpu
from jax.sharding import PartitionSpec as P

HEADS = 12
HEAD = 64
LANES = 128
TILE = 256
VMEM_LIMIT = 127 * 512 * 1024
MICRO = 2
N_ACT = "act"
N_ACTS = "acts"
N_ACT_T = "act_t"
N_AT = "at"
N_BG = "bg"
N_CF = "cf"
N_CG = "cg"
N_CTX = "ctx"
N_CTX_T = "ctx_t"
N_DER = "der"
N_DK = "dk"
N_DQ = "dq"
N_DV = "dv"
N_E = "e"
N_FS = "fs"
N_G = "g"
N_GA = "ga"
N_GF = "gf"
N_GRADS = "grads"
N_HG = "hg"
N_HID = "hid"
N_HIDDEN = "hidden"
N_HID_T = "hid_t"
N_IG = "ig"
N_INV = "inv"
N_K = "k"
N_KEEP1 = "keep1"
N_KEEP2 = "keep2"
N_KEEP3 = "keep3"
N_LG = "lg"
N_MASK = "mask"
N_NA = "na"
N_NF = "nf"
N_O = "o"
N_OFS = "ofs"
N_OG = "og"
N_PA = "pa"
N_PB = "pb"
N_PB0 = "pb0"
N_PB1 = "pb1"
N_PC = "pc"
N_PS = "ps"
N_Q = "q"
N_RA = "ra"
N_RES = "res"
N_RF = "rf"
N_SENT1 = "sent1"
N_SENT2 = "sent2"
N_SENT3 = "sent3"
N_V = "v"
N_VA = "va"
N_WI = "wi"
N_WK = "wk"
N_WO = "wo"
N_WORK = "work"
N_WQ = "wq"
N_WU = "wu"
N_WV = "wv"
N_X = "x"
N_X_T = "x_t"
N__T = "_t"
BF = jnp.bfloat16
F32 = jnp.float32
ANY = pl.BlockSpec(memory_space=pl.ANY)
SMEM = pl.BlockSpec(memory_space=pltpu.SMEM)
VMEM = pl.BlockSpec(memory_space=pltpu.VMEM)


def dot(left, right):
    return lax.dot_general(left, right, (((1,), (0,)), ((), ())), preferred_element_type=F32)


def dot_nt(left, right):
    return lax.dot_general(left, right, (((1,), (1,)), ((), ())), preferred_element_type=F32)


def dot_tn(left, right):
    return lax.dot_general(left, right, (((0,), (0,)), ((), ())), preferred_element_type=F32)


def gelu_pair(u):
    d = 1.0 + 0.23164188580 * jnp.abs(u)
    t = pl.reciprocal(d, approx=True)
    poly = t * (0.127414796 + t * (-0.142248368 + t * (0.7107068705 + t * (-0.7265760135 + t * 0.5307027145))))
    bell = jnp.exp2(u * u * -0.7213475204444817)
    tail = poly * bell
    cdf = jnp.where(u >= 0, 1.0 - tail, tail)
    return u * cdf, cdf + u * (bell * 0.3989422804014327)


def ds(index, size):
    if isinstance(index, int):
        return slice(index * size, (index + 1) * size)
    return pl.ds(pl.multiple_of(index * size, size), size)


def stage_query(r):
    rows, width = r.x.shape
    for j in range(width // TILE):
        cols = slice(j * TILE, (j + 1) * TILE)
        r.q[:, cols] = ((dot(r.x[...], r.wq[:, cols]) + r.bq[:, cols].astype(F32)).astype(BF) * HEAD ** -0.5).astype(BF)


def stage_key(r):
    for j in range(r.x.shape[1] // TILE):
        cols = slice(j * TILE, (j + 1) * TILE)
        r.k[:, cols] = dot(r.x[...], r.wk[:, cols]).astype(BF)


def stage_value(r):
    rows, width = r.x.shape
    one = jnp.ones((rows, LANES), BF)
    for j in range(width // TILE):
        cols = slice(j * TILE, (j + 1) * TILE)
        vv = (dot(r.x[...], r.wv[:, cols]) + r.bv[:, cols].astype(F32)).astype(BF)
        r.v[:, cols] = vv
        for h in range(TILE // LANES):
            at = (j * (TILE // LANES) + h) * TILE
            r.va[:, at:at + LANES] = vv[:, h * LANES:(h + 1) * LANES]
            r.va[:, at + LANES:at + TILE] = one


def stage_mask(r, seg_row):
    rows = r.x.shape[0]
    ids = jnp.broadcast_to(seg_row.astype(F32), (8, rows))
    r.mask[...] = jnp.where(jnp.transpose(ids)[:, 0:1] == ids[0:1, :], 0.0, -1e30)


def stage_attention(r):
    rows, width = r.x.shape
    low = lax.broadcasted_iota(jnp.int32, (1, LANES), 1) < HEAD
    qb = 128

    def pair(p, _):
        kp = r.k[:, ds(p, LANES)]
        vp = r.va[:, ds(p, TILE)]
        kz = [jnp.where(low, kp, jnp.zeros_like(kp)), jnp.where(low, jnp.zeros_like(kp), kp)]
        for b in range(rows // qb):
            rr = slice(b * qb, (b + 1) * qb)
            qp = r.q[rr, ds(p, LANES)]
            parts = []
            for h in range(2):
                s = dot_nt(qp, kz[h]) + r.mask[rr, :]
                top = jnp.max(s, axis=-1, keepdims=True)
                ee = jnp.exp(s - top).astype(BF)
                r.e[2 * p + h, rr, :] = ee
                o = dot(ee, vp)
                inv = 1.0 / o[:, LANES:]
                parts.append((o[:, :LANES] * inv, inv))
            c = jnp.where(low, parts[0][0], parts[1][0])
            r.inv[rr, ds(p, LANES)] = jnp.where(low, parts[0][1], parts[1][1])
            r.cf[rr, ds(p, LANES)] = c
            r.ctx[rr, ds(p, LANES)] = c.astype(BF)
        return 0

    lax.fori_loop(0, width // LANES, pair, 0, unroll=3)


def normal(r, rr, n_ref, s_ref):
    t = r.work[rr, :]
    t = t - jnp.mean(t, axis=-1, keepdims=True)
    scale = lax.rsqrt(jnp.mean(t * t, axis=-1, keepdims=True) + 1e-12)
    n = t * scale
    n_ref[rr, :] = n.astype(BF)
    s_ref[rr, :] = jnp.broadcast_to(scale, (n.shape[0], LANES))
    return n


def stage_branch(r):
    rows, width = r.x.shape
    for j in range(width // TILE):
        cols = slice(j * TILE, (j + 1) * TILE)
        r.work[:, cols] = dot(r.ctx[...], r.wo[:, cols]) + r.bo[:, cols].astype(F32) + r.x[:, cols].astype(F32)

    def norm(b, _):
        rr = ds(b, 64)
        h = normal(r, rr, r.na, r.ra) * r.ga[...].astype(F32) + r.sa[...].astype(F32)
        r.hidden[rr, :] = h
        r.hid[rr, :] = h.astype(BF)
        return 0

    lax.fori_loop(0, rows // 64, norm, 0, unroll=8)


def stage_inner(r):
    wide = r.act.shape[1]

    def feed(j, _):
        cols = ds(j, TILE)
        for b in range(r.hid.shape[0] // LANES):
            rr = slice(b * LANES, (b + 1) * LANES)
            a, g = gelu_pair(dot(r.hid[rr, :], r.wi[:, cols]) + r.bi[:, cols].astype(F32))
            r.act[rr, cols] = a.astype(BF)
            r.der[rr, cols] = g.astype(BF)
        return 0

    lax.fori_loop(0, wide // TILE, feed, 0, unroll=4)


def stage_outer(r):
    rows, width = r.x.shape
    for j in range(width // TILE):
        cols = slice(j * TILE, (j + 1) * TILE)
        r.work[:, cols] = dot(r.act[...], r.wu[:, cols]) + r.bu[:, cols].astype(F32) + r.hidden[:, cols]

    def last(b, _):
        rr = ds(b, 64)
        r.res[rr, :] = (normal(r, rr, r.nf, r.rf) * r.gf[...].astype(F32) + r.sf[...].astype(F32)).astype(BF)
        return 0

    lax.fori_loop(0, rows // 64, last, 0, unroll=8)


def norm_back(grad, n_ref, scale, gain, out, low_out, small):
    rows, width = out.shape

    def norm(b, sums):
        rr = ds(b, 64)
        t = grad[rr, :].astype(F32)
        n = n_ref[rr, :].astype(F32)
        s = t * gain[...].astype(F32)
        m1 = jnp.mean(s, axis=-1, keepdims=True)
        m2 = jnp.mean(s * n, axis=-1, keepdims=True)
        f = (s - m1 - n * m2) * scale[rr, 0:1]
        out[rr, :] = f
        low = f.astype(BF)
        low_out[rr, :] = low
        parts = (t * n, t, low.astype(F32))
        return tuple(a + jnp.sum(b.reshape(8, 8, width), axis=0) for a, b in zip(sums, parts))

    zero = jnp.zeros((8, width), F32)
    sums = lax.fori_loop(0, rows // 64, norm, (zero, zero, zero), unroll=8)
    small[...] = jnp.zeros_like(small)
    for i in range(3):
        small[i:i + 1, :width] = jnp.sum(sums[i], axis=0, keepdims=True)


def stage_inner_back(r):
    wide = r.der.shape[1]

    def inner(j, _):
        cols = ds(j, TILE)
        low = (dot_nt(r.og[...], r.wu[cols, :]) * r.der[:, cols].astype(F32)).astype(BF)
        r.ig[:, cols] = low
        return 0

    lax.fori_loop(0, wide // TILE, inner, 0, unroll=6)


def stage_hidden_back(r):
    for j in range(r.hg.shape[0] // TILE):
        rr = slice(j * TILE, (j + 1) * TILE)
        r.hg[rr, :] = r.hg[rr, :] + dot_nt(r.ig[rr, :], r.wi[...])


def stage_context_back(r):
    for j in range(r.bg.shape[1] // TILE):
        cols = slice(j * TILE, (j + 1) * TILE)
        r.cg[:, cols] = dot_nt(r.bg[...], r.wo[cols, :]).astype(BF)


def attention_back_pair(r, p):
    low = lax.broadcasted_iota(jnp.int32, (1, LANES), 1) < HEAD
    cols = ds(p, LANES)
    kp, vp, qp = r.k[:, cols], r.v[:, cols], r.q[:, cols]
    co = (r.cg[:, cols].astype(F32) * r.inv[:, cols]).astype(BF)
    prod = co.astype(F32) * r.cf[:, cols]
    qt, ct = jnp.transpose(qp), jnp.transpose(co)
    zb = jnp.zeros_like(kp)
    dqs, dks, dvs = [], [], []
    for h in range(2):
        mine = low if h == 0 else jnp.logical_not(low)
        part = slice(h * HEAD, (h + 1) * HEAD)
        weighted = jnp.sum(jnp.where(mine, prod, 0.0), axis=-1, keepdims=True)
        ee = r.e[2 * p + h]
        dp = dot_nt(jnp.where(mine, co, zb), vp) - weighted
        sg = (ee.astype(F32) * dp).astype(BF)
        dvs.append(dot(ct[part], ee))
        dqs.append(dot(sg, jnp.where(mine, kp, zb)))
        dks.append(dot(qt[part], sg))
    r.dq[:, cols] = ((dqs[0] + dqs[1]) * HEAD ** -0.5).astype(BF)
    r.dk[:, cols] = jnp.transpose(jnp.concatenate(dks, axis=0)).astype(BF)
    r.dv[:, cols] = jnp.transpose(jnp.concatenate(dvs, axis=0)).astype(BF)


def stage_attention_back(r):
    def pair(p, _):
        attention_back_pair(r, p)
        return 0

    lax.fori_loop(0, r.cg.shape[1] // LANES, pair, 0, unroll=3)


def stage_layer_grad(r):
    for j in range(r.hg.shape[1] // TILE):
        cols = slice(j * TILE, (j + 1) * TILE)
        t = r.hg[:, cols] + dot_nt(r.dq[...], r.wq[cols, :]) + dot_nt(r.dk[...], r.wk[cols, :]) + dot_nt(r.dv[...], r.wv[cols, :])
        r.lg[:, cols] = t.astype(BF)


class Refs:
    pass


class Moves:
    def __init__(self, sems):
        self.sems, self.open, self.used = sems, {}, 0

    def start(self, *pairs):
        for name, src, dst in pairs:
            self.open[name] = (src, dst, self.used)
            self.used += 1
            self.copy(name).start()

    def copy(self, name):
        src, dst, at = self.open[name]
        return pltpu.make_async_copy(src, dst, self.sems.at[at])

    def wait(self, *names):
        for name in names or list(self.open):
            self.copy(name).wait()
            del self.open[name]


KEPT = (N_X, N_CTX, N_HID, N_ACT)
STATE = (N_Q, N_K, N_V, N_E, N_INV, N_CF, N_NA, N_RA, N_DER, N_NF, N_RF)
FEED = (N_OG, N_IG, N_FS)
ATT = (N_BG, N_DQ, N_DK, N_DV, N_AT)
WEIGHTS = (N_WQ, N_WK, N_WV, N_WO, N_WI, N_WU)
VECTORS = ("bq", "bv", "bo", N_GA, "sa", "bi", "bu", N_GF, "sf")


def shapes_of(rows, width, wide):
    row, row32, broad = ((rows, width), BF), ((rows, width), F32), ((rows, wide), BF)
    square = ((width, width), BF)
    table = {n: row for n in (N_X, N_Q, N_K, N_V, N_CTX, N_NA, N_HID, N_NF, N_RES, N_G, N_OG, N_BG, N_CG, N_DQ, N_DK, N_DV, N_LG)}
    table.update({n: row32 for n in (N_INV, N_CF, N_WORK, N_HIDDEN, N_HG)})
    table.update({n: broad for n in (N_ACT, N_DER, N_IG)})
    table.update({n: square for n in (N_WQ, N_WK, N_WV, N_WO)})
    table.update(wi=((width, wide), BF), wu=((wide, width), BF), e=((HEADS, rows, rows), BF), mask=((rows, rows), F32),
                 va=((rows, 2 * width), BF), ra=((rows, LANES), F32), rf=((rows, LANES), F32), fs=((8, wide), F32), at=((8, width), F32),
                 acts=((MICRO, rows, width), BF), grads=((MICRO, rows, width), BF))
    table.update({n + N__T: (table[n][0][::-1], BF) for n in (N_ACT, N_HID, N_CTX, N_X)})
    part, rest = (8, width // 4, width), (8, width // 4 + 16, width)
    table.update(pa=((2,) + part, BF), pc=((2,) + part, BF), pb=((2,) + rest, BF), sent2=(rest, BF), keep2=(rest, BF))
    table.update({n: (part, BF) for n in (N_SENT1, N_KEEP1, N_SENT3, N_KEEP3)})
    table.update(
                 ps=((8, wide), F32), left=((2, width, rows), BF), right=((4, rows, width), BF))
    return table


def layer_call(kernel, name, sizes, small_in, big_in, outs, alias, buffers, flops, moves=40):
    table = shapes_of(*sizes)
    n_small, n_big = len(small_in), len(big_in)
    names = [n for n in outs if n in alias]

    def run(*refs):
        small, big = refs[:n_small], refs[n_small:n_small + n_big]
        at = n_small + n_big + len(names)
        out = dict(zip(outs, refs[at:at + len(outs)]))
        r = Refs()
        for n, ref in zip(buffers, refs[at + len(outs):-1]):
            setattr(r, n, ref)
        kernel(r, small, big, out, Moves(refs[-1]))

    res = pl.pallas_call(
        run,
        out_shape=[jax.ShapeDtypeStruct(*table[n]) for n in outs],
        in_specs=[SMEM] + [VMEM] * (n_small - 1) + [ANY] * (n_big + len(names)),
        out_specs=[ANY] * len(outs),
        scratch_shapes=[pltpu.VMEM(*table[n]) for n in buffers] + [pltpu.SemaphoreType.DMA((moves,))],
        input_output_aliases={n_small + n_big + i: outs.index(n) for i, n in enumerate(names)},
        compiler_params=pltpu.CompilerParams(vmem_limit_bytes=VMEM_LIMIT),
        cost_estimate=pl.CostEstimate(flops=flops, bytes_accessed=30_000_000, transcendentals=0),
        name=name,
    )(*small_in, *big_in, *[alias[n] for n in names])
    return dict(zip(outs, res))


def run_forward(go, seg, x, micro, w, acts, sizes):
    outs = (N_RES, N_ACTS) + KEPT + STATE

    def kernel(r, small, big, out, mv):
        seg_row = small[1]
        for n, ref in zip(VECTORS, small[2:]):
            setattr(r, n, ref)
        src = dict(zip(WEIGHTS, big[1:]))

        @pl.when(small[0][0] == 1)
        def _():
            forward_stages(r, seg_row[micro], big[0].at[micro], src, mv,
                           lambda *names: mv.start(*[(N_O + n, getattr(r, n), out[n]) for n in names]))
            mv.start((N_ACTS, r.res, out[N_ACTS].at[micro]))
            mv.wait()

    buffers = KEPT + STATE + WEIGHTS + (N_RES, N_VA, N_MASK, N_WORK, N_HIDDEN)
    rows, width, wide = sizes
    return layer_call(kernel, "forward", sizes, [go, seg] + [w[n] for n in VECTORS], [x] + [w[n] for n in WEIGHTS], outs, {N_ACTS: acts} if micro else {},
                      buffers, 2 * rows * 12 * width * width)


def forward_stages(r, seg_row, x_src, src, mv, put):
    def load(*names):
        mv.start(*[(n, src[n], getattr(r, n)) for n in names])

    mv.start((N_X, x_src, r.x))
    load(N_WQ, N_WK, N_WV)
    stage_mask(r, seg_row)
    mv.wait(N_X, N_WQ)
    stage_query(r)
    mv.wait(N_WK)
    load(N_WO, N_WI)
    stage_key(r)
    mv.wait(N_WV)
    stage_value(r)
    put(N_X, N_Q, N_K, N_V)
    load(N_WU)
    stage_attention(r)
    put(N_E, N_INV, N_CF, N_CTX)
    mv.wait(N_WO)
    stage_branch(r)
    put(N_NA, N_RA, N_HID)
    mv.wait(N_WI)
    stage_inner(r)
    put(N_ACT, N_DER)
    mv.wait(N_WU)
    stage_outer(r)
    put(N_RES, N_NF, N_RF)


def run_layer(go, seg, x, g, micro, w, kept, sizes):
    outs = (N_ACTS, N_LG, N_GRADS) + KEPT + FEED + ATT

    def kernel(r, small, big, out, mv):
        seg_row = small[1]
        for n, ref in zip(VECTORS, small[2:]):
            setattr(r, n, ref)
        src = dict(zip(WEIGHTS, big[2:]))
        r.hg, r.ig = r.work, r.der

        def put(*names):
            mv.start(*[(N_O + n, getattr(r, n), out[n]) for n in names if n in outs])

        @pl.when(small[0][0] == 1)
        def _():
            forward_stages(r, seg_row[micro], big[0], src, mv, put)
            mv.start((N_G, big[1].at[micro], r.g), (N_ACTS, r.res, out[N_ACTS].at[micro]))
            mv.wait(N_G)
            norm_back(r.g, r.nf, r.rf, r.gf, r.hg, r.og, r.fs)
            put(N_OG)
            stage_inner_back(r)
            put(N_IG, N_FS)
            stage_hidden_back(r)
            norm_back(r.hg, r.na, r.ra, r.ga, r.hg, r.bg, r.at)
            put(N_BG)
            stage_context_back(r)
            stage_attention_back(r)
            put(N_DQ, N_DK, N_DV)
            stage_layer_grad(r)
            put(N_LG, N_AT)
            mv.start((N_GRADS, r.lg, out[N_GRADS].at[micro]))
            mv.wait()

    buffers = KEPT + STATE + WEIGHTS + (N_RES, N_VA, N_MASK, N_WORK, N_HIDDEN, N_G, N_OG, N_FS, N_BG, N_CG, N_DQ, N_DK, N_DV,
                                        N_AT, N_LG)
    rows, width, wide = sizes
    return layer_call(kernel, "layer", sizes, [go, seg] + [w[n] for n in VECTORS], [x, g] + [w[n] for n in WEIGHTS], outs, kept,
                      buffers, 2 * rows * 26 * width * width)


def run_back(go, g, state, micro, old, w, sizes):
    outs = (N_GRADS,) + FEED + ATT
    names = (N_G, N_NF, N_RF, N_WU, N_DER, N_WI, N_NA, N_RA, N_WO, N_Q, N_K, N_V, N_INV, N_CF, N_E, N_WQ, N_WK, N_WV)

    def kernel(r, small, big, out, mv):
        r.gf, r.ga = small[1:3]
        r.ig = r.der
        src = dict(zip(names, big))

        def load(*names):
            mv.start(*[(n, src[n], getattr(r, n)) for n in names])

        def put(*names):
            mv.start(*[(N_O + n, getattr(r, n), out[n]) for n in names])

        @pl.when(small[0][0] == 1)
        def _():
            load(N_G, N_NF, N_RF)
            load(N_WU, N_DER)
            mv.wait(N_G, N_NF, N_RF)
            norm_back(r.g, r.nf, r.rf, r.gf, r.hg, r.og, r.fs)
            put(N_OG)
            mv.wait(N_WU, N_DER)
            load(N_WI, N_NA, N_RA, N_WO)
            stage_inner_back(r)
            put(N_IG, N_FS)
            mv.wait(N_WI)
            load(N_Q, N_K, N_V, N_INV, N_CF, N_E)
            stage_hidden_back(r)
            mv.wait(N_NA, N_RA, N_WO)
            norm_back(r.hg, r.na, r.ra, r.ga, r.hg, r.bg, r.at)
            put(N_BG, N_AT)
            load(N_WQ, N_WK, N_WV)
            stage_context_back(r)
            mv.wait(N_Q, N_K, N_V, N_INV, N_CF, N_E)
            stage_attention_back(r)
            put(N_DQ, N_DK, N_DV)
            mv.wait(N_WQ, N_WK, N_WV)
            stage_layer_grad(r)
            mv.start((N_GRADS, r.lg, out[N_GRADS].at[micro]))
            mv.wait()

    rows, width, wide = sizes
    big = [g, state[N_NF], state[N_RF], w[N_WU], state[N_DER], w[N_WI], state[N_NA], state[N_RA], w[N_WO]]
    big += [state[n] for n in (N_Q, N_K, N_V, N_INV, N_CF, N_E)] + [w[N_WQ], w[N_WK], w[N_WV]]
    return layer_call(kernel, "backward", sizes, [go, w[N_GF], w[N_GA]], big, outs, old,
                      names + (N_OG, N_HG, N_FS, N_BG, N_CG, N_DQ, N_DK, N_DV, N_AT, N_LG), 2 * rows * 14 * width * width)


def run_flip(go, kept, old, sizes):
    outs = (N_ACT_T, N_HID_T, N_CTX_T, N_X_T)
    names = (N_ACT, N_HID, N_CTX, N_X)

    def kernel(r, small, big, out, mv):
        @pl.when(small[0][0] == 1)
        def _():
            mv.start(*[(n, src, getattr(r, n)) for n, src in zip(names, big)])
            for n in reversed(names):
                mv.wait(n)
                src, dst = getattr(r, n), getattr(r, n + N__T)

                def turn(j, _, src=src, dst=dst):
                    dst[ds(j, TILE), :] = jnp.transpose(src[:, ds(j, TILE)])
                    return 0

                lax.fori_loop(0, src.shape[1] // TILE, turn, 0)
                mv.start((n + N__T, dst, out[n + N__T]))
            mv.wait()

    return layer_call(kernel, "transposes", sizes, [go], [kept[n] for n in names], outs, old, names + outs, 4_000_000_000)


def run_partial(go, kept, a, kept1, flip, sizes):
    turned = (N_ACT_T, N_HID_T, N_CTX_T, N_X_T)
    outs = (N_PA, N_PC, N_PB, N_PS) + turned
    names = (N_ACT, N_OG, N_HID, N_IG, N_CTX, N_BG, N_X, N_DQ, N_DK, N_DV)
    rows, width, wide = sizes
    chunk = width // 4
    per = width // chunk

    def kernel(r, small, big, out, mv):
        mv.start(*[(n, src, getattr(r, n)) for n, src in zip(names, big)])
        ones = jnp.ones((8, rows), BF)
        mv.wait(N_ACT, N_OG)
        for i in range(2):
            def first(j, _, i=i):
                cols = pl.ds(pl.multiple_of(i * (wide // 2) + 2 * j * chunk, LANES), 2 * chunk)
                t = dot_tn(r.act[:, cols], r.og[...]).astype(BF)
                r.pa[i, 2 * j] = t[:chunk]
                r.pa[i, 2 * j + 1] = t[chunk:]
                return 0

            lax.fori_loop(0, 4, first, 0, unroll=2)
        mv.start((N_PA, r.pa, out[N_PA]))
        mv.wait(N_HID, N_IG)
        r.hid_t[...] = jnp.transpose(r.hid[...])
        for b in range(4):
            g = r.ig[:, b * width:(b + 1) * width]
            t = dot(r.hid_t[...], g).astype(BF)
            for c in range(per):
                r.pc[b // 2, b % 2 * per + c] = t[c * chunk:(c + 1) * chunk]
            r.ps[:, b * width:(b + 1) * width] = dot(ones, g)
        mv.start((N_PC, r.pc, out[N_PC]), (N_PS, r.ps, out[N_PS]))
        mv.wait(N_CTX, N_BG, N_X, N_DQ, N_DK, N_DV)
        r.x_t[...] = jnp.transpose(r.x[...])
        r.ctx_t[...] = jnp.transpose(r.ctx[...])
        r.pb[:, :, chunk:, :] = jnp.zeros((2, 8, 16, width), BF)
        for n, (left, right) in enumerate(((r.ctx_t, r.bg), (r.x_t, r.dq), (r.x_t, r.dk), (r.x_t, r.dv))):
            t = dot(left[...], right[...]).astype(BF)
            for c in range(per):
                r.pb[n // 2, n % 2 * per + c, :chunk, :] = t[c * chunk:(c + 1) * chunk]
        mv.start((N_PB, r.pb, out[N_PB]))

        @pl.when(small[0][0] == 0)
        def _():
            for i, n in enumerate((N_ACT, N_HID, N_CTX, N_X)):
                mv.start((n, big[10 + i], getattr(r, n)))
            for i, n in enumerate((N_ACT, N_HID, N_CTX, N_X)):
                mv.wait(n)
                src, dst = getattr(r, n), getattr(r, turned[i])

                def turn(j, _, src=src, dst=dst):
                    dst[ds(j, TILE), :] = jnp.transpose(src[:, ds(j, TILE)])
                    return 0

                lax.fori_loop(0, src.shape[1] // TILE, turn, 0)
                mv.start((turned[i], dst, out[turned[i]]))
            mv.wait(*turned)

        mv.wait(N_PA, N_PC, N_PB, N_PS)

    src = dict(kept, **a)
    big = [src[n] for n in names] + [kept1[n] for n in (N_ACT, N_HID, N_CTX, N_X)]
    res = layer_call(kernel, "weight_gradient_0", sizes, [go], big, outs, flip, names + outs, 2 * rows * 12 * width * width)
    return res, res


def run_feed(go, g, state, t1, t, p, w, sizes):
    outs = (N_FS, N_HG, N_SENT1, N_KEEP1, N_SENT3, N_KEEP3, N_PS)
    rows, width, wide = sizes
    chunk = width // 4
    per = width // chunk
    half = wide // 2

    def kernel(r, small, big, out, mv):
        r.gf = small[1]
        r.ig = r.der
        side = [1 - small[0][1], small[0][1]]
        begin = [pl.multiple_of(n * half, half) for n in side]
        mine, others = small[0][0] == 1, small[0][0] == 0

        @pl.when(mine)
        def _():
            mv.start(*[(n, src, getattr(r, n)) for n, src in zip((N_G, N_NF, N_RF), big)])

        @pl.when(others)
        def _():
            mv.start((N_OG, big[8], r.og), (N_IG, big[9], r.der))

        mv.start(("act0", big[5].at[pl.ds(begin[0], half), :], r.act_t.at[:half, :]), ("pa0", big[10].at[side[0]], r.pa.at[0]))

        @pl.when(mine)
        def _():
            mv.start((N_WU, big[3], r.wu), (N_DER, big[4], r.der))

        mv.start(("act1", big[5].at[pl.ds(begin[1], half), :], r.act_t.at[half:, :]), ("pa1", big[10].at[side[1]], r.pa.at[1]))
        mv.start((N_HID_T, big[6], r.hid_t), ("pc0", big[11].at[side[0]], r.pc.at[0]), ("pc1", big[11].at[side[1]], r.pc.at[1]))

        @pl.when(mine)
        def _():
            mv.start((N_WI, big[7], r.wi))
            mv.wait(N_G, N_NF, N_RF)
            norm_back(r.g, r.nf, r.rf, r.gf, r.hg, r.og, r.fs)
            mv.start((N_OFS, r.fs, out[N_FS]))

        @pl.when(others)
        def _():
            mv.wait(N_OG, N_IG)

        for i, n in enumerate((N_SENT1, N_KEEP1)):
            mv.wait("act%d" % i, "pa%d" % i)

            def outer(j, _, i=i):
                rr = pl.ds(pl.multiple_of(i * half + 2 * j * chunk, 2 * chunk), 2 * chunk)
                t = dot(r.act_t[rr, :], r.og[...])
                r.pa[i, 2 * j] = (r.pa[i, 2 * j].astype(F32) + t[:chunk]).astype(BF)
                r.pa[i, 2 * j + 1] = (r.pa[i, 2 * j + 1].astype(F32) + t[chunk:]).astype(BF)
                return 0

            lax.fori_loop(0, 4, outer, 0, unroll=2)
            mv.start((n, r.pa.at[i], out[n]))

        @pl.when(mine)
        def _():
            mv.wait(N_WU, N_DER)
            stage_inner_back(r)

        mv.wait(N_HID_T)
        ones = jnp.ones((8, rows), BF)
        for i, n in enumerate((N_SENT3, N_KEEP3)):
            mv.wait("pc%d" % i)
            for b in range(2):
                at = pl.multiple_of(begin[i] + b * width, width)
                part = r.der[:, pl.ds(at, width)]
                t = dot(r.hid_t[...], part)
                for c in range(per):
                    r.pc[i, b * per + c] = (r.pc[i, b * per + c].astype(F32) + t[c * chunk:(c + 1) * chunk]).astype(BF)
                r.ps[:, pl.ds(at, width)] = dot(ones, part)
            mv.start((n, r.pc.at[i], out[n]))
        mv.start((N_PS, r.ps, out[N_PS]))

        @pl.when(mine)
        def _():
            mv.wait(N_WI)
            stage_hidden_back(r)
            mv.start((N_HG, r.hg, out[N_HG]))
            mv.wait(N_HG, N_OFS)

        mv.wait(N_SENT1, N_KEEP1, N_SENT3, N_KEEP3, N_PS)

    big = [g, state[N_NF], state[N_RF], w[N_WU], state[N_DER], t[N_ACT_T], t[N_HID_T], w[N_WI], t1[N_OG], t1[N_IG], p[N_PA], p[N_PC]]
    return layer_call(kernel, "feed_gradient", sizes, [go, w[N_GF]], big, outs, {N_FS: t1[N_FS]},
                      (N_G, N_NF, N_RF, N_WU, N_WI, N_DER, N_ACT_T, N_HID_T, N_PA, N_PC, N_HG, N_OG, N_FS, N_PS), 8 * rows * width * wide)


def run_rest(go, hg, state, micro, grads, t1, t, p, sums, w, sizes):
    outs = (N_GRADS, N_SENT2, N_KEEP2)
    rows, width, wide = sizes
    names = (N_HG, N_NA, N_RA, N_WO, N_INV, N_CF, N_Q, N_K, N_V, N_E, N_WQ, N_WK, N_WV)
    right = (N_BG, N_DQ, N_DK, N_DV)

    def kernel(r, small, big, out, mv):
        r.ga, fs0, fs1, at0, at1, ps0, ps1, dq0, dv0 = small[1:]
        for i, n in enumerate(right):
            setattr(r, n, r.right.at[i])
        side = [1 - small[0][1], small[0][1]]
        mine, others = small[0][0] == 1, small[0][0] == 0
        src = dict(zip(names, big))
        pairs = width // LANES

        def load(*names):
            mv.start(*[(n, src[n], getattr(r, n)) for n in names])

        @pl.when(mine)
        def _():
            load(N_HG, N_NA, N_RA)
            load(N_WO, N_INV, N_CF, N_Q, N_K, N_V)
            for p in range(0, pairs, 2):
                mv.start(("e%d" % p, big[9].at[2 * p:2 * p + 4], r.e.at[2 * p:2 * p + 4]))
            load(N_WQ, N_WK, N_WV)

        @pl.when(others)
        def _():
            mv.start(*[(n, ref, getattr(r, n)) for n, ref in zip(right, big[15:])])

        mv.start((N_CTX_T, big[13], r.left.at[0]), (N_X_T, big[14], r.left.at[1]))
        mv.start((N_PB0, big[19].at[side[0]], r.pb.at[0]), (N_PB1, big[19].at[side[1]], r.pb.at[1]))
        chunk = r.pb.shape[2] - 16
        per = width // chunk

        @pl.when(mine)
        def _():
            mv.wait(N_HG, N_NA, N_RA)
            norm_back(r.hg, r.na, r.ra, r.ga, r.hg, r.bg, r.at)
            mv.wait(N_WO)
            stage_context_back(r)
            mv.wait(N_INV, N_CF, N_Q, N_K, N_V)
            for p in range(pairs):
                if p % 2 == 0:
                    mv.copy("e%d" % p).wait()
                    del mv.open["e%d" % p]
                attention_back_pair(r, p)

        @pl.when(others)
        def _():
            mv.wait(*right)
            r.at[...] = at1[...]

        mv.wait(N_CTX_T, N_X_T, N_PB0, N_PB1)
        ones = jnp.ones((8, rows), BF)
        fs = fs0[...] + fs1[...]
        at = at0[...] + r.at[...]
        ps = ps0[...] + ps1[...]
        dqs = dot(ones, dq0[...]) + dot(ones, r.right[1])
        dvs = dot(ones, dv0[...]) + dot(ones, r.right[3])
        lines = [dqs[0:1], dvs[0:1], at[2:3], at[0:1], at[1:2], fs[2:3, :width], fs[0:1, :width], fs[1:2, :width]]
        lines += [ps[0:1, i * width:(i + 1) * width] for i in range(wide // width)]
        lines += [jnp.zeros((16 - len(lines), width), F32)]
        lines = jnp.concatenate(lines, axis=0).astype(BF)
        r.pb[0, 0, chunk:, :] = lines
        r.pb[1, 0, chunk:, :] = lines
        for n in range(4):
            which = side[n // 2] * 2 + n % 2
            lhs = jnp.minimum(which, 1)
            v = dot(r.left[lhs], r.right[which])
            for c in range(per):
                at = n % 2 * per + c
                r.pb[n // 2, at, :chunk, :] = (r.pb[n // 2, at, :chunk, :].astype(F32) + v[c * chunk:(c + 1) * chunk]).astype(BF)
            if n % 2:
                mv.start((outs[1 + n // 2], r.pb.at[n // 2], out[outs[1 + n // 2]]))

        @pl.when(mine)
        def _():
            mv.wait(N_WQ, N_WK, N_WV)
            stage_layer_grad(r)
            mv.start((N_GRADS, r.lg, out[N_GRADS].at[micro]))
            mv.wait(N_GRADS)

        mv.wait(N_SENT2, N_KEEP2)

    big = [hg] + [state[N_NA], state[N_RA], w[N_WO]] + [state[n] for n in (N_INV, N_CF, N_Q, N_K, N_V, N_E)] + [w[N_WQ], w[N_WK], w[N_WV]]
    big += [t[N_CTX_T], t[N_X_T]] + [t1[n] for n in right] + [p[N_PB]]
    return layer_call(kernel, "attention_gradient", sizes, [go, w[N_GA]] + sums, big, outs, {N_GRADS: grads},
                      names + (N_CG, "right", "left", N_PB, N_AT, N_LG), 24 * rows * width * width)


def unpack_kernel(place, *rest, kinds, pieces, n_alias, n_lines):
    count = len(pieces)
    n_take = 2 * count * len(kinds)
    take, rest = rest[:n_take], rest[n_take:]
    lines, rest = rest[:n_lines], rest[n_lines + n_alias:]
    outs, small = rest[:n_alias], rest[n_alias:-5]
    low, high, tiny, sin, sout = rest[-5:]
    chunk, width = high.shape[1:]
    per = width // chunk
    loads = [pltpu.make_async_copy(src.at[:chunk, :], low.at[u], sin.at[u]) for u, src in enumerate(take)]
    loads += [pltpu.make_async_copy(src.at[chunk:, :], tiny.at[u], sin.at[n_take + u]) for u, src in enumerate(lines)]
    for c in loads:
        c.start()
    for u in range(n_take):
        kind, at = kinds[u // (2 * count)], u % (2 * count)
        first = sum((1, 1, 4)[k] for k in kinds[:u // (2 * count)])
        core = place[0] if at < count else 1 - place[0]
        rank = place[1] if at < count else 7 - place[1]
        index = core * 8 + lax.rem(rank + 9 - pieces[at % count], 8)
        loads[u].wait()
        high[u] = low[u].astype(F32)
        row = pl.ds(pl.multiple_of(lax.rem(index, per) * chunk, 8), chunk)
        if kind == 0:
            pltpu.make_async_copy(high.at[u], outs[first].at[pl.ds(pl.multiple_of(index * chunk, 8), chunk), :], sout.at[u]).start()
        elif kind == 1:
            col = pl.ds(pl.multiple_of(index // per * width, width), width)
            pltpu.make_async_copy(high.at[u], outs[first].at[row, col], sout.at[u]).start()
        else:
            for n in range(4):
                @pl.when(index // per == n)
                def _(n=n, u=u, row=row, first=first):
                    pltpu.make_async_copy(high.at[u], outs[first + n].at[row, :], sout.at[u]).start()
    if n_lines:
        for c in loads[n_take:]:
            c.wait()
        t = tiny[lax.rem(place[1] + 1, 8)].astype(F32)
        for i in range(8):
            small[i][...] = t[i:i + 1]
        for i in range(small[8].shape[1] // width):
            small[8][:, i * width:(i + 1) * width] = t[8 + i:9 + i]
    for u in range(n_take):
        pltpu.make_async_copy(high.at[u], outs[0].at[:chunk, :width], sout.at[u]).wait()


def run_unpack(place, rings, kinds, pieces, old, final):
    width = rings[0].pieces[0].shape[1]
    chunk = width // 4
    count, wide = len(pieces), 4 * width
    sd = jax.ShapeDtypeStruct
    shapes = [s for k in kinds for s in ([sd((wide, width), F32)], [sd((width, wide), F32)], [sd((width, width), F32)] * 4)[k]]
    lines = rings[-1].pieces if final else []
    small = [sd((1, width), F32)] * 8 + [sd((1, wide), F32)] if lines else []
    take = [side[u] for ring in rings for side in (ring.pieces, ring.others) for u in pieces]
    n_in = 1 + len(take) + len(lines)
    old = list(old or [])

    def kernel(*refs):
        inputs, rest = refs[:n_in], refs[n_in + len(old):]
        unpack_kernel(*inputs, *[None] * len(shapes), *rest, kinds=kinds, pieces=pieces, n_alias=len(shapes), n_lines=len(lines))

    n = len(take)
    return pl.pallas_call(
        kernel,
        out_shape=shapes + small,
        in_specs=[SMEM] + [ANY] * (n_in - 1 + len(old)),
        out_specs=[ANY] * len(shapes) + [VMEM] * len(small),
        scratch_shapes=[pltpu.VMEM((n, chunk, width), BF), pltpu.VMEM((n, chunk, width), F32), pltpu.VMEM((8, 16, width), BF),
                        pltpu.SemaphoreType.DMA((n + 8,)), pltpu.SemaphoreType.DMA((n,))],
        input_output_aliases={n_in + i: i for i in range(len(old))},
        compiler_params=pltpu.CompilerParams(vmem_limit_bytes=VMEM_LIMIT),
        cost_estimate=pl.CostEstimate(flops=0, bytes_accessed=6 * n * chunk * width, transcendentals=0),
        name="unpack",
    )(place, *take, *lines, *old)


def ring_tables():
    chips = [(z, 0) for z in range(4)] + [(z, 1) for z in reversed(range(4))]
    step = []
    for at, (z, y) in enumerate(chips):
        for core in range(2):
            nz, ny = chips[(at + 1) % 8] if core == 0 else chips[at - 1]
            step.append((z * 4 + y * 2 + core, nz * 4 + ny * 2 + core))
    swap = [(d, d ^ 1) for d in range(16)]
    return step, swap


def ring_place():
    d = lax.axis_index("dp")
    z, y, core = d // 4, (d // 2) % 2, d % 2
    at = jnp.where(y == 0, z, 7 - z)
    return core, jnp.where(core == 0, at, 7 - at)


def after(value, *earlier):
    return lax.optimization_barrier((value, *earlier))[0]


class Ring:
    def __init__(self, parts, rank, step, swap):
        self.parts, self.rank, self.step, self.swap = parts, rank, step, swap
        self.count, self.pieces, self.others = 0, [], []
        self.current = self.own(rank)

    def own(self, index):
        index = lax.rem(index, 8)
        return sum(lax.dynamic_index_in_dim(part, index, 0, keepdims=False) for part in self.parts)

    def advance(self):
        got = lax.ppermute(self.current, "dp", self.step)
        if self.count < 7:
            got = got + self.own(self.rank + 7 - self.count)
        self.current = got
        self.count += 1
        if self.count >= 7:
            self.pieces.append(self.current)
            self.others.append(lax.ppermute(self.current, "dp", self.swap))

    def hold(self, *earlier):
        self.current = after(self.current, *earlier)


def body(inputs, segments, cotangent, query_weight, query_bias, key_weight, value_weight, value_bias, output_weight, output_bias,
         attention_gain, attention_shift, inner_weight, inner_bias, outer_weight, outer_bias, feed_gain, feed_shift):
    micros, local, rows, width = inputs.shape
    wide = inner_weight.shape[2]
    sizes = (rows, width, wide)
    w = dict(wq=query_weight[0], wk=key_weight[0], wv=value_weight[0], wo=output_weight[0], wi=inner_weight[0], wu=outer_weight[0],
             bq=query_bias, bv=value_bias, bo=output_bias, ga=attention_gain, sa=attention_shift, bi=inner_bias, bu=outer_bias,
             gf=feed_gain, sf=feed_shift)
    x_all = inputs.reshape(micros, rows, width)
    g_all = cotangent.reshape(micros, rows, width)
    section = lax.axis_index("section")
    core, rank = ring_place()
    on0 = jnp.stack([1 - section, core]).astype(jnp.int32)
    on1 = jnp.stack([section, core]).astype(jnp.int32)
    place = jnp.stack([core, rank]).astype(jnp.int32)
    up = partial(lax.ppermute, axis_name="section", perm=[(0, 1)])
    down = partial(lax.ppermute, axis_name="section", perm=[(1, 0)])

    def some(source, names):
        return {n: source[n] for n in names}

    s0 = run_forward(on0, segments, x_all, 0, w, None, sizes)
    x10 = up(s0[N_RES])
    s1 = run_forward(on0, segments, x_all, 1, w, s0[N_ACTS], sizes)
    x11 = up(s1[N_RES])
    flip = run_flip(after(on0, s1[N_RES]), s1, {}, sizes)
    t0 = run_layer(after(on1, flip[N_ACT_T]), segments, x10, g_all, 0, w, dict(some(s0, KEPT), acts=s1[N_ACTS]), sizes)
    g00 = down(t0[N_LG])
    t1 = run_layer(after(on1, t0[N_LG]), segments, x11, g_all, 1, w, dict(some(s1, KEPT), acts=t0[N_ACTS], grads=t0[N_GRADS]), sizes)
    g01 = down(t1[N_LG])
    a0 = run_back(after(on0, t1[N_LG]), g00, s0, 0, dict(some(t0, FEED + ATT), grads=t1[N_GRADS]), w, sizes)
    part, flip = run_partial(after(on0, a0[N_GRADS]), t0, a0, t1, flip, sizes)
    step, swap = ring_tables()
    ring = lax.axis_size("dp") == 16
    f1 = run_feed(after(on0, part[N_PB]), g01, s1, t1, flip, part, w, sizes)
    sums = [a0[N_FS], f1[N_FS], a0[N_AT], t1[N_AT], part[N_PS], f1[N_PS], a0[N_DQ], a0[N_DV]]
    r1 = run_rest(on0, f1[N_HG], s1, 1, a0[N_GRADS], t1, flip, part, sums, w, sizes)
    if ring:
        pairs = [(f1[N_SENT1], f1[N_KEEP1]), (f1[N_SENT3], f1[N_KEEP3]), (r1[N_SENT2], r1[N_KEEP2])]
        rings = []
        for sent, keep in pairs:
            first = after(rank, *[each.current for each in rings])
            rings.append(Ring((keep, lax.ppermute(sent, "dp", swap)), first, step, swap))
        for count in range(1, 15):
            for each in rings:
                each.advance()
            if count == 11:
                weights = run_unpack(after(place, *[each.current for each in rings]), rings, (0, 1, 2), range(4), None, False)
            if count == 12:
                for each in rings:
                    each.hold(weights[0])
        unpacked = run_unpack(place, rings, (0, 1, 2), range(4, 8), weights, True)
        outer_g, inner_g, fours = unpacked[0], unpacked[1], unpacked[2:]
    else:
        total = []
        for sent, keep in ((f1[N_SENT1], f1[N_KEEP1]), (f1[N_SENT3], f1[N_KEEP3]), (r1[N_SENT2], r1[N_KEEP2])):
            whole = jnp.where(core == 0, jnp.stack([keep, sent]), jnp.stack([sent, keep]))
            total.append(lax.psum(whole, "dp").astype(F32))
        tail = width // 4
        outer_g = total[0].reshape(wide, width)
        inner_g = total[1].reshape(wide // width, width, width).transpose(1, 0, 2).reshape(width, wide)
        lines = total[2][0, 0, tail:]
        fours = list(total[2][:, :, :tail].reshape(4, width, width)) + [lines[i:i + 1] for i in range(8)]
        fours.append(lines[8:8 + wide // width].reshape(1, wide))
    (wo_g, wq_g, wk_g, wv_g, bq_g, bv_g, bo_g, ga_g, sa_g, bu_g, gf_g, sf_g, bi_g) = fours
    shape = (1, micros, local, rows, width)
    return (t1[N_ACTS].reshape(shape), r1[N_GRADS].reshape(shape), wq_g[None], bq_g, wk_g[None], wv_g[None], bv_g, wo_g[None], bo_g,
            ga_g, sa_g, inner_g[None], bi_g, outer_g[None], bu_g, gf_g, sf_g)


def solution(mesh):
    rows3 = P(None, "dp", None, None)
    matrix, vector = P("section", None, None), P("section", None)
    results = P("section", None, "dp", None, None)
    return jax.shard_map(
        body,
        mesh=mesh,
        in_specs=(rows3, P(None, "dp", None), rows3, matrix, vector, matrix, matrix, vector, matrix, vector, vector, vector,
                  matrix, vector, matrix, vector, vector, vector),
        out_specs=(results, results, matrix, vector, matrix, matrix, vector, matrix, vector, vector, vector, matrix, vector,
                   matrix, vector, vector, vector),
        check_vma=False,
    )
```

```python
from functools import partial

import jax
import jax.numpy as jnp
from jax import lax
from jax.experimental import pallas as pl
from jax.experimental.pallas import tpu as pltpu
from jax.sharding import PartitionSpec as P

HEADS = 12
HEAD = 64
LANES = 128
TILE = 256
VMEM_LIMIT = 127 * 512 * 1024
MICRO = 2
N_ACT = "act"
N_ACTS = "acts"
N_ACT_T = "act_t"
N_AT = "at"
N_BG = "bg"
N_CF = "cf"
N_CG = "cg"
N_CTX = "ctx"
N_CTX_T = "ctx_t"
N_DER = "der"
N_DK = "dk"
N_DQ = "dq"
N_DV = "dv"
N_E = "e"
N_FS = "fs"
N_G = "g"
N_GA = "ga"
N_GF = "gf"
N_GRADS = "grads"
N_HG = "hg"
N_HID = "hid"
N_HIDDEN = "hidden"
N_HID_T = "hid_t"
N_IG = "ig"
N_INV = "inv"
N_K = "k"
N_KEEP1 = "keep1"
N_KEEP2 = "keep2"
N_KEEP3 = "keep3"
N_LG = "lg"
N_MASK = "mask"
N_NA = "na"
N_NF = "nf"
N_O = "o"
N_OFS = "ofs"
N_OG = "og"
N_PA = "pa"
N_PB = "pb"
N_PB0 = "pb0"
N_PB1 = "pb1"
N_PC = "pc"
N_PS = "ps"
N_Q = "q"
N_RA = "ra"
N_RES = "res"
N_RF = "rf"
N_SENT1 = "sent1"
N_SENT2 = "sent2"
N_SENT3 = "sent3"
N_V = "v"
N_VA = "va"
N_WI = "wi"
N_WK = "wk"
N_WO = "wo"
N_WORK = "work"
N_WQ = "wq"
N_WU = "wu"
N_WV = "wv"
N_X = "x"
N_X_T = "x_t"
N__T = "_t"
BF = jnp.bfloat16
F32 = jnp.float32
ANY = pl.BlockSpec(memory_space=pl.ANY)
SMEM = pl.BlockSpec(memory_space=pltpu.SMEM)
VMEM = pl.BlockSpec(memory_space=pltpu.VMEM)


def dot(left, right):
    return lax.dot_general(left, right, (((1,), (0,)), ((), ())), preferred_element_type=F32)


def dot_nt(left, right):
    return lax.dot_general(left, right, (((1,), (1,)), ((), ())), preferred_element_type=F32)


def dot_tn(left, right):
    return lax.dot_general(left, right, (((0,), (0,)), ((), ())), preferred_element_type=F32)


def gelu_pair(u):
    d = 1.0 + 0.23164188580 * jnp.abs(u)
    t = pl.reciprocal(d, approx=True)
    poly = t * (0.127414796 + t * (-0.142248368 + t * (0.7107068705 + t * (-0.7265760135 + t * 0.5307027145))))
    bell = jnp.exp2(u * u * -0.7213475204444817)
    tail = poly * bell
    cdf = jnp.where(u >= 0, 1.0 - tail, tail)
    return u * cdf, cdf + u * (bell * 0.3989422804014327)


def ds(index, size):
    if isinstance(index, int):
        return slice(index * size, (index + 1) * size)
    return pl.ds(pl.multiple_of(index * size, size), size)


def stage_query(r):
    rows, width = r.x.shape
    for j in range(width // TILE):
        cols = slice(j * TILE, (j + 1) * TILE)
        r.q[:, cols] = ((dot(r.x[...], r.wq[:, cols]) + r.bq[:, cols].astype(F32)).astype(BF) * HEAD ** -0.5).astype(BF)


def stage_key(r):
    for j in range(r.x.shape[1] // TILE):
        cols = slice(j * TILE, (j + 1) * TILE)
        r.k[:, cols] = dot(r.x[...], r.wk[:, cols]).astype(BF)


def stage_value(r):
    rows, width = r.x.shape
    one = jnp.ones((rows, LANES), BF)
    for j in range(width // TILE):
        cols = slice(j * TILE, (j + 1) * TILE)
        vv = (dot(r.x[...], r.wv[:, cols]) + r.bv[:, cols].astype(F32)).astype(BF)
        r.v[:, cols] = vv
        for h in range(TILE // LANES):
            at = (j * (TILE // LANES) + h) * TILE
            r.va[:, at:at + LANES] = vv[:, h * LANES:(h + 1) * LANES]
            r.va[:, at + LANES:at + TILE] = one


def stage_mask(r, seg_row):
    rows = r.x.shape[0]
    ids = jnp.broadcast_to(seg_row.astype(F32), (8, rows))
    r.mask[...] = jnp.where(jnp.transpose(ids)[:, 0:1] == ids[0:1, :], 0.0, -1e30)


def stage_attention(r):
    rows, width = r.x.shape
    low = lax.broadcasted_iota(jnp.int32, (1, LANES), 1) < HEAD
    qb = 128

    def pair(p, _):
        kp = r.k[:, ds(p, LANES)]
        vp = r.va[:, ds(p, TILE)]
        kz = [jnp.where(low, kp, jnp.zeros_like(kp)), jnp.where(low, jnp.zeros_like(kp), kp)]
        for b in range(rows // qb):
            rr = slice(b * qb, (b + 1) * qb)
            qp = r.q[rr, ds(p, LANES)]
            parts = []
            for h in range(2):
                s = dot_nt(qp, kz[h]) + r.mask[rr, :]
                top = jnp.max(s, axis=-1, keepdims=True)
                ee = jnp.exp(s - top).astype(BF)
                r.e[2 * p + h, rr, :] = ee
                o = dot(ee, vp)
                inv = 1.0 / o[:, LANES:]
                parts.append((o[:, :LANES] * inv, inv))
            c = jnp.where(low, parts[0][0], parts[1][0])
            r.inv[rr, ds(p, LANES)] = jnp.where(low, parts[0][1], parts[1][1])
            r.cf[rr, ds(p, LANES)] = c
            r.ctx[rr, ds(p, LANES)] = c.astype(BF)
        return 0

    lax.fori_loop(0, width // LANES, pair, 0, unroll=3)


def normal(r, rr, n_ref, s_ref):
    t = r.work[rr, :]
    t = t - jnp.mean(t, axis=-1, keepdims=True)
    scale = lax.rsqrt(jnp.mean(t * t, axis=-1, keepdims=True) + 1e-12)
    n = t * scale
    n_ref[rr, :] = n.astype(BF)
    s_ref[rr, :] = jnp.broadcast_to(scale, (n.shape[0], LANES))
    return n


def stage_branch(r):
    rows, width = r.x.shape
    for j in range(width // TILE):
        cols = slice(j * TILE, (j + 1) * TILE)
        r.work[:, cols] = dot(r.ctx[...], r.wo[:, cols]) + r.bo[:, cols].astype(F32) + r.x[:, cols].astype(F32)

    def norm(b, _):
        rr = ds(b, 64)
        h = normal(r, rr, r.na, r.ra) * r.ga[...].astype(F32) + r.sa[...].astype(F32)
        r.hidden[rr, :] = h
        r.hid[rr, :] = h.astype(BF)
        return 0

    lax.fori_loop(0, rows // 64, norm, 0, unroll=8)


def stage_feed(r):
    rows, width = r.hid.shape
    wide = r.act.shape[1]
    tiles, groups = wide // TILE, wide // width
    per = tiles // groups

    def feed(j):
        cols = slice(j * TILE, (j + 1) * TILE)
        for b in range(rows // LANES):
            rr = slice(b * LANES, (b + 1) * LANES)
            a, g = gelu_pair(dot(r.hid[rr, :], r.wi[:, cols]) + r.bi[:, cols].astype(F32))
            r.act[rr, cols] = a.astype(BF)
            r.der[rr, cols] = g.astype(BF)

    def outer(i, k):
        span, cols = slice(i * width, (i + 1) * width), slice(k * TILE, (k + 1) * TILE)
        t = dot(r.act[:, span], r.wu[span, cols])
        if i == 0:
            r.work[:, cols] = t + r.bu[:, cols].astype(F32) + r.hidden[:, cols]
        else:
            r.work[:, cols] = r.work[:, cols] + t

    for i in range(groups + 1):
        for k in range(per):
            if i > 0:
                outer(i - 1, k)
            if i < groups:
                feed(i * per + k)


def stage_last(r):
    def last(b, _):
        rr = ds(b, 64)
        r.res[rr, :] = (normal(r, rr, r.nf, r.rf) * r.gf[...].astype(F32) + r.sf[...].astype(F32)).astype(BF)
        return 0

    lax.fori_loop(0, r.hid.shape[0] // 64, last, 0, unroll=8)


def norm_back(grad, n_ref, scale, gain, out, low_out, small):
    rows, width = out.shape

    def norm(b, sums):
        rr = ds(b, 64)
        t = grad[rr, :].astype(F32)
        n = n_ref[rr, :].astype(F32)
        s = t * gain[...].astype(F32)
        m1 = jnp.mean(s, axis=-1, keepdims=True)
        m2 = jnp.mean(s * n, axis=-1, keepdims=True)
        f = (s - m1 - n * m2) * scale[rr, 0:1]
        out[rr, :] = f
        low = f.astype(BF)
        low_out[rr, :] = low
        parts = (t * n, t, low.astype(F32))
        return tuple(a + jnp.sum(b.reshape(8, 8, width), axis=0) for a, b in zip(sums, parts))

    zero = jnp.zeros((8, width), F32)
    sums = lax.fori_loop(0, rows // 64, norm, (zero, zero, zero), unroll=8)
    small[...] = jnp.zeros_like(small)
    for i in range(3):
        small[i:i + 1, :width] = jnp.sum(sums[i], axis=0, keepdims=True)


def stage_inner_back(r):
    wide = r.der.shape[1]

    def inner(j, _):
        cols = ds(j, TILE)
        low = (dot_nt(r.og[...], r.wu[cols, :]) * r.der[:, cols].astype(F32)).astype(BF)
        r.ig[:, cols] = low
        return 0

    lax.fori_loop(0, wide // TILE, inner, 0, unroll=6)


def stage_hidden_back(r):
    for j in range(r.hg.shape[0] // TILE):
        rr = slice(j * TILE, (j + 1) * TILE)
        r.hg[rr, :] = r.hg[rr, :] + dot_nt(r.ig[rr, :], r.wi[...])


def stage_context_back(r):
    for j in range(r.bg.shape[1] // TILE):
        cols = slice(j * TILE, (j + 1) * TILE)
        r.cg[:, cols] = dot_nt(r.bg[...], r.wo[cols, :]).astype(BF)


def attention_back_pair(r, p):
    low = lax.broadcasted_iota(jnp.int32, (1, LANES), 1) < HEAD
    cols = ds(p, LANES)
    kp, vp, qp = r.k[:, cols], r.v[:, cols], r.q[:, cols]
    co = (r.cg[:, cols].astype(F32) * r.inv[:, cols]).astype(BF)
    prod = co.astype(F32) * r.cf[:, cols]
    qt, ct = jnp.transpose(qp), jnp.transpose(co)
    zb = jnp.zeros_like(kp)
    dqs, dks, dvs = [], [], []
    for h in range(2):
        mine = low if h == 0 else jnp.logical_not(low)
        part = slice(h * HEAD, (h + 1) * HEAD)
        weighted = jnp.sum(jnp.where(mine, prod, 0.0), axis=-1, keepdims=True)
        ee = r.e[2 * p + h]
        dp = dot_nt(jnp.where(mine, co, zb), vp) - weighted
        sg = (ee.astype(F32) * dp).astype(BF)
        dvs.append(dot(ct[part], ee))
        dqs.append(dot(sg, jnp.where(mine, kp, zb)))
        dks.append(dot(qt[part], sg))
    r.dq[:, cols] = ((dqs[0] + dqs[1]) * HEAD ** -0.5).astype(BF)
    r.dk[:, cols] = jnp.transpose(jnp.concatenate(dks, axis=0)).astype(BF)
    r.dv[:, cols] = jnp.transpose(jnp.concatenate(dvs, axis=0)).astype(BF)


def stage_attention_back(r):
    def pair(p, _):
        attention_back_pair(r, p)
        return 0

    lax.fori_loop(0, r.cg.shape[1] // LANES, pair, 0, unroll=3)


def stage_layer_grad(r):
    for j in range(r.hg.shape[1] // TILE):
        cols = slice(j * TILE, (j + 1) * TILE)
        t = r.hg[:, cols] + dot_nt(r.dq[...], r.wq[cols, :]) + dot_nt(r.dk[...], r.wk[cols, :]) + dot_nt(r.dv[...], r.wv[cols, :])
        r.lg[:, cols] = t.astype(BF)


class Refs:
    pass


class Moves:
    def __init__(self, sems):
        self.sems, self.open, self.used = sems, {}, 0

    def start(self, *pairs):
        for name, src, dst in pairs:
            self.open[name] = (src, dst, self.used)
            self.used += 1
            self.copy(name).start()

    def copy(self, name):
        src, dst, at = self.open[name]
        return pltpu.make_async_copy(src, dst, self.sems.at[at])

    def wait(self, *names):
        for name in names or list(self.open):
            self.copy(name).wait()
            del self.open[name]


KEPT = (N_X, N_CTX, N_HID, N_ACT)
STATE = (N_Q, N_K, N_V, N_E, N_INV, N_CF, N_NA, N_RA, N_DER, N_NF, N_RF)
FEED = (N_OG, N_IG, N_FS)
ATT = (N_BG, N_DQ, N_DK, N_DV, N_AT)
WEIGHTS = (N_WQ, N_WK, N_WV, N_WO, N_WI, N_WU)
VECTORS = ("bq", "bv", "bo", N_GA, "sa", "bi", "bu", N_GF, "sf")


def shapes_of(rows, width, wide):
    row, row32, broad = ((rows, width), BF), ((rows, width), F32), ((rows, wide), BF)
    square = ((width, width), BF)
    table = {n: row for n in (N_X, N_Q, N_K, N_V, N_CTX, N_NA, N_HID, N_NF, N_RES, N_G, N_OG, N_BG, N_CG, N_DQ, N_DK, N_DV, N_LG)}
    table.update({n: row32 for n in (N_INV, N_CF, N_WORK, N_HIDDEN, N_HG)})
    table.update({n: broad for n in (N_ACT, N_DER, N_IG)})
    table.update({n: square for n in (N_WQ, N_WK, N_WV, N_WO)})
    table.update(wi=((width, wide), BF), wu=((wide, width), BF), e=((HEADS, rows, rows), BF), mask=((rows, rows), F32),
                 va=((rows, 2 * width), BF), ra=((rows, LANES), F32), rf=((rows, LANES), F32), fs=((8, wide), F32), at=((8, width), F32),
                 acts=((MICRO, rows, width), BF), grads=((MICRO, rows, width), BF))
    table.update({n + N__T: (table[n][0][::-1], BF) for n in (N_ACT, N_HID, N_CTX, N_X)})
    part, rest = (8, width // 4, width), (8, width // 4 + 16, width)
    table.update(pa=((2,) + part, BF), pc=((2,) + part, BF), pb=((2,) + rest, BF), sent2=(rest, BF), keep2=(rest, BF))
    table.update({n: (part, BF) for n in (N_SENT1, N_KEEP1, N_SENT3, N_KEEP3)})
    table.update(
                 ps=((8, wide), F32), left=((2, width, rows), BF), right=((4, rows, width), BF))
    return table


def layer_call(kernel, name, sizes, small_in, big_in, outs, alias, buffers, flops, moves=40):
    table = shapes_of(*sizes)
    n_small, n_big = len(small_in), len(big_in)
    names = [n for n in outs if n in alias]

    def run(*refs):
        small, big = refs[:n_small], refs[n_small:n_small + n_big]
        at = n_small + n_big + len(names)
        out = dict(zip(outs, refs[at:at + len(outs)]))
        r = Refs()
        for n, ref in zip(buffers, refs[at + len(outs):-1]):
            setattr(r, n, ref)
        kernel(r, small, big, out, Moves(refs[-1]))

    res = pl.pallas_call(
        run,
        out_shape=[jax.ShapeDtypeStruct(*table[n]) for n in outs],
        in_specs=[SMEM] + [VMEM] * (n_small - 1) + [ANY] * (n_big + len(names)),
        out_specs=[ANY] * len(outs),
        scratch_shapes=[pltpu.VMEM(*table[n]) for n in buffers] + [pltpu.SemaphoreType.DMA((moves,))],
        input_output_aliases={n_small + n_big + i: outs.index(n) for i, n in enumerate(names)},
        compiler_params=pltpu.CompilerParams(vmem_limit_bytes=VMEM_LIMIT),
        cost_estimate=pl.CostEstimate(flops=flops, bytes_accessed=30_000_000, transcendentals=0),
        name=name,
    )(*small_in, *big_in, *[alias[n] for n in names])
    return dict(zip(outs, res))


def run_forward(go, seg, x, micro, w, acts, sizes):
    outs = (N_RES, N_ACTS) + KEPT + STATE

    def kernel(r, small, big, out, mv):
        seg_row = small[1]
        for n, ref in zip(VECTORS, small[2:]):
            setattr(r, n, ref)
        src = dict(zip(WEIGHTS, big[1:]))

        @pl.when(small[0][0] == 1)
        def _():
            forward_stages(r, seg_row[micro], big[0].at[micro], src, mv,
                           lambda *names: mv.start(*[(N_O + n, getattr(r, n), out[n]) for n in names]))
            mv.start((N_ACTS, r.res, out[N_ACTS].at[micro]))
            mv.wait()

    buffers = KEPT + STATE + WEIGHTS + (N_RES, N_VA, N_MASK, N_WORK, N_HIDDEN)
    rows, width, wide = sizes
    return layer_call(kernel, "forward", sizes, [go, seg] + [w[n] for n in VECTORS], [x] + [w[n] for n in WEIGHTS], outs, {N_ACTS: acts} if micro else {},
                      buffers, 2 * rows * 12 * width * width)


def forward_stages(r, seg_row, x_src, src, mv, put):
    def load(*names):
        mv.start(*[(n, src[n], getattr(r, n)) for n in names])

    mv.start((N_X, x_src, r.x))
    load(N_WQ, N_WK, N_WV)
    stage_mask(r, seg_row)
    mv.wait(N_X, N_WQ)
    stage_query(r)
    mv.wait(N_WK)
    load(N_WO, N_WI)
    stage_key(r)
    mv.wait(N_WV)
    stage_value(r)
    put(N_X, N_Q, N_K, N_V)
    load(N_WU)
    stage_attention(r)
    put(N_E, N_INV, N_CF, N_CTX)
    mv.wait(N_WO)
    stage_branch(r)
    put(N_NA, N_RA, N_HID)
    mv.wait(N_WI, N_WU)
    stage_feed(r)
    put(N_ACT, N_DER)
    stage_last(r)
    put(N_RES, N_NF, N_RF)


def run_layer(go, seg, x, g, micro, w, kept, sizes):
    outs = (N_ACTS, N_LG, N_GRADS) + KEPT + FEED + ATT

    def kernel(r, small, big, out, mv):
        seg_row = small[1]
        for n, ref in zip(VECTORS, small[2:]):
            setattr(r, n, ref)
        src = dict(zip(WEIGHTS, big[2:]))
        r.hg, r.ig = r.work, r.der

        def put(*names):
            mv.start(*[(N_O + n, getattr(r, n), out[n]) for n in names if n in outs])

        @pl.when(small[0][0] == 1)
        def _():
            forward_stages(r, seg_row[micro], big[0], src, mv, put)
            mv.start((N_G, big[1].at[micro], r.g), (N_ACTS, r.res, out[N_ACTS].at[micro]))
            mv.wait(N_G)
            norm_back(r.g, r.nf, r.rf, r.gf, r.hg, r.og, r.fs)
            put(N_OG)
            stage_inner_back(r)
            put(N_IG, N_FS)
            stage_hidden_back(r)
            norm_back(r.hg, r.na, r.ra, r.ga, r.hg, r.bg, r.at)
            put(N_BG)
            stage_context_back(r)
            stage_attention_back(r)
            put(N_DQ, N_DK, N_DV)
            stage_layer_grad(r)
            put(N_LG, N_AT)
            mv.start((N_GRADS, r.lg, out[N_GRADS].at[micro]))
            mv.wait()

    buffers = KEPT + STATE + WEIGHTS + (N_RES, N_VA, N_MASK, N_WORK, N_HIDDEN, N_G, N_OG, N_FS, N_BG, N_CG, N_DQ, N_DK, N_DV,
                                        N_AT, N_LG)
    rows, width, wide = sizes
    return layer_call(kernel, "layer", sizes, [go, seg] + [w[n] for n in VECTORS], [x, g] + [w[n] for n in WEIGHTS], outs, kept,
                      buffers, 2 * rows * 26 * width * width)


def run_back(go, g, state, micro, old, w, sizes):
    outs = (N_GRADS,) + FEED + ATT
    names = (N_G, N_NF, N_RF, N_WU, N_DER, N_WI, N_NA, N_RA, N_WO, N_Q, N_K, N_V, N_INV, N_CF, N_E, N_WQ, N_WK, N_WV)

    def kernel(r, small, big, out, mv):
        r.gf, r.ga = small[1:3]
        r.ig = r.der
        src = dict(zip(names, big))

        def load(*names):
            mv.start(*[(n, src[n], getattr(r, n)) for n in names])

        def put(*names):
            mv.start(*[(N_O + n, getattr(r, n), out[n]) for n in names])

        @pl.when(small[0][0] == 1)
        def _():
            load(N_G, N_NF, N_RF)
            load(N_WU, N_DER)
            mv.wait(N_G, N_NF, N_RF)
            norm_back(r.g, r.nf, r.rf, r.gf, r.hg, r.og, r.fs)
            put(N_OG)
            mv.wait(N_WU, N_DER)
            load(N_WI, N_NA, N_RA, N_WO)
            stage_inner_back(r)
            put(N_IG, N_FS)
            mv.wait(N_WI)
            load(N_Q, N_K, N_V, N_INV, N_CF, N_E)
            stage_hidden_back(r)
            mv.wait(N_NA, N_RA, N_WO)
            norm_back(r.hg, r.na, r.ra, r.ga, r.hg, r.bg, r.at)
            put(N_BG, N_AT)
            load(N_WQ, N_WK, N_WV)
            stage_context_back(r)
            mv.wait(N_Q, N_K, N_V, N_INV, N_CF, N_E)
            stage_attention_back(r)
            put(N_DQ, N_DK, N_DV)
            mv.wait(N_WQ, N_WK, N_WV)
            stage_layer_grad(r)
            mv.start((N_GRADS, r.lg, out[N_GRADS].at[micro]))
            mv.wait()

    rows, width, wide = sizes
    big = [g, state[N_NF], state[N_RF], w[N_WU], state[N_DER], w[N_WI], state[N_NA], state[N_RA], w[N_WO]]
    big += [state[n] for n in (N_Q, N_K, N_V, N_INV, N_CF, N_E)] + [w[N_WQ], w[N_WK], w[N_WV]]
    return layer_call(kernel, "backward", sizes, [go, w[N_GF], w[N_GA]], big, outs, old,
                      names + (N_OG, N_HG, N_FS, N_BG, N_CG, N_DQ, N_DK, N_DV, N_AT, N_LG), 2 * rows * 14 * width * width)


def run_flip(go, kept, old, sizes):
    outs = (N_ACT_T, N_HID_T, N_CTX_T, N_X_T)
    names = (N_ACT, N_HID, N_CTX, N_X)

    def kernel(r, small, big, out, mv):
        @pl.when(small[0][0] == 1)
        def _():
            mv.start(*[(n, src, getattr(r, n)) for n, src in zip(names, big)])
            for n in reversed(names):
                mv.wait(n)
                src, dst = getattr(r, n), getattr(r, n + N__T)

                def turn(j, _, src=src, dst=dst):
                    dst[ds(j, TILE), :] = jnp.transpose(src[:, ds(j, TILE)])
                    return 0

                lax.fori_loop(0, src.shape[1] // TILE, turn, 0)
                mv.start((n + N__T, dst, out[n + N__T]))
            mv.wait()

    return layer_call(kernel, "transposes", sizes, [go], [kept[n] for n in names], outs, old, names + outs, 4_000_000_000)


def run_partial(go, kept, a, kept1, flip, sizes):
    turned = (N_ACT_T, N_HID_T, N_CTX_T, N_X_T)
    outs = (N_PA, N_PC, N_PB, N_PS) + turned
    names = (N_ACT, N_OG, N_HID, N_IG, N_CTX, N_BG, N_X, N_DQ, N_DK, N_DV)
    rows, width, wide = sizes
    chunk = width // 4
    per = width // chunk

    def kernel(r, small, big, out, mv):
        mv.start(*[(n, src, getattr(r, n)) for n, src in zip(names, big)])
        ones = jnp.ones((8, rows), BF)
        mv.wait(N_ACT, N_OG)
        for i in range(2):
            def first(j, _, i=i):
                cols = pl.ds(pl.multiple_of(i * (wide // 2) + 2 * j * chunk, LANES), 2 * chunk)
                t = dot_tn(r.act[:, cols], r.og[...]).astype(BF)
                r.pa[i, 2 * j] = t[:chunk]
                r.pa[i, 2 * j + 1] = t[chunk:]
                return 0

            lax.fori_loop(0, 4, first, 0, unroll=2)
        mv.start((N_PA, r.pa, out[N_PA]))
        mv.wait(N_HID, N_IG)
        r.hid_t[...] = jnp.transpose(r.hid[...])
        for b in range(4):
            g = r.ig[:, b * width:(b + 1) * width]
            t = dot(r.hid_t[...], g).astype(BF)
            for c in range(per):
                r.pc[b // 2, b % 2 * per + c] = t[c * chunk:(c + 1) * chunk]
            r.ps[:, b * width:(b + 1) * width] = dot(ones, g)
        mv.start((N_PC, r.pc, out[N_PC]), (N_PS, r.ps, out[N_PS]))
        mv.wait(N_CTX, N_BG, N_X, N_DQ, N_DK, N_DV)
        r.x_t[...] = jnp.transpose(r.x[...])
        r.ctx_t[...] = jnp.transpose(r.ctx[...])
        r.pb[:, :, chunk:, :] = jnp.zeros((2, 8, 16, width), BF)
        for n, (left, right) in enumerate(((r.ctx_t, r.bg), (r.x_t, r.dq), (r.x_t, r.dk), (r.x_t, r.dv))):
            t = dot(left[...], right[...]).astype(BF)
            for c in range(per):
                r.pb[n // 2, n % 2 * per + c, :chunk, :] = t[c * chunk:(c + 1) * chunk]
        mv.start((N_PB, r.pb, out[N_PB]))

        @pl.when(small[0][0] == 0)
        def _():
            for i, n in enumerate((N_ACT, N_HID, N_CTX, N_X)):
                mv.start((n, big[10 + i], getattr(r, n)))
            for i, n in enumerate((N_ACT, N_HID, N_CTX, N_X)):
                mv.wait(n)
                src, dst = getattr(r, n), getattr(r, turned[i])

                def turn(j, _, src=src, dst=dst):
                    dst[ds(j, TILE), :] = jnp.transpose(src[:, ds(j, TILE)])
                    return 0

                lax.fori_loop(0, src.shape[1] // TILE, turn, 0)
                mv.start((turned[i], dst, out[turned[i]]))
            mv.wait(*turned)

        mv.wait(N_PA, N_PC, N_PB, N_PS)

    src = dict(kept, **a)
    big = [src[n] for n in names] + [kept1[n] for n in (N_ACT, N_HID, N_CTX, N_X)]
    res = layer_call(kernel, "weight_gradient_0", sizes, [go], big, outs, flip, names + outs, 2 * rows * 12 * width * width)
    return res, res


def run_feed(go, g, state, t1, t, p, w, sizes):
    outs = (N_FS, N_HG, N_SENT1, N_KEEP1, N_SENT3, N_KEEP3, N_PS)
    rows, width, wide = sizes
    chunk = width // 4
    per = width // chunk
    half = wide // 2

    def kernel(r, small, big, out, mv):
        r.gf = small[1]
        r.ig = r.der
        side = [1 - small[0][1], small[0][1]]
        begin = [pl.multiple_of(n * half, half) for n in side]
        mine, others = small[0][0] == 1, small[0][0] == 0

        @pl.when(mine)
        def _():
            mv.start(*[(n, src, getattr(r, n)) for n, src in zip((N_G, N_NF, N_RF), big)])

        @pl.when(others)
        def _():
            mv.start((N_OG, big[8], r.og), (N_IG, big[9], r.der))

        mv.start(("act0", big[5].at[pl.ds(begin[0], half), :], r.act_t.at[:half, :]), ("pa0", big[10].at[side[0]], r.pa.at[0]))

        mv.start(("act1", big[5].at[pl.ds(begin[1], half), :], r.act_t.at[half:, :]), ("pa1", big[10].at[side[1]], r.pa.at[1]))

        @pl.when(mine)
        def _():
            mv.start((N_WU, big[3], r.wu), (N_DER, big[4], r.der))

        mv.start((N_HID_T, big[6], r.hid_t), ("pc0", big[11].at[side[0]], r.pc.at[0]), ("pc1", big[11].at[side[1]], r.pc.at[1]))

        @pl.when(mine)
        def _():
            mv.start((N_WI, big[7], r.wi))
            mv.wait(N_G, N_NF, N_RF)
            norm_back(r.g, r.nf, r.rf, r.gf, r.hg, r.og, r.fs)
            mv.start((N_OFS, r.fs, out[N_FS]))

        @pl.when(others)
        def _():
            mv.wait(N_OG, N_IG)

        for i, n in enumerate((N_SENT1, N_KEEP1)):
            mv.wait("act%d" % i, "pa%d" % i)

            def outer(j, _, i=i):
                rr = pl.ds(pl.multiple_of(i * half + 2 * j * chunk, 2 * chunk), 2 * chunk)
                t = dot(r.act_t[rr, :], r.og[...])
                r.pa[i, 2 * j] = (r.pa[i, 2 * j].astype(F32) + t[:chunk]).astype(BF)
                r.pa[i, 2 * j + 1] = (r.pa[i, 2 * j + 1].astype(F32) + t[chunk:]).astype(BF)
                return 0

            lax.fori_loop(0, 4, outer, 0, unroll=2)
            mv.start((n, r.pa.at[i], out[n]))

        @pl.when(mine)
        def _():
            mv.wait(N_WU, N_DER)
            stage_inner_back(r)

        mv.wait(N_HID_T)
        ones = jnp.ones((8, rows), BF)
        for i, n in enumerate((N_SENT3, N_KEEP3)):
            mv.wait("pc%d" % i)
            for b in range(2):
                at = pl.multiple_of(begin[i] + b * width, width)
                part = r.der[:, pl.ds(at, width)]
                t = dot(r.hid_t[...], part)
                for c in range(per):
                    r.pc[i, b * per + c] = (r.pc[i, b * per + c].astype(F32) + t[c * chunk:(c + 1) * chunk]).astype(BF)
                r.ps[:, pl.ds(at, width)] = dot(ones, part)
            mv.start((n, r.pc.at[i], out[n]))
        mv.start((N_PS, r.ps, out[N_PS]))

        @pl.when(mine)
        def _():
            mv.wait(N_WI)
            stage_hidden_back(r)
            mv.start((N_HG, r.hg, out[N_HG]))
            mv.wait(N_HG, N_OFS)

        mv.wait(N_SENT1, N_KEEP1, N_SENT3, N_KEEP3, N_PS)

    big = [g, state[N_NF], state[N_RF], w[N_WU], state[N_DER], t[N_ACT_T], t[N_HID_T], w[N_WI], t1[N_OG], t1[N_IG], p[N_PA], p[N_PC]]
    return layer_call(kernel, "feed_gradient", sizes, [go, w[N_GF]], big, outs, {N_FS: t1[N_FS]},
                      (N_G, N_NF, N_RF, N_WU, N_WI, N_DER, N_ACT_T, N_HID_T, N_PA, N_PC, N_HG, N_OG, N_FS, N_PS), 8 * rows * width * wide)


def run_rest(go, hg, state, micro, grads, t1, t, p, sums, w, sizes):
    outs = (N_GRADS, N_SENT2, N_KEEP2)
    rows, width, wide = sizes
    names = (N_HG, N_NA, N_RA, N_WO, N_INV, N_CF, N_Q, N_K, N_V, N_E, N_WQ, N_WK, N_WV)
    right = (N_BG, N_DQ, N_DK, N_DV)

    def kernel(r, small, big, out, mv):
        r.ga, fs0, fs1, at0, at1, ps0, ps1, dq0, dv0 = small[1:]
        for i, n in enumerate(right):
            setattr(r, n, r.right.at[i])
        side = [1 - small[0][1], small[0][1]]
        mine, others = small[0][0] == 1, small[0][0] == 0
        src = dict(zip(names, big))
        pairs = width // LANES

        def load(*names):
            mv.start(*[(n, src[n], getattr(r, n)) for n in names])

        @pl.when(mine)
        def _():
            load(N_HG, N_NA, N_RA)
            load(N_WO, N_INV, N_CF, N_Q, N_K, N_V)
            for p in range(0, pairs, 2):
                mv.start(("e%d" % p, big[9].at[2 * p:2 * p + 4], r.e.at[2 * p:2 * p + 4]))
            load(N_WQ, N_WK, N_WV)

        @pl.when(others)
        def _():
            mv.start(*[(n, ref, getattr(r, n)) for n, ref in zip(right, big[15:])])

        mv.start((N_CTX_T, big[13], r.left.at[0]), (N_X_T, big[14], r.left.at[1]))
        mv.start((N_PB0, big[19].at[side[0]], r.pb.at[0]), (N_PB1, big[19].at[side[1]], r.pb.at[1]))
        chunk = r.pb.shape[2] - 16
        per = width // chunk

        @pl.when(mine)
        def _():
            mv.wait(N_HG, N_NA, N_RA)
            norm_back(r.hg, r.na, r.ra, r.ga, r.hg, r.bg, r.at)
            mv.wait(N_WO)
            stage_context_back(r)
            mv.wait(N_INV, N_CF, N_Q, N_K, N_V)
            for p in range(pairs):
                if p % 2 == 0:
                    mv.copy("e%d" % p).wait()
                    del mv.open["e%d" % p]
                attention_back_pair(r, p)

        @pl.when(others)
        def _():
            mv.wait(*right)
            r.at[...] = at1[...]

        mv.wait(N_CTX_T, N_X_T, N_PB0, N_PB1)
        ones = jnp.ones((8, rows), BF)
        fs = fs0[...] + fs1[...]
        at = at0[...] + r.at[...]
        ps = ps0[...] + ps1[...]
        dqs = dot(ones, dq0[...]) + dot(ones, r.right[1])
        dvs = dot(ones, dv0[...]) + dot(ones, r.right[3])
        lines = [dqs[0:1], dvs[0:1], at[2:3], at[0:1], at[1:2], fs[2:3, :width], fs[0:1, :width], fs[1:2, :width]]
        lines += [ps[0:1, i * width:(i + 1) * width] for i in range(wide // width)]
        lines += [jnp.zeros((16 - len(lines), width), F32)]
        lines = jnp.concatenate(lines, axis=0).astype(BF)
        r.pb[0, 0, chunk:, :] = lines
        r.pb[1, 0, chunk:, :] = lines
        for n in range(4):
            which = side[n // 2] * 2 + n % 2
            lhs = jnp.minimum(which, 1)
            v = dot(r.left[lhs], r.right[which])
            for c in range(per):
                at = n % 2 * per + c
                r.pb[n // 2, at, :chunk, :] = (r.pb[n // 2, at, :chunk, :].astype(F32) + v[c * chunk:(c + 1) * chunk]).astype(BF)
            if n % 2:
                mv.start((outs[1 + n // 2], r.pb.at[n // 2], out[outs[1 + n // 2]]))

        @pl.when(mine)
        def _():
            mv.wait(N_WQ, N_WK, N_WV)
            stage_layer_grad(r)
            mv.start((N_GRADS, r.lg, out[N_GRADS].at[micro]))
            mv.wait(N_GRADS)

        mv.wait(N_SENT2, N_KEEP2)

    big = [hg] + [state[N_NA], state[N_RA], w[N_WO]] + [state[n] for n in (N_INV, N_CF, N_Q, N_K, N_V, N_E)] + [w[N_WQ], w[N_WK], w[N_WV]]
    big += [t[N_CTX_T], t[N_X_T]] + [t1[n] for n in right] + [p[N_PB]]
    return layer_call(kernel, "attention_gradient", sizes, [go, w[N_GA]] + sums, big, outs, {N_GRADS: grads},
                      names + (N_CG, "right", "left", N_PB, N_AT, N_LG), 24 * rows * width * width)


def unpack_kernel(place, *rest, kinds, pieces, n_alias, n_lines):
    count = len(pieces)
    n_take = 2 * count * len(kinds)
    take, rest = rest[:n_take], rest[n_take:]
    lines, rest = rest[:n_lines], rest[n_lines + n_alias:]
    outs, small = rest[:n_alias], rest[n_alias:-5]
    low, high, tiny, sin, sout = rest[-5:]
    chunk, width = high.shape[1:]
    per = width // chunk
    loads = [pltpu.make_async_copy(src.at[:chunk, :], low.at[u], sin.at[u]) for u, src in enumerate(take)]
    loads += [pltpu.make_async_copy(src.at[chunk:, :], tiny.at[u], sin.at[n_take + u]) for u, src in enumerate(lines)]
    for c in loads:
        c.start()
    for u in range(n_take):
        kind, at = kinds[u // (2 * count)], u % (2 * count)
        first = sum((1, 1, 4)[k] for k in kinds[:u // (2 * count)])
        core = place[0] if at < count else 1 - place[0]
        rank = place[1] if at < count else 7 - place[1]
        index = core * 8 + lax.rem(rank + 9 - pieces[at % count], 8)
        loads[u].wait()
        high[u] = low[u].astype(F32)
        row = pl.ds(pl.multiple_of(lax.rem(index, per) * chunk, 8), chunk)
        if kind == 0:
            pltpu.make_async_copy(high.at[u], outs[first].at[pl.ds(pl.multiple_of(index * chunk, 8), chunk), :], sout.at[u]).start()
        elif kind == 1:
            col = pl.ds(pl.multiple_of(index // per * width, width), width)
            pltpu.make_async_copy(high.at[u], outs[first].at[row, col], sout.at[u]).start()
        else:
            for n in range(4):
                @pl.when(index // per == n)
                def _(n=n, u=u, row=row, first=first):
                    pltpu.make_async_copy(high.at[u], outs[first + n].at[row, :], sout.at[u]).start()
    if n_lines:
        for c in loads[n_take:]:
            c.wait()
        t = tiny[lax.rem(place[1] + 1, 8)].astype(F32)
        for i in range(8):
            small[i][...] = t[i:i + 1]
        for i in range(small[8].shape[1] // width):
            small[8][:, i * width:(i + 1) * width] = t[8 + i:9 + i]
    for u in range(n_take):
        pltpu.make_async_copy(high.at[u], outs[0].at[:chunk, :width], sout.at[u]).wait()


def run_unpack(place, rings, kinds, pieces, old, final):
    width = rings[0].pieces[0].shape[1]
    chunk = width // 4
    count, wide = len(pieces), 4 * width
    sd = jax.ShapeDtypeStruct
    shapes = [s for k in kinds for s in ([sd((wide, width), F32)], [sd((width, wide), F32)], [sd((width, width), F32)] * 4)[k]]
    lines = rings[-1].pieces if final else []
    small = [sd((1, width), F32)] * 8 + [sd((1, wide), F32)] if lines else []
    take = [side[u] for ring in rings for side in (ring.pieces, ring.others) for u in pieces]
    n_in = 1 + len(take) + len(lines)
    old = list(old or [])

    def kernel(*refs):
        inputs, rest = refs[:n_in], refs[n_in + len(old):]
        unpack_kernel(*inputs, *[None] * len(shapes), *rest, kinds=kinds, pieces=pieces, n_alias=len(shapes), n_lines=len(lines))

    n = len(take)
    return pl.pallas_call(
        kernel,
        out_shape=shapes + small,
        in_specs=[SMEM] + [ANY] * (n_in - 1 + len(old)),
        out_specs=[ANY] * len(shapes) + [VMEM] * len(small),
        scratch_shapes=[pltpu.VMEM((n, chunk, width), BF), pltpu.VMEM((n, chunk, width), F32), pltpu.VMEM((8, 16, width), BF),
                        pltpu.SemaphoreType.DMA((n + 8,)), pltpu.SemaphoreType.DMA((n,))],
        input_output_aliases={n_in + i: i for i in range(len(old))},
        compiler_params=pltpu.CompilerParams(vmem_limit_bytes=VMEM_LIMIT),
        cost_estimate=pl.CostEstimate(flops=0, bytes_accessed=6 * n * chunk * width, transcendentals=0),
        name="unpack",
    )(place, *take, *lines, *old)


def ring_tables():
    chips = [(z, 0) for z in range(4)] + [(z, 1) for z in reversed(range(4))]
    step = []
    for at, (z, y) in enumerate(chips):
        for core in range(2):
            nz, ny = chips[(at + 1) % 8] if core == 0 else chips[at - 1]
            step.append((z * 4 + y * 2 + core, nz * 4 + ny * 2 + core))
    swap = [(d, d ^ 1) for d in range(16)]
    return step, swap


def ring_place():
    d = lax.axis_index("dp")
    z, y, core = d // 4, (d // 2) % 2, d % 2
    at = jnp.where(y == 0, z, 7 - z)
    return core, jnp.where(core == 0, at, 7 - at)


def after(value, *earlier):
    return lax.optimization_barrier((value, *earlier))[0]


class Ring:
    def __init__(self, parts, rank, step, swap):
        self.parts, self.rank, self.step, self.swap = parts, rank, step, swap
        self.count, self.pieces, self.others, self.last = 0, [], [], None
        self.current = self.own(rank)

    def own(self, index):
        index = lax.rem(index, 8)
        return sum(lax.dynamic_index_in_dim(part, index, 0, keepdims=False) for part in self.parts)

    def advance(self):
        got = lax.ppermute(self.current, "dp", self.step)
        if self.count < 7:
            got = got + self.own(self.rank + 7 - self.count)
        self.current = got
        self.count += 1
        if self.last is not None:
            self.current = after(self.current, self.last)
        if self.count >= 7:
            self.pieces.append(self.current)
            self.others.append(lax.ppermute(self.current, "dp", self.swap))

    def hold(self, *earlier):
        self.current = after(self.current, *earlier)


def body(inputs, segments, cotangent, query_weight, query_bias, key_weight, value_weight, value_bias, output_weight, output_bias,
         attention_gain, attention_shift, inner_weight, inner_bias, outer_weight, outer_bias, feed_gain, feed_shift):
    micros, local, rows, width = inputs.shape
    wide = inner_weight.shape[2]
    sizes = (rows, width, wide)
    w = dict(wq=query_weight[0], wk=key_weight[0], wv=value_weight[0], wo=output_weight[0], wi=inner_weight[0], wu=outer_weight[0],
             bq=query_bias, bv=value_bias, bo=output_bias, ga=attention_gain, sa=attention_shift, bi=inner_bias, bu=outer_bias,
             gf=feed_gain, sf=feed_shift)
    x_all = inputs.reshape(micros, rows, width)
    g_all = cotangent.reshape(micros, rows, width)
    section = lax.axis_index("section")
    core, rank = ring_place()
    on0 = jnp.stack([1 - section, core]).astype(jnp.int32)
    on1 = jnp.stack([section, core]).astype(jnp.int32)
    place = jnp.stack([core, rank]).astype(jnp.int32)
    up = partial(lax.ppermute, axis_name="section", perm=[(0, 1)])
    down = partial(lax.ppermute, axis_name="section", perm=[(1, 0)])

    def some(source, names):
        return {n: source[n] for n in names}

    s0 = run_forward(on0, segments, x_all, 0, w, None, sizes)
    x10 = up(s0[N_RES])
    s1 = run_forward(on0, segments, x_all, 1, w, s0[N_ACTS], sizes)
    x11 = up(s1[N_RES])
    flip = run_flip(after(on0, s1[N_RES]), s1, {}, sizes)
    t0 = run_layer(after(on1, flip[N_ACT_T]), segments, x10, g_all, 0, w, dict(some(s0, KEPT), acts=s1[N_ACTS]), sizes)
    g00 = down(t0[N_LG])
    t1 = run_layer(after(on1, t0[N_LG]), segments, x11, g_all, 1, w, dict(some(s1, KEPT), acts=t0[N_ACTS], grads=t0[N_GRADS]), sizes)
    g01 = down(t1[N_LG])
    a0 = run_back(after(on0, t1[N_LG]), g00, s0, 0, dict(some(t0, FEED + ATT), grads=t1[N_GRADS]), w, sizes)
    part, flip = run_partial(after(on0, a0[N_GRADS]), t0, a0, t1, flip, sizes)
    step, swap = ring_tables()
    ring = lax.axis_size("dp") == 16
    f1 = run_feed(after(on0, part[N_PB]), g01, s1, t1, flip, part, w, sizes)
    sums = [a0[N_FS], f1[N_FS], a0[N_AT], t1[N_AT], part[N_PS], f1[N_PS], a0[N_DQ], a0[N_DV]]
    r1 = run_rest(on0, f1[N_HG], s1, 1, a0[N_GRADS], t1, flip, part, sums, w, sizes)
    if ring:
        pairs = [(f1[N_SENT1], f1[N_KEEP1]), (f1[N_SENT3], f1[N_KEEP3]), (r1[N_SENT2], r1[N_KEEP2])]
        rings = []
        for sent, keep in pairs:
            first = after(rank, *[each.current for each in rings])
            rings.append(Ring((keep, lax.ppermute(sent, "dp", swap)), first, step, swap))
        for count in range(1, 15):
            for each in rings:
                each.advance()
            if count == 11:
                weights = run_unpack(after(place, *[each.current for each in rings]), rings, (0, 1, 2), range(4), None, False)
            if count == 12:
                for each in rings:
                    each.hold(weights[0])
            if count == 13:
                weights = run_unpack(after(place, *[each.current for each in rings]), rings, (0, 1, 2), range(4, 7), weights, False)
                for each in rings:
                    each.last = weights[0]
        unpacked = run_unpack(place, rings, (0, 1, 2), range(7, 8), weights, True)
        outer_g, inner_g, fours = unpacked[0], unpacked[1], unpacked[2:]
    else:
        total = []
        for sent, keep in ((f1[N_SENT1], f1[N_KEEP1]), (f1[N_SENT3], f1[N_KEEP3]), (r1[N_SENT2], r1[N_KEEP2])):
            whole = jnp.where(core == 0, jnp.stack([keep, sent]), jnp.stack([sent, keep]))
            total.append(lax.psum(whole, "dp").astype(F32))
        tail = width // 4
        outer_g = total[0].reshape(wide, width)
        inner_g = total[1].reshape(wide // width, width, width).transpose(1, 0, 2).reshape(width, wide)
        lines = total[2][0, 0, tail:]
        fours = list(total[2][:, :, :tail].reshape(4, width, width)) + [lines[i:i + 1] for i in range(8)]
        fours.append(lines[8:8 + wide // width].reshape(1, wide))
    (wo_g, wq_g, wk_g, wv_g, bq_g, bv_g, bo_g, ga_g, sa_g, bu_g, gf_g, sf_g, bi_g) = fours
    shape = (1, micros, local, rows, width)
    return (t1[N_ACTS].reshape(shape), r1[N_GRADS].reshape(shape), wq_g[None], bq_g, wk_g[None], wv_g[None], bv_g, wo_g[None], bo_g,
            ga_g, sa_g, inner_g[None], bi_g, outer_g[None], bu_g, gf_g, sf_g)


def solution(mesh):
    rows3 = P(None, "dp", None, None)
    matrix, vector = P("section", None, None), P("section", None)
    results = P("section", None, "dp", None, None)
    return jax.shard_map(
        body,
        mesh=mesh,
        in_specs=(rows3, P(None, "dp", None), rows3, matrix, vector, matrix, matrix, vector, matrix, vector, vector, vector,
                  matrix, vector, matrix, vector, vector, vector),
        out_specs=(results, results, matrix, vector, matrix, matrix, vector, matrix, vector, vector, vector, matrix, vector,
                   matrix, vector, vector, vector),
        check_vma=False,
    )
```

```python
from functools import partial

import jax
import jax.numpy as jnp
from jax import lax
from jax.experimental import pallas as pl
from jax.experimental.pallas import tpu as pltpu
from jax.sharding import PartitionSpec as P

HEADS = 12
HEAD = 64
LANES = 128
TILE = 256
VMEM_LIMIT = 127 * 512 * 1024
MICRO = 2
N_ACT = "act"
N_ACTS = "acts"
N_ACT_T = "act_t"
N_AT = "at"
N_BG = "bg"
N_CF = "cf"
N_CG = "cg"
N_CTX = "ctx"
N_CTX_T = "ctx_t"
N_DER = "der"
N_DK = "dk"
N_DQ = "dq"
N_DV = "dv"
N_E = "e"
N_FS = "fs"
N_G = "g"
N_GA = "ga"
N_GF = "gf"
N_GRADS = "grads"
N_HG = "hg"
N_HID = "hid"
N_HIDDEN = "hidden"
N_HID_T = "hid_t"
N_IG = "ig"
N_INV = "inv"
N_K = "k"
N_KEEP1 = "keep1"
N_KEEP2 = "keep2"
N_KEEP3 = "keep3"
N_LG = "lg"
N_MASK = "mask"
N_NA = "na"
N_NF = "nf"
N_O = "o"
N_OFS = "ofs"
N_OG = "og"
N_PA = "pa"
N_PB = "pb"
N_PB0 = "pb0"
N_PB1 = "pb1"
N_PC = "pc"
N_PS = "ps"
N_Q = "q"
N_RA = "ra"
N_RES = "res"
N_RF = "rf"
N_SENT1 = "sent1"
N_SENT2 = "sent2"
N_SENT3 = "sent3"
N_V = "v"
N_VA = "va"
N_WI = "wi"
N_WK = "wk"
N_WO = "wo"
N_WORK = "work"
N_WQ = "wq"
N_WU = "wu"
N_WV = "wv"
N_X = "x"
N_X_T = "x_t"
N__T = "_t"
BF = jnp.bfloat16
F32 = jnp.float32
ANY = pl.BlockSpec(memory_space=pl.ANY)
SMEM = pl.BlockSpec(memory_space=pltpu.SMEM)
VMEM = pl.BlockSpec(memory_space=pltpu.VMEM)


def dot(left, right):
    return lax.dot_general(left, right, (((1,), (0,)), ((), ())), preferred_element_type=F32)


def dot_nt(left, right):
    return lax.dot_general(left, right, (((1,), (1,)), ((), ())), preferred_element_type=F32)


def dot_tn(left, right):
    return lax.dot_general(left, right, (((0,), (0,)), ((), ())), preferred_element_type=F32)


def gelu_pair(u):
    d = 1.0 + 0.23164188580 * jnp.abs(u)
    t = pl.reciprocal(d, approx=True)
    poly = t * (0.127414796 + t * (-0.142248368 + t * (0.7107068705 + t * (-0.7265760135 + t * 0.5307027145))))
    bell = jnp.exp2(u * u * -0.7213475204444817)
    tail = poly * bell
    cdf = jnp.where(u >= 0, 1.0 - tail, tail)
    return u * cdf, cdf + u * (bell * 0.3989422804014327)


def ds(index, size):
    if isinstance(index, int):
        return slice(index * size, (index + 1) * size)
    return pl.ds(pl.multiple_of(index * size, size), size)


def stage_query(r):
    rows, width = r.x.shape
    for j in range(width // TILE):
        cols = slice(j * TILE, (j + 1) * TILE)
        r.q[:, cols] = ((dot(r.x[...], r.wq[:, cols]) + r.bq[:, cols].astype(F32)).astype(BF) * HEAD ** -0.5).astype(BF)


def stage_key(r):
    for j in range(r.x.shape[1] // TILE):
        cols = slice(j * TILE, (j + 1) * TILE)
        r.k[:, cols] = dot(r.x[...], r.wk[:, cols]).astype(BF)


def stage_value(r):
    rows, width = r.x.shape
    one = jnp.ones((rows, LANES), BF)
    for j in range(width // TILE):
        cols = slice(j * TILE, (j + 1) * TILE)
        vv = (dot(r.x[...], r.wv[:, cols]) + r.bv[:, cols].astype(F32)).astype(BF)
        r.v[:, cols] = vv
        for h in range(TILE // LANES):
            at = (j * (TILE // LANES) + h) * TILE
            r.va[:, at:at + LANES] = vv[:, h * LANES:(h + 1) * LANES]
            r.va[:, at + LANES:at + TILE] = one


def stage_mask(r, seg_row):
    rows = r.x.shape[0]
    ids = jnp.broadcast_to(seg_row.astype(F32), (8, rows))
    r.mask[...] = jnp.where(jnp.transpose(ids)[:, 0:1] == ids[0:1, :], 0.0, -1e30)


def stage_attention(r):
    rows, width = r.x.shape
    low = lax.broadcasted_iota(jnp.int32, (1, LANES), 1) < HEAD
    qb = 128

    def pair(p, _):
        kp = r.k[:, ds(p, LANES)]
        vp = r.va[:, ds(p, TILE)]
        kz = [jnp.where(low, kp, jnp.zeros_like(kp)), jnp.where(low, jnp.zeros_like(kp), kp)]
        for b in range(rows // qb):
            rr = slice(b * qb, (b + 1) * qb)
            qp = r.q[rr, ds(p, LANES)]
            parts = []
            for h in range(2):
                s = dot_nt(qp, kz[h]) + r.mask[rr, :]
                top = jnp.max(s, axis=-1, keepdims=True)
                ee = jnp.exp(s - top).astype(BF)
                r.e[2 * p + h, rr, :] = ee
                o = dot(ee, vp)
                inv = 1.0 / o[:, LANES:]
                parts.append((o[:, :LANES] * inv, inv))
            c = jnp.where(low, parts[0][0], parts[1][0])
            r.inv[rr, ds(p, LANES)] = jnp.where(low, parts[0][1], parts[1][1])
            r.cf[rr, ds(p, LANES)] = c
            r.ctx[rr, ds(p, LANES)] = c.astype(BF)
        return 0

    lax.fori_loop(0, width // LANES, pair, 0, unroll=3)


def normal(r, rr, n_ref, s_ref):
    t = r.work[rr, :]
    t = t - jnp.mean(t, axis=-1, keepdims=True)
    scale = lax.rsqrt(jnp.mean(t * t, axis=-1, keepdims=True) + 1e-12)
    n = t * scale
    n_ref[rr, :] = n.astype(BF)
    s_ref[rr, :] = jnp.broadcast_to(scale, (n.shape[0], LANES))
    return n


def stage_branch(r):
    rows, width = r.x.shape
    for j in range(width // TILE):
        cols = slice(j * TILE, (j + 1) * TILE)
        r.work[:, cols] = dot(r.ctx[...], r.wo[:, cols]) + r.bo[:, cols].astype(F32) + r.x[:, cols].astype(F32)

    def norm(b, _):
        rr = ds(b, 64)
        h = normal(r, rr, r.na, r.ra) * r.ga[...].astype(F32) + r.sa[...].astype(F32)
        r.hidden[rr, :] = h
        r.hid[rr, :] = h.astype(BF)
        return 0

    lax.fori_loop(0, rows // 64, norm, 0, unroll=8)


def stage_inner(r):
    wide = r.act.shape[1]

    def feed(j, _):
        cols = ds(j, TILE)
        for b in range(r.hid.shape[0] // LANES):
            rr = slice(b * LANES, (b + 1) * LANES)
            a, g = gelu_pair(dot(r.hid[rr, :], r.wi[:, cols]) + r.bi[:, cols].astype(F32))
            r.act[rr, cols] = a.astype(BF)
            r.der[rr, cols] = g.astype(BF)
        return 0

    lax.fori_loop(0, wide // TILE, feed, 0, unroll=4)


def stage_outer(r):
    rows, width = r.x.shape
    for j in range(width // TILE):
        cols = slice(j * TILE, (j + 1) * TILE)
        r.work[:, cols] = dot(r.act[...], r.wu[:, cols]) + r.bu[:, cols].astype(F32) + r.hidden[:, cols]

    def last(b, _):
        rr = ds(b, 64)
        r.res[rr, :] = (normal(r, rr, r.nf, r.rf) * r.gf[...].astype(F32) + r.sf[...].astype(F32)).astype(BF)
        return 0

    lax.fori_loop(0, rows // 64, last, 0, unroll=8)


def norm_back(grad, n_ref, scale, gain, out, low_out, small):
    rows, width = out.shape

    def norm(b, sums):
        rr = ds(b, 64)
        t = grad[rr, :].astype(F32)
        n = n_ref[rr, :].astype(F32)
        s = t * gain[...].astype(F32)
        m1 = jnp.mean(s, axis=-1, keepdims=True)
        m2 = jnp.mean(s * n, axis=-1, keepdims=True)
        f = (s - m1 - n * m2) * scale[rr, 0:1]
        out[rr, :] = f
        low = f.astype(BF)
        low_out[rr, :] = low
        parts = (t * n, t, low.astype(F32))
        return tuple(a + jnp.sum(b.reshape(8, 8, width), axis=0) for a, b in zip(sums, parts))

    zero = jnp.zeros((8, width), F32)
    sums = lax.fori_loop(0, rows // 64, norm, (zero, zero, zero), unroll=8)
    small[...] = jnp.zeros_like(small)
    for i in range(3):
        small[i:i + 1, :width] = jnp.sum(sums[i], axis=0, keepdims=True)


def stage_inner_back(r):
    wide = r.der.shape[1]

    def inner(j, _):
        cols = ds(j, TILE)
        low = (dot_nt(r.og[...], r.wu[cols, :]) * r.der[:, cols].astype(F32)).astype(BF)
        r.ig[:, cols] = low
        return 0

    lax.fori_loop(0, wide // TILE, inner, 0, unroll=6)


def stage_hidden_back(r):
    for j in range(r.hg.shape[0] // TILE):
        rr = slice(j * TILE, (j + 1) * TILE)
        r.hg[rr, :] = r.hg[rr, :] + dot_nt(r.ig[rr, :], r.wi[...])


def stage_context_back(r):
    for j in range(r.bg.shape[1] // TILE):
        cols = slice(j * TILE, (j + 1) * TILE)
        r.cg[:, cols] = dot_nt(r.bg[...], r.wo[cols, :]).astype(BF)


def attention_back_pair(r, p):
    low = lax.broadcasted_iota(jnp.int32, (1, LANES), 1) < HEAD
    cols = ds(p, LANES)
    kp, vp, qp = r.k[:, cols], r.v[:, cols], r.q[:, cols]
    co = (r.cg[:, cols].astype(F32) * r.inv[:, cols]).astype(BF)
    prod = co.astype(F32) * r.cf[:, cols]
    qt, ct = jnp.transpose(qp), jnp.transpose(co)
    zb = jnp.zeros_like(kp)
    dqs, dks, dvs = [], [], []
    for h in range(2):
        mine = low if h == 0 else jnp.logical_not(low)
        part = slice(h * HEAD, (h + 1) * HEAD)
        weighted = jnp.sum(jnp.where(mine, prod, 0.0), axis=-1, keepdims=True)
        ee = r.e[2 * p + h]
        dp = dot_nt(jnp.where(mine, co, zb), vp) - weighted
        sg = (ee.astype(F32) * dp).astype(BF)
        dvs.append(dot(ct[part], ee))
        dqs.append(dot(sg, jnp.where(mine, kp, zb)))
        dks.append(dot(qt[part], sg))
    r.dq[:, cols] = ((dqs[0] + dqs[1]) * HEAD ** -0.5).astype(BF)
    r.dk[:, cols] = jnp.transpose(jnp.concatenate(dks, axis=0)).astype(BF)
    r.dv[:, cols] = jnp.transpose(jnp.concatenate(dvs, axis=0)).astype(BF)


def stage_attention_back(r):
    def pair(p, _):
        attention_back_pair(r, p)
        return 0

    lax.fori_loop(0, r.cg.shape[1] // LANES, pair, 0, unroll=3)


def stage_layer_grad(r):
    for j in range(r.hg.shape[1] // TILE):
        cols = slice(j * TILE, (j + 1) * TILE)
        t = r.hg[:, cols] + dot_nt(r.dq[...], r.wq[cols, :]) + dot_nt(r.dk[...], r.wk[cols, :]) + dot_nt(r.dv[...], r.wv[cols, :])
        r.lg[:, cols] = t.astype(BF)


class Refs:
    pass


class Moves:
    def __init__(self, sems):
        self.sems, self.open, self.used = sems, {}, 0

    def start(self, *pairs):
        for name, src, dst in pairs:
            self.open[name] = (src, dst, self.used)
            self.used += 1
            self.copy(name).start()

    def copy(self, name):
        src, dst, at = self.open[name]
        return pltpu.make_async_copy(src, dst, self.sems.at[at])

    def wait(self, *names):
        for name in names or list(self.open):
            self.copy(name).wait()
            del self.open[name]


KEPT = (N_X, N_CTX, N_HID, N_ACT)
STATE = (N_Q, N_K, N_V, N_E, N_INV, N_CF, N_NA, N_RA, N_DER, N_NF, N_RF)
FEED = (N_OG, N_IG, N_FS)
ATT = (N_BG, N_DQ, N_DK, N_DV, N_AT)
WEIGHTS = (N_WQ, N_WK, N_WV, N_WO, N_WI, N_WU)
VECTORS = ("bq", "bv", "bo", N_GA, "sa", "bi", "bu", N_GF, "sf")


def shapes_of(rows, width, wide):
    row, row32, broad = ((rows, width), BF), ((rows, width), F32), ((rows, wide), BF)
    square = ((width, width), BF)
    table = {n: row for n in (N_X, N_Q, N_K, N_V, N_CTX, N_NA, N_HID, N_NF, N_RES, N_G, N_OG, N_BG, N_CG, N_DQ, N_DK, N_DV, N_LG)}
    table.update({n: row32 for n in (N_INV, N_CF, N_WORK, N_HIDDEN, N_HG)})
    table.update({n: broad for n in (N_ACT, N_DER, N_IG)})
    table.update({n: square for n in (N_WQ, N_WK, N_WV, N_WO)})
    table.update(wi=((width, wide), BF), wu=((wide, width), BF), e=((HEADS, rows, rows), BF), mask=((rows, rows), F32),
                 va=((rows, 2 * width), BF), ra=((rows, LANES), F32), rf=((rows, LANES), F32), fs=((8, wide), F32), at=((8, width), F32),
                 acts=((MICRO, rows, width), BF), grads=((MICRO, rows, width), BF))
    table.update({n + N__T: (table[n][0][::-1], BF) for n in (N_ACT, N_HID, N_CTX, N_X)})
    part, rest = (8, width // 4, width), (8, width // 4 + 16, width)
    table.update(pa=((2,) + part, BF), pc=((2,) + part, BF), pb=((2,) + rest, BF), sent2=(rest, BF), keep2=(rest, BF))
    table.update({n: (part, BF) for n in (N_SENT1, N_KEEP1, N_SENT3, N_KEEP3)})
    table.update(
                 ps=((8, wide), F32), left=((2, width, rows), BF), right=((4, rows, width), BF))
    return table


def layer_call(kernel, name, sizes, small_in, big_in, outs, alias, buffers, flops, moves=40):
    table = shapes_of(*sizes)
    n_small, n_big = len(small_in), len(big_in)
    names = [n for n in outs if n in alias]

    def run(*refs):
        small, big = refs[:n_small], refs[n_small:n_small + n_big]
        at = n_small + n_big + len(names)
        out = dict(zip(outs, refs[at:at + len(outs)]))
        r = Refs()
        for n, ref in zip(buffers, refs[at + len(outs):-1]):
            setattr(r, n, ref)
        kernel(r, small, big, out, Moves(refs[-1]))

    res = pl.pallas_call(
        run,
        out_shape=[jax.ShapeDtypeStruct(*table[n]) for n in outs],
        in_specs=[SMEM] + [VMEM] * (n_small - 1) + [ANY] * (n_big + len(names)),
        out_specs=[ANY] * len(outs),
        scratch_shapes=[pltpu.VMEM(*table[n]) for n in buffers] + [pltpu.SemaphoreType.DMA((moves,))],
        input_output_aliases={n_small + n_big + i: outs.index(n) for i, n in enumerate(names)},
        compiler_params=pltpu.CompilerParams(vmem_limit_bytes=VMEM_LIMIT),
        cost_estimate=pl.CostEstimate(flops=flops, bytes_accessed=30_000_000, transcendentals=0),
        name=name,
    )(*small_in, *big_in, *[alias[n] for n in names])
    return dict(zip(outs, res))


def run_forward(go, seg, x, micro, w, acts, sizes):
    outs = (N_RES, N_ACTS) + KEPT + STATE

    def kernel(r, small, big, out, mv):
        seg_row = small[1]
        for n, ref in zip(VECTORS, small[2:]):
            setattr(r, n, ref)
        src = dict(zip(WEIGHTS, big[1:]))

        @pl.when(small[0][0] == 1)
        def _():
            forward_stages(r, seg_row[micro], big[0].at[micro], src, mv,
                           lambda *names: mv.start(*[(N_O + n, getattr(r, n), out[n]) for n in names]))
            mv.start((N_ACTS, r.res, out[N_ACTS].at[micro]))
            mv.wait()

    buffers = KEPT + STATE + WEIGHTS + (N_RES, N_VA, N_MASK, N_WORK, N_HIDDEN)
    rows, width, wide = sizes
    return layer_call(kernel, "forward", sizes, [go, seg] + [w[n] for n in VECTORS], [x] + [w[n] for n in WEIGHTS], outs, {N_ACTS: acts} if micro else {},
                      buffers, 2 * rows * 12 * width * width)


def forward_stages(r, seg_row, x_src, src, mv, put):
    def load(*names):
        mv.start(*[(n, src[n], getattr(r, n)) for n in names])

    mv.start((N_X, x_src, r.x))
    load(N_WQ, N_WK, N_WV)
    stage_mask(r, seg_row)
    mv.wait(N_X, N_WQ)
    stage_query(r)
    mv.wait(N_WK)
    load(N_WO, N_WI)
    stage_key(r)
    mv.wait(N_WV)
    stage_value(r)
    put(N_X, N_Q, N_K, N_V)
    load(N_WU)
    stage_attention(r)
    put(N_E, N_INV, N_CF, N_CTX)
    mv.wait(N_WO)
    stage_branch(r)
    put(N_NA, N_RA, N_HID)
    mv.wait(N_WI)
    stage_inner(r)
    put(N_ACT, N_DER)
    mv.wait(N_WU)
    stage_outer(r)
    put(N_RES, N_NF, N_RF)


def run_layer(go, seg, x, g, micro, w, kept, sizes):
    outs = (N_ACTS, N_LG, N_GRADS) + KEPT + FEED + ATT

    def kernel(r, small, big, out, mv):
        seg_row = small[1]
        for n, ref in zip(VECTORS, small[2:]):
            setattr(r, n, ref)
        src = dict(zip(WEIGHTS, big[2:]))
        r.hg, r.ig = r.work, r.der

        def put(*names):
            mv.start(*[(N_O + n, getattr(r, n), out[n]) for n in names if n in outs])

        @pl.when(small[0][0] == 1)
        def _():
            forward_stages(r, seg_row[micro], big[0], src, mv, put)
            mv.start((N_G, big[1].at[micro], r.g), (N_ACTS, r.res, out[N_ACTS].at[micro]))
            mv.wait(N_G)
            norm_back(r.g, r.nf, r.rf, r.gf, r.hg, r.og, r.fs)
            put(N_OG)
            stage_inner_back(r)
            put(N_IG, N_FS)
            stage_hidden_back(r)
            norm_back(r.hg, r.na, r.ra, r.ga, r.hg, r.bg, r.at)
            put(N_BG)
            stage_context_back(r)
            stage_attention_back(r)
            put(N_DQ, N_DK, N_DV)
            stage_layer_grad(r)
            put(N_LG, N_AT)
            mv.start((N_GRADS, r.lg, out[N_GRADS].at[micro]))
            mv.wait()

    buffers = KEPT + STATE + WEIGHTS + (N_RES, N_VA, N_MASK, N_WORK, N_HIDDEN, N_G, N_OG, N_FS, N_BG, N_CG, N_DQ, N_DK, N_DV,
                                        N_AT, N_LG)
    rows, width, wide = sizes
    return layer_call(kernel, "layer", sizes, [go, seg] + [w[n] for n in VECTORS], [x, g] + [w[n] for n in WEIGHTS], outs, kept,
                      buffers, 2 * rows * 26 * width * width)


def run_back(go, g, state, micro, old, w, sizes):
    outs = (N_GRADS,) + FEED + ATT
    names = (N_G, N_NF, N_RF, N_WU, N_DER, N_WI, N_NA, N_RA, N_WO, N_Q, N_K, N_V, N_INV, N_CF, N_E, N_WQ, N_WK, N_WV)

    def kernel(r, small, big, out, mv):
        r.gf, r.ga = small[1:3]
        r.ig = r.der
        src = dict(zip(names, big))

        def load(*names):
            mv.start(*[(n, src[n], getattr(r, n)) for n in names])

        def put(*names):
            mv.start(*[(N_O + n, getattr(r, n), out[n]) for n in names])

        @pl.when(small[0][0] == 1)
        def _():
            load(N_G, N_NF, N_RF)
            load(N_WU, N_DER)
            mv.wait(N_G, N_NF, N_RF)
            norm_back(r.g, r.nf, r.rf, r.gf, r.hg, r.og, r.fs)
            put(N_OG)
            mv.wait(N_WU, N_DER)
            load(N_WI, N_NA, N_RA, N_WO)
            stage_inner_back(r)
            put(N_IG, N_FS)
            mv.wait(N_WI)
            load(N_Q, N_K, N_V, N_INV, N_CF, N_E)
            stage_hidden_back(r)
            mv.wait(N_NA, N_RA, N_WO)
            norm_back(r.hg, r.na, r.ra, r.ga, r.hg, r.bg, r.at)
            put(N_BG, N_AT)
            load(N_WQ, N_WK, N_WV)
            stage_context_back(r)
            mv.wait(N_Q, N_K, N_V, N_INV, N_CF, N_E)
            stage_attention_back(r)
            put(N_DQ, N_DK, N_DV)
            mv.wait(N_WQ, N_WK, N_WV)
            stage_layer_grad(r)
            mv.start((N_GRADS, r.lg, out[N_GRADS].at[micro]))
            mv.wait()

    rows, width, wide = sizes
    big = [g, state[N_NF], state[N_RF], w[N_WU], state[N_DER], w[N_WI], state[N_NA], state[N_RA], w[N_WO]]
    big += [state[n] for n in (N_Q, N_K, N_V, N_INV, N_CF, N_E)] + [w[N_WQ], w[N_WK], w[N_WV]]
    return layer_call(kernel, "backward", sizes, [go, w[N_GF], w[N_GA]], big, outs, old,
                      names + (N_OG, N_HG, N_FS, N_BG, N_CG, N_DQ, N_DK, N_DV, N_AT, N_LG), 2 * rows * 14 * width * width)


def run_flip(go, kept, old, sizes):
    outs = (N_ACT_T, N_HID_T, N_CTX_T, N_X_T)
    names = (N_ACT, N_HID, N_CTX, N_X)

    def kernel(r, small, big, out, mv):
        @pl.when(small[0][0] == 1)
        def _():
            mv.start(*[(n, src, getattr(r, n)) for n, src in zip(names, big)])
            for n in reversed(names):
                mv.wait(n)
                src, dst = getattr(r, n), getattr(r, n + N__T)

                def turn(j, _, src=src, dst=dst):
                    dst[ds(j, TILE), :] = jnp.transpose(src[:, ds(j, TILE)])
                    return 0

                lax.fori_loop(0, src.shape[1] // TILE, turn, 0)
                mv.start((n + N__T, dst, out[n + N__T]))
            mv.wait()

    return layer_call(kernel, "transposes", sizes, [go], [kept[n] for n in names], outs, old, names + outs, 4_000_000_000)


def run_partial(go, kept, a, kept1, flip, sizes):
    turned = (N_ACT_T, N_HID_T, N_CTX_T, N_X_T)
    outs = (N_PA, N_PC, N_PB, N_PS) + turned
    names = (N_ACT, N_OG, N_HID, N_IG, N_CTX, N_BG, N_X, N_DQ, N_DK, N_DV)
    rows, width, wide = sizes
    chunk = width // 4
    per = width // chunk

    def kernel(r, small, big, out, mv):
        mv.start(*[(n, src, getattr(r, n)) for n, src in zip(names, big)])
        ones = jnp.ones((8, rows), BF)
        mv.wait(N_ACT, N_OG)
        for i in range(2):
            def first(j, _, i=i):
                cols = pl.ds(pl.multiple_of(i * (wide // 2) + 2 * j * chunk, LANES), 2 * chunk)
                t = dot_tn(r.act[:, cols], r.og[...]).astype(BF)
                r.pa[i, 2 * j] = t[:chunk]
                r.pa[i, 2 * j + 1] = t[chunk:]
                return 0

            lax.fori_loop(0, 4, first, 0, unroll=2)
        mv.start((N_PA, r.pa, out[N_PA]))
        mv.wait(N_HID, N_IG)
        r.hid_t[...] = jnp.transpose(r.hid[...])
        for b in range(4):
            g = r.ig[:, b * width:(b + 1) * width]
            t = dot(r.hid_t[...], g).astype(BF)
            for c in range(per):
                r.pc[b // 2, b % 2 * per + c] = t[c * chunk:(c + 1) * chunk]
            r.ps[:, b * width:(b + 1) * width] = dot(ones, g)
        mv.start((N_PC, r.pc, out[N_PC]), (N_PS, r.ps, out[N_PS]))
        mv.wait(N_CTX, N_BG, N_X, N_DQ, N_DK, N_DV)
        r.x_t[...] = jnp.transpose(r.x[...])
        r.ctx_t[...] = jnp.transpose(r.ctx[...])
        r.pb[:, :, chunk:, :] = jnp.zeros((2, 8, 16, width), BF)
        for n, (left, right) in enumerate(((r.ctx_t, r.bg), (r.x_t, r.dq), (r.x_t, r.dk), (r.x_t, r.dv))):
            t = dot(left[...], right[...]).astype(BF)
            for c in range(per):
                r.pb[n // 2, n % 2 * per + c, :chunk, :] = t[c * chunk:(c + 1) * chunk]
        mv.start((N_PB, r.pb, out[N_PB]))

        @pl.when(small[0][0] == 0)
        def _():
            for i, n in enumerate((N_ACT, N_HID, N_CTX, N_X)):
                mv.start((n, big[10 + i], getattr(r, n)))
            for i, n in enumerate((N_ACT, N_HID, N_CTX, N_X)):
                mv.wait(n)
                src, dst = getattr(r, n), getattr(r, turned[i])

                def turn(j, _, src=src, dst=dst):
                    dst[ds(j, TILE), :] = jnp.transpose(src[:, ds(j, TILE)])
                    return 0

                lax.fori_loop(0, src.shape[1] // TILE, turn, 0)
                mv.start((turned[i], dst, out[turned[i]]))
            mv.wait(*turned)

        mv.wait(N_PA, N_PC, N_PB, N_PS)

    src = dict(kept, **a)
    big = [src[n] for n in names] + [kept1[n] for n in (N_ACT, N_HID, N_CTX, N_X)]
    res = layer_call(kernel, "weight_gradient_0", sizes, [go], big, outs, flip, names + outs, 2 * rows * 12 * width * width)
    return res, res


def run_feed(go, g, state, t1, t, p, w, sizes):
    outs = (N_FS, N_HG, N_SENT1, N_KEEP1, N_SENT3, N_KEEP3, N_PS)
    rows, width, wide = sizes
    chunk = width // 4
    per = width // chunk
    half = wide // 2

    def kernel(r, small, big, out, mv):
        r.gf = small[1]
        r.ig = r.der
        side = [1 - small[0][1], small[0][1]]
        begin = [pl.multiple_of(n * half, half) for n in side]
        mine, others = small[0][0] == 1, small[0][0] == 0

        @pl.when(mine)
        def _():
            mv.start(*[(n, src, getattr(r, n)) for n, src in zip((N_G, N_NF, N_RF), big)])

        @pl.when(others)
        def _():
            mv.start((N_OG, big[8], r.og), (N_IG, big[9], r.der))

        mv.start(("act0", big[5].at[pl.ds(begin[0], half), :], r.act_t.at[:half, :]), ("pa0", big[10].at[side[0]], r.pa.at[0]))

        mv.start(("act1", big[5].at[pl.ds(begin[1], half), :], r.act_t.at[half:, :]), ("pa1", big[10].at[side[1]], r.pa.at[1]))

        @pl.when(mine)
        def _():
            mv.start((N_WU, big[3], r.wu), (N_DER, big[4], r.der))

        mv.start((N_HID_T, big[6], r.hid_t), ("pc0", big[11].at[side[0]], r.pc.at[0]), ("pc1", big[11].at[side[1]], r.pc.at[1]))

        @pl.when(mine)
        def _():
            mv.start((N_WI, big[7], r.wi))
            mv.wait(N_G, N_NF, N_RF)
            norm_back(r.g, r.nf, r.rf, r.gf, r.hg, r.og, r.fs)
            mv.start((N_OFS, r.fs, out[N_FS]))

        @pl.when(others)
        def _():
            mv.wait(N_OG, N_IG)

        for i, n in enumerate((N_SENT1, N_KEEP1)):
            mv.wait("act%d" % i, "pa%d" % i)

            def outer(j, _, i=i):
                rr = pl.ds(pl.multiple_of(i * half + 2 * j * chunk, 2 * chunk), 2 * chunk)
                t = dot(r.act_t[rr, :], r.og[...])
                r.pa[i, 2 * j] = (r.pa[i, 2 * j].astype(F32) + t[:chunk]).astype(BF)
                r.pa[i, 2 * j + 1] = (r.pa[i, 2 * j + 1].astype(F32) + t[chunk:]).astype(BF)
                return 0

            lax.fori_loop(0, 4, outer, 0, unroll=2)
            mv.start((n, r.pa.at[i], out[n]))

        @pl.when(mine)
        def _():
            mv.wait(N_WU, N_DER)
            stage_inner_back(r)

        mv.wait(N_HID_T)
        ones = jnp.ones((8, rows), BF)
        for i, n in enumerate((N_SENT3, N_KEEP3)):
            mv.wait("pc%d" % i)
            for b in range(2):
                at = pl.multiple_of(begin[i] + b * width, width)
                part = r.der[:, pl.ds(at, width)]
                t = dot(r.hid_t[...], part)
                for c in range(per):
                    r.pc[i, b * per + c] = (r.pc[i, b * per + c].astype(F32) + t[c * chunk:(c + 1) * chunk]).astype(BF)
                r.ps[:, pl.ds(at, width)] = dot(ones, part)
            mv.start((n, r.pc.at[i], out[n]))
        mv.start((N_PS, r.ps, out[N_PS]))

        @pl.when(mine)
        def _():
            mv.wait(N_WI)
            stage_hidden_back(r)
            mv.start((N_HG, r.hg, out[N_HG]))
            mv.wait(N_HG, N_OFS)

        mv.wait(N_SENT1, N_KEEP1, N_SENT3, N_KEEP3, N_PS)

    big = [g, state[N_NF], state[N_RF], w[N_WU], state[N_DER], t[N_ACT_T], t[N_HID_T], w[N_WI], t1[N_OG], t1[N_IG], p[N_PA], p[N_PC]]
    return layer_call(kernel, "feed_gradient", sizes, [go, w[N_GF]], big, outs, {N_FS: t1[N_FS]},
                      (N_G, N_NF, N_RF, N_WU, N_WI, N_DER, N_ACT_T, N_HID_T, N_PA, N_PC, N_HG, N_OG, N_FS, N_PS), 8 * rows * width * wide)


def run_rest(go, hg, state, micro, grads, t1, t, p, sums, w, sizes):
    outs = (N_GRADS, N_SENT2, N_KEEP2)
    rows, width, wide = sizes
    names = (N_HG, N_NA, N_RA, N_WO, N_INV, N_CF, N_Q, N_K, N_V, N_E, N_WQ, N_WK, N_WV)
    right = (N_BG, N_DQ, N_DK, N_DV)

    def kernel(r, small, big, out, mv):
        r.ga, fs0, fs1, at0, at1, ps0, ps1, dq0, dv0 = small[1:]
        for i, n in enumerate(right):
            setattr(r, n, r.right.at[i])
        side = [1 - small[0][1], small[0][1]]
        mine, others = small[0][0] == 1, small[0][0] == 0
        src = dict(zip(names, big))
        pairs = width // LANES

        def load(*names):
            mv.start(*[(n, src[n], getattr(r, n)) for n in names])

        @pl.when(mine)
        def _():
            load(N_HG, N_NA, N_RA)
            load(N_WO, N_INV, N_CF, N_Q, N_K, N_V)
            for p in range(0, pairs, 2):
                mv.start(("e%d" % p, big[9].at[2 * p:2 * p + 4], r.e.at[2 * p:2 * p + 4]))
            load(N_WQ, N_WK, N_WV)

        @pl.when(others)
        def _():
            mv.start(*[(n, ref, getattr(r, n)) for n, ref in zip(right, big[15:])])

        mv.start((N_CTX_T, big[13], r.left.at[0]), (N_X_T, big[14], r.left.at[1]))
        mv.start((N_PB0, big[19].at[side[0]], r.pb.at[0]), (N_PB1, big[19].at[side[1]], r.pb.at[1]))
        chunk = r.pb.shape[2] - 16
        per = width // chunk

        @pl.when(mine)
        def _():
            mv.wait(N_HG, N_NA, N_RA)
            norm_back(r.hg, r.na, r.ra, r.ga, r.hg, r.bg, r.at)
            mv.wait(N_WO)
            stage_context_back(r)
            mv.wait(N_INV, N_CF, N_Q, N_K, N_V)
            for p in range(pairs):
                if p % 2 == 0:
                    mv.copy("e%d" % p).wait()
                    del mv.open["e%d" % p]
                attention_back_pair(r, p)

        @pl.when(others)
        def _():
            mv.wait(*right)
            r.at[...] = at1[...]

        mv.wait(N_CTX_T, N_X_T, N_PB0, N_PB1)
        ones = jnp.ones((8, rows), BF)
        fs = fs0[...] + fs1[...]
        at = at0[...] + r.at[...]
        ps = ps0[...] + ps1[...]
        dqs = dot(ones, dq0[...]) + dot(ones, r.right[1])
        dvs = dot(ones, dv0[...]) + dot(ones, r.right[3])
        lines = [dqs[0:1], dvs[0:1], at[2:3], at[0:1], at[1:2], fs[2:3, :width], fs[0:1, :width], fs[1:2, :width]]
        lines += [ps[0:1, i * width:(i + 1) * width] for i in range(wide // width)]
        lines += [jnp.zeros((16 - len(lines), width), F32)]
        lines = jnp.concatenate(lines, axis=0).astype(BF)
        r.pb[0, 0, chunk:, :] = lines
        r.pb[1, 0, chunk:, :] = lines
        for n in range(4):
            which = side[n // 2] * 2 + n % 2
            lhs = jnp.minimum(which, 1)
            v = dot(r.left[lhs], r.right[which])
            for c in range(per):
                at = n % 2 * per + c
                r.pb[n // 2, at, :chunk, :] = (r.pb[n // 2, at, :chunk, :].astype(F32) + v[c * chunk:(c + 1) * chunk]).astype(BF)
            if n % 2:
                mv.start((outs[1 + n // 2], r.pb.at[n // 2], out[outs[1 + n // 2]]))

        @pl.when(mine)
        def _():
            mv.wait(N_WQ, N_WK, N_WV)
            stage_layer_grad(r)
            mv.start((N_GRADS, r.lg, out[N_GRADS].at[micro]))
            mv.wait(N_GRADS)

        mv.wait(N_SENT2, N_KEEP2)

    big = [hg] + [state[N_NA], state[N_RA], w[N_WO]] + [state[n] for n in (N_INV, N_CF, N_Q, N_K, N_V, N_E)] + [w[N_WQ], w[N_WK], w[N_WV]]
    big += [t[N_CTX_T], t[N_X_T]] + [t1[n] for n in right] + [p[N_PB]]
    return layer_call(kernel, "attention_gradient", sizes, [go, w[N_GA]] + sums, big, outs, {N_GRADS: grads},
                      names + (N_CG, "right", "left", N_PB, N_AT, N_LG), 24 * rows * width * width)


def unpack_kernel(place, *rest, kinds, pieces, n_alias, n_lines):
    count = len(pieces)
    n_take = 2 * count * len(kinds)
    take, rest = rest[:n_take], rest[n_take:]
    lines, rest = rest[:n_lines], rest[n_lines + n_alias:]
    outs, small = rest[:n_alias], rest[n_alias:-5]
    low, high, tiny, sin, sout = rest[-5:]
    chunk, width = high.shape[1:]
    per = width // chunk
    loads = [pltpu.make_async_copy(src.at[:chunk, :], low.at[u], sin.at[u]) for u, src in enumerate(take)]
    loads += [pltpu.make_async_copy(src.at[chunk:, :], tiny.at[u], sin.at[n_take + u]) for u, src in enumerate(lines)]
    for c in loads:
        c.start()
    for u in range(n_take):
        kind, at = kinds[u // (2 * count)], u % (2 * count)
        first = sum((1, 1, 4)[k] for k in kinds[:u // (2 * count)])
        core = place[0] if at < count else 1 - place[0]
        rank = place[1] if at < count else 7 - place[1]
        index = core * 8 + lax.rem(rank + 9 - pieces[at % count], 8)
        loads[u].wait()
        high[u] = low[u].astype(F32)
        row = pl.ds(pl.multiple_of(lax.rem(index, per) * chunk, 8), chunk)
        if kind == 0:
            pltpu.make_async_copy(high.at[u], outs[first].at[pl.ds(pl.multiple_of(index * chunk, 8), chunk), :], sout.at[u]).start()
        elif kind == 1:
            col = pl.ds(pl.multiple_of(index // per * width, width), width)
            pltpu.make_async_copy(high.at[u], outs[first].at[row, col], sout.at[u]).start()
        else:
            for n in range(4):
                @pl.when(index // per == n)
                def _(n=n, u=u, row=row, first=first):
                    pltpu.make_async_copy(high.at[u], outs[first + n].at[row, :], sout.at[u]).start()
    if n_lines:
        for c in loads[n_take:]:
            c.wait()
        t = tiny[lax.rem(place[1] + 1, 8)].astype(F32)
        for i in range(8):
            small[i][...] = t[i:i + 1]
        for i in range(small[8].shape[1] // width):
            small[8][:, i * width:(i + 1) * width] = t[8 + i:9 + i]
    for u in range(n_take):
        pltpu.make_async_copy(high.at[u], outs[0].at[:chunk, :width], sout.at[u]).wait()


def run_unpack(place, rings, kinds, pieces, old, final):
    width = rings[0].pieces[0].shape[1]
    chunk = width // 4
    count, wide = len(pieces), 4 * width
    sd = jax.ShapeDtypeStruct
    shapes = [s for k in kinds for s in ([sd((wide, width), F32)], [sd((width, wide), F32)], [sd((width, width), F32)] * 4)[k]]
    lines = rings[-1].pieces if final else []
    small = [sd((1, width), F32)] * 8 + [sd((1, wide), F32)] if lines else []
    take = [side[u] for ring in rings for side in (ring.pieces, ring.others) for u in pieces]
    n_in = 1 + len(take) + len(lines)
    old = list(old or [])

    def kernel(*refs):
        inputs, rest = refs[:n_in], refs[n_in + len(old):]
        unpack_kernel(*inputs, *[None] * len(shapes), *rest, kinds=kinds, pieces=pieces, n_alias=len(shapes), n_lines=len(lines))

    n = len(take)
    return pl.pallas_call(
        kernel,
        out_shape=shapes + small,
        in_specs=[SMEM] + [ANY] * (n_in - 1 + len(old)),
        out_specs=[ANY] * len(shapes) + [VMEM] * len(small),
        scratch_shapes=[pltpu.VMEM((n, chunk, width), BF), pltpu.VMEM((n, chunk, width), F32), pltpu.VMEM((8, 16, width), BF),
                        pltpu.SemaphoreType.DMA((n + 8,)), pltpu.SemaphoreType.DMA((n,))],
        input_output_aliases={n_in + i: i for i in range(len(old))},
        compiler_params=pltpu.CompilerParams(vmem_limit_bytes=VMEM_LIMIT),
        cost_estimate=pl.CostEstimate(flops=0, bytes_accessed=6 * n * chunk * width, transcendentals=0),
        name="unpack",
    )(place, *take, *lines, *old)


def ring_tables():
    chips = [(z, 0) for z in range(4)] + [(z, 1) for z in reversed(range(4))]
    step = []
    for at, (z, y) in enumerate(chips):
        for core in range(2):
            nz, ny = chips[(at + 1) % 8] if core == 0 else chips[at - 1]
            step.append((z * 4 + y * 2 + core, nz * 4 + ny * 2 + core))
    swap = [(d, d ^ 1) for d in range(16)]
    return step, swap


def ring_place():
    d = lax.axis_index("dp")
    z, y, core = d // 4, (d // 2) % 2, d % 2
    at = jnp.where(y == 0, z, 7 - z)
    return core, jnp.where(core == 0, at, 7 - at)


def after(value, *earlier):
    return lax.optimization_barrier((value, *earlier))[0]


class Ring:
    def __init__(self, parts, rank, step, swap):
        self.parts, self.rank, self.step, self.swap = parts, rank, step, swap
        self.count, self.pieces, self.others, self.last = 0, [], [], None
        self.current = self.own(rank)

    def own(self, index):
        index = lax.rem(index, 8)
        return sum(lax.dynamic_index_in_dim(part, index, 0, keepdims=False) for part in self.parts)

    def advance(self):
        got = lax.ppermute(self.current, "dp", self.step)
        if self.count < 7:
            got = got + self.own(self.rank + 7 - self.count)
        self.current = got
        self.count += 1
        if self.last is not None:
            self.current = after(self.current, self.last)
        if self.count >= 7:
            self.pieces.append(self.current)
            self.others.append(lax.ppermute(self.current, "dp", self.swap))

    def hold(self, *earlier):
        self.current = after(self.current, *earlier)


def body(inputs, segments, cotangent, query_weight, query_bias, key_weight, value_weight, value_bias, output_weight, output_bias,
         attention_gain, attention_shift, inner_weight, inner_bias, outer_weight, outer_bias, feed_gain, feed_shift):
    micros, local, rows, width = inputs.shape
    wide = inner_weight.shape[2]
    sizes = (rows, width, wide)
    w = dict(wq=query_weight[0], wk=key_weight[0], wv=value_weight[0], wo=output_weight[0], wi=inner_weight[0], wu=outer_weight[0],
             bq=query_bias, bv=value_bias, bo=output_bias, ga=attention_gain, sa=attention_shift, bi=inner_bias, bu=outer_bias,
             gf=feed_gain, sf=feed_shift)
    x_all = inputs.reshape(micros, rows, width)
    g_all = cotangent.reshape(micros, rows, width)
    section = lax.axis_index("section")
    core, rank = ring_place()
    on0 = jnp.stack([1 - section, core]).astype(jnp.int32)
    on1 = jnp.stack([section, core]).astype(jnp.int32)
    place = jnp.stack([core, rank]).astype(jnp.int32)
    up = partial(lax.ppermute, axis_name="section", perm=[(0, 1)])
    down = partial(lax.ppermute, axis_name="section", perm=[(1, 0)])

    def some(source, names):
        return {n: source[n] for n in names}

    s0 = run_forward(on0, segments, x_all, 0, w, None, sizes)
    x10 = up(s0[N_RES])
    s1 = run_forward(on0, segments, x_all, 1, w, s0[N_ACTS], sizes)
    x11 = up(s1[N_RES])
    flip = run_flip(after(on0, s1[N_RES]), s1, {}, sizes)
    t0 = run_layer(after(on1, flip[N_ACT_T]), segments, x10, g_all, 0, w, dict(some(s0, KEPT), acts=s1[N_ACTS]), sizes)
    g00 = down(t0[N_LG])
    t1 = run_layer(after(on1, t0[N_LG]), segments, x11, g_all, 1, w, dict(some(s1, KEPT), acts=t0[N_ACTS], grads=t0[N_GRADS]), sizes)
    g01 = down(t1[N_LG])
    a0 = run_back(after(on0, t1[N_LG]), g00, s0, 0, dict(some(t0, FEED + ATT), grads=t1[N_GRADS]), w, sizes)
    part, flip = run_partial(after(on0, a0[N_GRADS]), t0, a0, t1, flip, sizes)
    step, swap = ring_tables()
    ring = lax.axis_size("dp") == 16
    f1 = run_feed(after(on0, part[N_PB]), g01, s1, t1, flip, part, w, sizes)
    sums = [a0[N_FS], f1[N_FS], a0[N_AT], t1[N_AT], part[N_PS], f1[N_PS], a0[N_DQ], a0[N_DV]]
    r1 = run_rest(on0, f1[N_HG], s1, 1, a0[N_GRADS], t1, flip, part, sums, w, sizes)
    if ring:
        pairs = [(f1[N_SENT1], f1[N_KEEP1]), (f1[N_SENT3], f1[N_KEEP3]), (r1[N_SENT2], r1[N_KEEP2])]
        rings = []
        for sent, keep in pairs:
            first = after(rank, *[each.current for each in rings])
            rings.append(Ring((keep, lax.ppermute(sent, "dp", swap)), first, step, swap))
        for count in range(1, 15):
            for each in rings:
                each.advance()
            if count == 11:
                weights = run_unpack(after(place, *[each.current for each in rings]), rings, (0, 1, 2), range(4), None, False)
            if count == 12:
                for each in rings:
                    each.hold(weights[0])
            if count == 13:
                weights = run_unpack(after(place, *[each.current for each in rings]), rings, (0, 1, 2), range(4, 7), weights, False)
                for each in rings:
                    each.last = weights[0]
        unpacked = run_unpack(place, rings, (0, 1, 2), range(7, 8), weights, True)
        outer_g, inner_g, fours = unpacked[0], unpacked[1], unpacked[2:]
    else:
        total = []
        for sent, keep in ((f1[N_SENT1], f1[N_KEEP1]), (f1[N_SENT3], f1[N_KEEP3]), (r1[N_SENT2], r1[N_KEEP2])):
            whole = jnp.where(core == 0, jnp.stack([keep, sent]), jnp.stack([sent, keep]))
            total.append(lax.psum(whole, "dp").astype(F32))
        tail = width // 4
        outer_g = total[0].reshape(wide, width)
        inner_g = total[1].reshape(wide // width, width, width).transpose(1, 0, 2).reshape(width, wide)
        lines = total[2][0, 0, tail:]
        fours = list(total[2][:, :, :tail].reshape(4, width, width)) + [lines[i:i + 1] for i in range(8)]
        fours.append(lines[8:8 + wide // width].reshape(1, wide))
    (wo_g, wq_g, wk_g, wv_g, bq_g, bv_g, bo_g, ga_g, sa_g, bu_g, gf_g, sf_g, bi_g) = fours
    shape = (1, micros, local, rows, width)
    return (t1[N_ACTS].reshape(shape), r1[N_GRADS].reshape(shape), wq_g[None], bq_g, wk_g[None], wv_g[None], bv_g, wo_g[None], bo_g,
            ga_g, sa_g, inner_g[None], bi_g, outer_g[None], bu_g, gf_g, sf_g)


def solution(mesh):
    rows3 = P(None, "dp", None, None)
    matrix, vector = P("section", None, None), P("section", None)
    results = P("section", None, "dp", None, None)
    return jax.shard_map(
        body,
        mesh=mesh,
        in_specs=(rows3, P(None, "dp", None), rows3, matrix, vector, matrix, matrix, vector, matrix, vector, vector, vector,
                  matrix, vector, matrix, vector, vector, vector),
        out_specs=(results, results, matrix, vector, matrix, matrix, vector, matrix, vector, vector, vector, matrix, vector,
                   matrix, vector, vector, vector),
        check_vma=False,
    )
```
